32 devices in a mesh: shard: 2 (over core), seq: 4 (over y, x), replica: 4 (over z).
Axes of the slice: x: 2, y: 2, z: 4, core: 2. Of those that a mesh axis runs over, the one named last changes fastest.
Arguments:
- tokens: bfloat16 [16, 256, 2048], P(('shard', 'replica'), 'seq'), may hold values from -6 to 6
- cotangent: bfloat16 [16, 256, 2048], P(('shard', 'replica'), 'seq'), may hold values from -6 to 6
- lengths: int32 [16], P(('shard', 'replica')), may hold values from 64 to 256, as said below
- norm_gains: bfloat16 [2, 2048], P(None, 'shard'), may hold values from 0.5 to 1.5
- w_in: bfloat16 [2048, 12288], P('shard'), may hold values from -0.125 to 0.125
- w_ab: bfloat16 [2048, 32], P('shard'), may hold values from -0.125 to 0.125
- conv_weight: bfloat16 [4, 8192], P(None, 'shard'), may hold values from -3 to 3
- gate_params: float32 [2, 16], replicated, as said below
- onorm_gain: float32 [256], replicated, may hold values from 0.5 to 1.5
- w_o: bfloat16 [4096, 2048], P('shard'), may hold values from -0.09375 to 0.09375
- w_gu: bfloat16 [2048, 11264], P('shard'), may hold values from -0.125 to 0.125
- w_down: bfloat16 [5632, 2048], P('shard'), may hold values from -0.078125 to 0.078125
Outputs:
- output: bfloat16 [16, 256, 2048], P(('shard', 'replica'), 'seq')
- input_grad: bfloat16 [16, 256, 2048], P(('shard', 'replica'), 'seq')
- norm_gains_grad: float32 [2, 2048], P(None, ('shard', 'seq'))
- w_in_grad: float32 [2048, 12288], P(('shard', 'seq'))
- w_ab_grad: float32 [2048, 32], P(('shard', 'seq'))
- conv_grad: float32 [4, 8192], P(None, ('shard', 'seq'))
- gate_params_grad: float32 [2, 16], replicated
- onorm_grad: float32 [256], replicated
- w_o_grad: float32 [4096, 2048], P(('shard', 'seq'))
- w_gu_grad: float32 [2048, 11264], P(('shard', 'seq'))
- w_down_grad: float32 [5632, 2048], P(('shard', 'seq'))
The draws below stay inside these ranges and needn't reach their ends.
Inputs may be any that keep to these rules, and one draw needn't show every extreme that they name: `lengths`: each aligned run of 2 slots holds one slot of exactly 256 valid tokens; positions from a slot's length on are padding. `gate_params`: row 0 holds the logarithms of the heads' decay speeds, row 1 the biases added before the softplus.
All inputs are finite; a program needn't handle non-finite values.
Results may differ from the reference program's by a relative error of at most 0.017.
Values may be sent and summed in bfloat16 or wider, within the bound.
No kernel may reach another device: no remote copies, remote signals or barrier semaphores. Data moves between devices by JAX's collectives and lax.ppermute only.
A program may use at most 576 MiB of HBM per device.

```python
import jax
import jax.numpy as jnp
from jax import lax

D = 2048
HEADS = 16
DK = 128
DV = 256
FF = 5632
KERNEL = 4
BLOCK = 64
MICRO = 2
TOK_SLOT = 64
KD = 2048
VD = 4096
CONVW = 8192
PROJW = 12288
SEQ_LEN = 256
SLOTS = 16


def draw_lengths(key, part):
    key = jax.random.fold_in(key, 11)
    first_key, second_key = jax.random.split(key)
    drawn = jax.random.randint(first_key, (SLOTS,), TOK_SLOT, SEQ_LEN + 1)
    groups = SLOTS // MICRO
    chosen = jax.random.randint(second_key, (groups,), 0, MICRO)
    full_slot = (jnp.arange(MICRO)[None, :] == chosen[:, None]).reshape(SLOTS)
    return jnp.where(full_slot, SEQ_LEN, drawn).astype(jnp.int32)


def draw_gate_params(key, part):
    key = jax.random.fold_in(key, 23)
    first_key, second_key = jax.random.split(key)
    log_speed = jax.random.uniform(first_key, (HEADS,), jnp.float32, -3.0, 1.0)
    step_bias = jax.random.uniform(second_key, (HEADS,), jnp.float32, -4.0, 0.0)
    return jnp.stack([log_speed, step_bias]).astype(jnp.float32)


def block_scale(own_key, shape, cuts, smallest, largest):
    def one(axis_at, blocks):
        steps = jax.random.uniform(jax.random.fold_in(jax.random.fold_in(own_key, 6), axis_at), (blocks,), jnp.float32, smallest / len(cuts), largest / len(cuts))
        return jnp.repeat(jnp.exp(steps), shape[axis_at] // blocks).reshape((-1,) + (1,) * (len(shape) - axis_at - 1))

    level = one(*cuts[0])
    for cut in cuts[1:]:
        level = level * one(*cut)
    return level


def gaussian(key, dims, width, bound, cuts=(), kind=jnp.bfloat16):
    loudness = block_scale(key, dims, cuts, -0.22, 0.18) if cuts else 1.0
    values = jax.random.normal(key, dims, jnp.float32) * width * loudness
    return jnp.minimum(jnp.maximum(values, -bound), bound).astype(kind)


def setup_inputs(seed: int = 0) -> dict:
    keys = jax.random.split(jax.random.key(seed), 13)
    return {
        "tokens": gaussian(keys[0], (SLOTS, SEQ_LEN, D), 1.0, 6.0, ((0, 8), (1, 4))),
        "cotangent": gaussian(keys[1], (SLOTS, SEQ_LEN, D), 1.0, 6.0, ((0, 8), (1, 4))),
        "lengths": draw_lengths(jax.random.fold_in(keys[12], 71), 0),
        "norm_gains": jnp.clip(1.0 + 0.1 * jax.random.normal(keys[3], (2, D), jnp.float32), 0.5, 1.5).astype(jnp.bfloat16),
        "w_in": gaussian(keys[4], (D, PROJW), D ** -0.5, 0.125, ((0, 2),)),
        "w_ab": gaussian(keys[5], (D, 2 * HEADS), D ** -0.5, 0.125, ((0, 2),)),
        "conv_weight": gaussian(keys[6], (KERNEL, CONVW), KERNEL ** -0.5, 3.0, ((1, 2),)),
        "gate_params": draw_gate_params(jax.random.fold_in(keys[12], 71), 0),
        "onorm_gain": jnp.clip(1.0 + 0.1 * jax.random.normal(keys[8], (DV,), jnp.float32), 0.5, 1.5),
        "w_o": gaussian(keys[9], (VD, D), VD ** -0.5, 0.09375, ((0, 2),)),
        "w_gu": gaussian(keys[10], (D, 2 * FF), D ** -0.5, 0.125, ((0, 2),)),
        "w_down": gaussian(keys[11], (FF, D), FF ** -0.5, 0.078125, ((0, 2),)),
    }


HIGHEST = lax.Precision.HIGHEST
EPS = 1e-06

@jax.custom_vjp
def low(v):
    return lax.optimization_barrier(v.astype(jnp.bfloat16)).astype(jnp.float32)

@jax.custom_vjp
def low_back(v):
    return v

def low_keep(v):
    return (low(v), None)

def low_pass(kept, grad):
    return (grad,)

def back_keep(v):
    return (v, None)

def back_low(kept, grad):
    return (low(grad),)
low.defvjp(low_keep, low_pass)
low_back.defvjp(back_keep, back_low)

def rms_scaled(values, gain):
    return values * lax.rsqrt(lax.optimization_barrier(jnp.mean(values * values, -1, keepdims=True)) + EPS) * gain

def matmul_hi(left, right):
    return jnp.matmul(left, right, precision=HIGHEST)

def token_step(state_now, block_item):
    query_row, key_row, value_row, decay_now, rate_now = block_item
    faded_state = jnp.exp(decay_now)[..., None, None] * state_now
    recalled = jnp.einsum('bhd,bhdw->bhw', key_row, faded_state, precision=HIGHEST)
    written = rate_now[..., None] * (value_row - recalled)
    state_now = faded_state + jnp.einsum('bhd,bhw->bhdw', key_row, written, precision=HIGHEST)
    return (state_now, jnp.einsum('bhd,bhdw->bhw', query_row, state_now, precision=HIGHEST))

@jax.checkpoint
def block_step(state_now, block_item):
    return lax.scan(token_step, state_now, block_item)

def delta_rule(queries, key_rows, values, decays, write_rate):
    batch_size, length = (queries.shape[0], queries.shape[1])

    def to_blocks(stacked):
        leading = jnp.moveaxis(stacked, 1, 0)
        return leading.reshape((length // BLOCK, BLOCK) + leading.shape[1:])
    blocks = tuple((to_blocks(stacked) for stacked in (queries, key_rows, values, decays, write_rate)))
    initial = jnp.zeros((batch_size, HEADS, DK, DV), jnp.float32)
    final_state, outputs = lax.scan(block_step, initial, blocks)
    outputs = outputs.reshape((length,) + outputs.shape[2:])
    return jnp.moveaxis(outputs, 0, 1)

def forward(inputs, valid_mask, norm_gains, w_in, w_ab, conv_weight, gate_params, onorm_gain, w_o, w_gu, w_down):
    batch_size, length = (inputs.shape[0], inputs.shape[1])
    normed = low(rms_scaled(inputs, norm_gains[0]))
    projected = matmul_hi(normed, w_in)
    conv_in = low_back(low(projected[..., :CONVW]))
    gate_pre = low_back(projected[..., CONVW:])
    rate_in = matmul_hi(normed, w_ab)
    padded = jnp.pad(conv_in, ((0, 0), (KERNEL - 1, 0), (0, 0)))
    mixed = sum((conv_weight[offset] * padded[:, offset:offset + length] for offset in range(KERNEL)))
    active = jax.nn.silu(mixed)
    queries = active[..., :KD].reshape(batch_size, length, HEADS, DK)
    key_rows = active[..., KD:2 * KD].reshape(batch_size, length, HEADS, DK)
    values = active[..., 2 * KD:].reshape(batch_size, length, HEADS, DV)
    queries = queries * lax.rsqrt(lax.optimization_barrier(jnp.sum(queries * queries, -1, keepdims=True)) + EPS) * DK ** (-0.5)
    key_rows = key_rows * lax.rsqrt(lax.optimization_barrier(jnp.sum(key_rows * key_rows, -1, keepdims=True)) + EPS)
    decays = -jnp.exp(gate_params[0]) * jax.nn.softplus(rate_in[..., :HEADS] + gate_params[1]) * valid_mask[..., None]
    write_rate = jax.nn.sigmoid(rate_in[..., HEADS:]) * valid_mask[..., None]
    outputs = delta_rule(queries, key_rows, values, decays, write_rate)
    gated = rms_scaled(outputs, onorm_gain).reshape(batch_size, length, VD) * jax.nn.silu(gate_pre)
    middle = inputs + low_back(matmul_hi(low(gated), w_o))
    renormed = low(rms_scaled(middle, norm_gains[1]))
    gate_up = low_back(matmul_hi(renormed, w_gu))
    hidden = low(jax.nn.silu(gate_up[..., :FF]) * gate_up[..., FF:])
    return middle + low_back(matmul_hi(hidden, w_down))

def reference(tokens, cotangent, lengths, norm_gains, w_in, w_ab, conv_weight, gate_params, onorm_gain, w_o, w_gu, w_down):
    weights = tuple((weight.astype(jnp.float32) for weight in (norm_gains, w_in, w_ab, conv_weight, gate_params, onorm_gain, w_o, w_gu, w_down)))
    groups = SLOTS // MICRO
    token_blocks = tokens.reshape(groups, MICRO, SEQ_LEN, D)
    cot_blocks = cotangent.reshape(groups, MICRO, SEQ_LEN, D)
    length_blocks = lengths.reshape(groups, MICRO)
    positions = jnp.arange(SEQ_LEN, dtype=jnp.int32)

    def batch_step(totals, block_item):
        block_in, block_cot, block_len = block_item
        valid_mask = (positions[None, :] < block_len[:, None]).astype(jnp.float32)

        def apply_layer(inputs, *params):
            return forward(inputs, valid_mask, *params)
        result, pullback = jax.vjp(apply_layer, block_in.astype(jnp.float32), *weights)
        gradients = pullback(block_cot.astype(jnp.float32))
        totals = tuple((running + fresh for running, fresh in zip(totals, gradients[1:])))
        return (totals, (result.astype(jnp.bfloat16), gradients[0].astype(jnp.bfloat16)))
    zeros_start = tuple((jnp.zeros_like(weight) for weight in weights))
    totals, outcome = lax.scan(batch_step, zeros_start, (token_blocks, cot_blocks, length_blocks))
    results, input_grads = outcome
    return (results.reshape(SLOTS, SEQ_LEN, D), input_grads.reshape(SLOTS, SEQ_LEN, D), totals[0], totals[1], totals[2], totals[3], totals[4], totals[5], totals[6], totals[7], totals[8])
```

```python
import functools

import jax
import jax.numpy as jnp
from jax import lax
from jax.experimental import pallas as pl
from jax.experimental.pallas import tpu as pltpu
from jax.sharding import PartitionSpec as P

D = 2048
HEADS = 16
DK = 128
DV = 256
FF = 5632
KERNEL = 4
KD = 2048
VD = 4096
CONVW = 8192
PROJW = 12288
EPS = 1e-06
HIGHEST = lax.Precision.HIGHEST
LOWEST_DECAY = -104.0
F32 = jnp.float32
BF16 = jnp.bfloat16
EVERY = ("shard", "seq", "replica")
GROUP = ("shard", "seq")


def mm(left, right, dims=((1,), (0,))):
    return lax.dot_general(
        left.astype(BF16), right.astype(BF16), (dims, ((), ())), preferred_element_type=F32
    )


def split(value):
    high = value.astype(BF16)
    return high, (value - high.astype(F32)).astype(BF16)


def mm3(left, right, dims=((1,), (0,))):
    left_high, left_low = split(left)
    right_high, right_low = split(right)
    return (
        mm(left_high, right_high, dims)
        + mm(left_high, right_low, dims)
        + mm(left_low, right_high, dims)
    )


ROWS_ROWS = ((1,), (1,))
COLS_COLS = ((0,), (0,))


def delayed(value, steps, rows):
    if steps == 0:
        return value
    return jnp.where(rows >= steps, pltpu.roll(value, steps, 0), 0.0)


def advanced(value, steps, rows):
    if steps == 0:
        return value
    length = value.shape[0]
    return jnp.where(rows < length - steps, pltpu.roll(value, length - steps, 0), 0.0)


def in_order(ref, place):
    pieces = ref.shape[0]
    return jnp.concatenate([ref[jnp.bitwise_xor(place, j), 0] for j in range(pieces)], 0)


def put_back(ref, place, value):
    pieces = ref.shape[0]
    width = value.shape[0] // pieces
    for j in range(pieces):
        ref[jnp.bitwise_xor(place, j), 0] = value[j * width : (j + 1) * width].astype(ref.dtype)


def convolved(source, taps, rows):
    mixed = taps[KERNEL - 1 : KERNEL] * source
    for offset in range(KERNEL - 1):
        mixed = mixed + taps[offset : offset + 1] * delayed(source, KERNEL - 1 - offset, rows)
    return mixed


def unit(value):
    scale = lax.rsqrt(jnp.sum(value * value, -1, keepdims=True) + EPS)
    return value * scale, scale


def decay_matrices(rates):
    length = rates.shape[1]
    row_ids = lax.broadcasted_iota(jnp.int32, (length, length), 0)
    col_ids = lax.broadcasted_iota(jnp.int32, (length, length), 1)
    decay_row = rates[0:1]
    rate_row = rates[1:2]
    diagonal = row_ids == col_ids
    running = jnp.sum(jnp.where(row_ids >= col_ids, decay_row, 0.0), 1, keepdims=True)
    running_row = jnp.sum(jnp.where(diagonal, running, 0.0), 0, keepdims=True)
    rate = jnp.sum(jnp.where(diagonal, rate_row, 0.0), 1, keepdims=True)
    spread = jnp.minimum(running - running_row, 0.0)
    weight = jnp.where(row_ids >= col_ids, jnp.exp(spread), 0.0)
    return row_ids, col_ids, rate, weight


def lower_inverse(system, row_ids, col_ids):
    length = system.shape[0]
    eye = (row_ids == col_ids).astype(F32)
    same = jnp.bitwise_xor(row_ids, col_ids)
    inverse = eye - jnp.where(same < 2, system, 0.0)
    size = 2
    while size < length:
        between = jnp.where((same >= size) & (same < 2 * size), system, 0.0)
        inverse = inverse - mm3(inverse, mm3(between, inverse))
        size *= 2
    return inverse


def head_inputs(place, q_ref, k_ref, v_ref, taps_q, taps_k, taps_v, rates_ref):
    raw = tuple(in_order(ref, place).astype(BF16).astype(F32) for ref in (q_ref, k_ref, v_ref))
    rows = lax.broadcasted_iota(jnp.int32, (raw[0].shape[0], 1), 0)
    mixed = tuple(
        convolved(source, taps[...].astype(F32), rows)
        for source, taps in zip(raw, (taps_q, taps_k, taps_v))
    )
    slopes = tuple(jax.nn.sigmoid(item) for item in mixed)
    query_unit, query_scale = unit(mixed[0] * slopes[0])
    key_rows, key_scale = unit(mixed[1] * slopes[1])
    values = mixed[2] * slopes[2]
    queries = query_unit * DK ** (-0.5)
    return raw, rows, mixed, slopes, queries, key_rows, values, query_unit, query_scale, key_scale


def forward_kernel(
    place_ref, q_ref, k_ref, v_ref, g_ref, taps_q, taps_k, taps_v, rates_ref, gain_ref,
    gated_ref, inverse_ref, update_ref,
):
    place = place_ref[0]
    items = head_inputs(place, q_ref, k_ref, v_ref, taps_q, taps_k, taps_v, rates_ref)
    queries, key_rows, values = items[4:7]
    row_ids, col_ids, rate, weight = decay_matrices(rates_ref[0, 0])
    system = jnp.where(
        row_ids > col_ids, rate * mm3(key_rows, key_rows, ROWS_ROWS) * weight, 0.0
    )
    inverse = lower_inverse(system, row_ids, col_ids)
    update = mm3(inverse, rate * values)
    scores = mm(queries, key_rows, ROWS_ROWS) * weight
    outputs = mm(scores, update)
    scaled = (
        outputs
        * lax.rsqrt(jnp.mean(outputs * outputs, -1, keepdims=True) + EPS)
        * gain_ref[...]
    )
    gate = in_order(g_ref, place)
    put_back(gated_ref, place, scaled * (gate * jax.nn.sigmoid(gate)))
    inverse_ref[0, 0] = inverse
    update_ref[0, 0] = update


def unit_back(grad, direction, scale):
    return scale * (grad - direction * jnp.sum(grad * direction, -1, keepdims=True))


def backward_kernel(
    place_ref, q_ref, k_ref, v_ref, g_ref, taps_q, taps_k, taps_v, rates_ref, gain_ref,
    inverse_ref, update_ref, grad_ref,
    dq_ref, dk_ref, dv_ref, dg_ref, small_ref,
):
    place = place_ref[0]
    raw, rows, mixed, slopes, queries, key_rows, values, query_unit, query_scale, key_scale = (
        head_inputs(place, q_ref, k_ref, v_ref, taps_q, taps_k, taps_v, rates_ref)
    )
    row_ids, col_ids, rate, weight = decay_matrices(rates_ref[0, 0])
    inner = mm3(key_rows, key_rows, ROWS_ROWS)
    strict = row_ids > col_ids
    keyed = jnp.where(strict, inner * weight, 0.0)
    scores = mm(queries, key_rows, ROWS_ROWS) * weight
    inverse = inverse_ref[0, 0]
    update = update_ref[0, 0]
    outputs = mm(scores, update)
    gate = in_order(g_ref, place)
    upstream = in_order(grad_ref, place).astype(F32)
    gate_slope = jax.nn.sigmoid(gate)
    out_scale = lax.rsqrt(jnp.mean(outputs * outputs, -1, keepdims=True) + EPS)
    out_unit = outputs * out_scale
    gain = gain_ref[...]
    scaled_grad = upstream * (gate * gate_slope)
    put_back(
        dg_ref, place, upstream * out_unit * gain * (gate_slope * (1.0 + gate * (1.0 - gate_slope)))
    )
    gain_grad = jnp.sum(scaled_grad * out_unit, 0, keepdims=True)
    unit_grad = scaled_grad * gain
    out_grad = out_scale * (
        unit_grad - out_unit * jnp.mean(unit_grad * out_unit, -1, keepdims=True)
    )
    scores_grad = jnp.where(row_ids >= col_ids, mm(out_grad, update, ROWS_ROWS), 0.0)
    update_grad = mm(scores, out_grad, COLS_COLS)
    target_grad = mm3(inverse, update_grad, COLS_COLS)
    system_grad = jnp.where(strict, -mm(target_grad, update, ROWS_ROWS), 0.0)
    value_grad = rate * target_grad
    keyed_grad = system_grad * keyed
    rate_grad = jnp.sum(target_grad * values, 1, keepdims=True) + jnp.sum(
        keyed_grad, 1, keepdims=True
    )
    spread_grad = keyed_grad * rate + scores_grad * scores
    inner_grad = system_grad * weight * rate
    raw_scores_grad = scores_grad * weight
    query_grad = mm(raw_scores_grad, key_rows) * DK ** (-0.5)
    key_grad = (
        mm(raw_scores_grad, queries, COLS_COLS)
        + mm(inner_grad, key_rows)
        + mm(inner_grad, key_rows, COLS_COLS)
    )
    diagonal = row_ids == col_ids
    column_sum = jnp.sum(spread_grad, 0, keepdims=True)
    running_grad = jnp.sum(spread_grad, 1, keepdims=True) - jnp.sum(
        jnp.where(diagonal, column_sum, 0.0), 1, keepdims=True
    )
    decay_grad = jnp.sum(jnp.where(row_ids >= col_ids, running_grad, 0.0), 0, keepdims=True)
    rate_grad_row = jnp.sum(jnp.where(diagonal, rate_grad, 0.0), 0, keepdims=True)
    active_grads = (
        unit_back(query_grad, query_unit, query_scale),
        unit_back(key_grad, key_rows, key_scale),
        value_grad,
    )
    starts = (0, DK, 2 * DK)
    small_ref[...] = jnp.zeros_like(small_ref)
    for at, grad_out, source, before, slope, taps, out_ref in zip(
        starts, active_grads, raw, mixed, slopes, (taps_q, taps_k, taps_v), (dq_ref, dk_ref, dv_ref)
    ):
        mixed_grad = grad_out * (slope * (1.0 + before * (1.0 - slope)))
        kernel = taps[...].astype(F32)
        width = source.shape[1]
        total = kernel[KERNEL - 1 : KERNEL] * mixed_grad
        for offset in range(KERNEL):
            steps = KERNEL - 1 - offset
            if steps:
                total = total + kernel[offset : offset + 1] * advanced(mixed_grad, steps, rows)
            small_ref[0, 0, offset : offset + 1, at : at + width] = jnp.sum(
                mixed_grad * delayed(source, steps, rows), 0, keepdims=True
            )
        put_back(out_ref, place, total)
    small_ref[0, 0, 4:5, 0:DV] = gain_grad
    length = decay_grad.shape[1]
    small_ref[0, 0, 5:6, 0:length] = decay_grad
    small_ref[0, 0, 6:7, 0:length] = rate_grad_row


def mixer_specs(pieces, row, heads, length):
    def piece(width, shift):
        return pl.BlockSpec((pieces, 1, row, width), lambda b, h, place: (0, b, 0, h + shift))

    def taps(width, shift):
        return pl.BlockSpec((KERNEL, width), lambda b, h, place: (0, h + shift))

    proj = [piece(DK, 0), piece(DK, heads), piece(DV, heads), piece(DV, 2 * heads)]
    kernel = [taps(DK, 0), taps(DK, heads), taps(DV, heads)]
    rates = pl.BlockSpec((1, 1, 8, length), lambda b, h, place: (b, h, 0, 0))
    gain = pl.BlockSpec((1, DV), lambda b, h, place: (0, 0))
    square = pl.BlockSpec((1, 1, length, length), lambda b, h, place: (b, h, 0, 0))
    return piece, proj, kernel, rates, gain, square


VMEM_LIMIT = 40 * 1024 * 1024


def mixer_forward(place, projected, taps, rates, gain):
    pieces, micro, row, _ = projected.shape
    heads, length = rates.shape[1], rates.shape[3]
    piece, proj, kernel, rate_spec, gain_spec, square = mixer_specs(pieces, row, heads, length)
    return pl.pallas_call(
        forward_kernel,
        grid_spec=pltpu.PrefetchScalarGridSpec(
            num_scalar_prefetch=1,
            grid=(micro, heads),
            in_specs=proj + kernel + [rate_spec, gain_spec],
            out_specs=[piece(DV, 0), square, square],
        ),
        out_shape=[
            jax.ShapeDtypeStruct((pieces, micro, row, heads * DV), BF16),
            jax.ShapeDtypeStruct((micro, heads, length, length), F32),
            jax.ShapeDtypeStruct((micro, heads, length, DV), F32),
        ],
        compiler_params=pltpu.CompilerParams(vmem_limit_bytes=VMEM_LIMIT),
    )(place, projected, projected, projected, projected, taps, taps, taps, rates, gain)


def mixer_backward(place, projected, taps, rates, gain, inverse, update, grad):
    pieces, micro, row, _ = projected.shape
    heads, length = rates.shape[1], rates.shape[3]
    piece, proj, kernel, rate_spec, gain_spec, square = mixer_specs(pieces, row, heads, length)
    small = pl.BlockSpec((1, 1, 8, 2 * DK + DV), lambda b, h, place: (b, h, 0, 0))

    def out(width):
        return jax.ShapeDtypeStruct((pieces, micro, row, heads * width), BF16)

    return pl.pallas_call(
        backward_kernel,
        grid_spec=pltpu.PrefetchScalarGridSpec(
            num_scalar_prefetch=1,
            grid=(micro, heads),
            in_specs=proj + kernel + [rate_spec, gain_spec, square, square, piece(DV, 0)],
            out_specs=[piece(DK, 0), piece(DK, 0), piece(DV, 0), piece(DV, 0), small],
        ),
        out_shape=[
            out(DK),
            out(DK),
            out(DV),
            out(DV),
            jax.ShapeDtypeStruct((micro, heads, 8, 2 * DK + DV), F32),
        ],
        compiler_params=pltpu.CompilerParams(vmem_limit_bytes=VMEM_LIMIT),
    )(
        place, projected, projected, projected, projected, taps, taps, taps, rates, gain,
        inverse, update, grad,
    )


def swapped(value, axis, step):
    count = lax.axis_size(axis)
    return lax.ppermute(value, axis, [(source, source ^ step) for source in range(count)])


def around(value, axis):
    return [value] + [swapped(value, axis, step) for step in range(1, lax.axis_size(axis))]


def settled(parts, index):
    stacked = jnp.stack(parts)
    return [
        lax.dynamic_index_in_dim(stacked, jnp.bitwise_xor(index, at), 0, keepdims=False)
        for at in range(len(parts))
    ]


def part_of(value, index, count, axis):
    width = value.shape[axis] // count
    return lax.dynamic_slice_in_dim(value, index * width, width, axis)


def dot(left, right):
    return jnp.dot(left, right, preferred_element_type=F32)


def dot_rows(left, right):
    return lax.dot_general(left, right, (((1,), (1,)), ((), ())), preferred_element_type=F32)


def dot_cols(left, right):
    return lax.dot_general(left, right, (((0,), (0,)), ((), ())), preferred_element_type=F32)


def rms_parts(values):
    return lax.rsqrt(jnp.mean(values * values, -1, keepdims=True) + EPS)


def rms_back(values, scale, gain, grad):
    weighted = grad * gain
    unit_rows = values * scale
    inner = jnp.mean(weighted * unit_rows, -1, keepdims=True)
    return scale * (weighted - unit_rows * inner), jnp.sum(grad * unit_rows, 0)


def body(
    tokens,
    cotangent,
    lengths,
    norm_gains,
    w_in,
    w_ab,
    conv_weight,
    gate_params,
    onorm_gain,
    w_o,
    w_gu,
    w_down,
):
    shards, seqs, replicas = (lax.axis_size(name) for name in EVERY)
    shard, seq = lax.axis_index("shard"), lax.axis_index("seq")
    owners = shards * seqs
    owner = shard * seqs + seq
    micro, row = tokens.shape[0], tokens.shape[1]
    flat = micro * row
    length = row * seqs
    heads = HEADS // seqs
    depth = D // shards
    key_width, value_width = heads * DK, heads * DV
    place = jnp.reshape(seq, (1,)).astype(jnp.int32)

    def blocks(value, count, axis=1):
        return [part_of(value, jnp.bitwise_xor(shard, step), count, axis) for step in range(count)]

    small = jnp.concatenate([norm_gains.reshape(-1), conv_weight.reshape(-1), w_ab.reshape(-1)])
    small = lax.all_gather(small, "shard")
    cuts = (norm_gains.size, norm_gains.size + conv_weight.size)
    gains = jnp.swapaxes(small[:, : cuts[0]].reshape(shards, 2, depth), 0, 1).reshape(2, D)
    gains = gains.astype(F32)
    taps_full = jnp.swapaxes(small[:, cuts[0] : cuts[1]].reshape(shards, KERNEL, -1), 0, 1)
    taps_full = taps_full.reshape(KERNEL, CONVW)
    ab_full = small[:, cuts[1] :].reshape(D, 2 * HEADS)

    def head_columns(value):
        return [
            part_of(value[..., :KD], seq, seqs, value.ndim - 1),
            part_of(value[..., KD : 2 * KD], seq, seqs, value.ndim - 1),
            part_of(value[..., 2 * KD : CONVW], seq, seqs, value.ndim - 1),
        ]

    in_own = jnp.concatenate(head_columns(w_in) + [part_of(w_in[:, CONVW:], seq, seqs, 1)], 1)
    in_parts = around(in_own, "shard")
    taps = jnp.concatenate(head_columns(taps_full), 1).astype(F32)
    out_parts = around(w_o, "shard")
    ff_shard = FF // shards

    def gate_up_columns(index):
        return jnp.concatenate(
            [part_of(w_gu[:, :FF], index, shards, 1), part_of(w_gu[:, FF:], index, shards, 1)], 1
        )

    gu_parts = [gate_up_columns(shard)] + [
        swapped(gate_up_columns(jnp.bitwise_xor(shard, step)), "shard", step)
        for step in range(1, shards)
    ]

    pieces = jnp.stack(around(tokens, "seq"))
    flat_all = pieces.reshape(seqs * flat, D).astype(F32)
    normed = (flat_all * rms_parts(flat_all) * gains[0]).astype(BF16)
    projected = sum(dot(left, right) for left, right in zip(blocks(normed, shards), in_parts))
    projected = projected.reshape(seqs, micro, row, -1)
    rate_in = dot(normed, ab_full).reshape(seqs, micro, row, 2, HEADS)
    rate_in = part_of(rate_in, seq, seqs, 4)
    rate_in = jnp.stack(settled(list(rate_in), seq))
    rate_in = jnp.transpose(rate_in, (3, 1, 4, 0, 2)).reshape(2, micro, heads, length)
    position = jnp.arange(length, dtype=jnp.int32)
    valid = (position[None, :] < lengths[:, None]).astype(F32)[:, None, :]
    own_params = part_of(gate_params, seq, seqs, 1)[:, None, :, None]
    rate_shifted = rate_in[0] + own_params[1]
    decays = -jnp.exp(own_params[0]) * jax.nn.softplus(rate_shifted) * valid
    written = jax.nn.sigmoid(rate_in[1])
    rates = jnp.stack([jnp.maximum(decays, LOWEST_DECAY), written * valid], 2)
    rates = jnp.pad(rates, ((0, 0), (0, 0), (0, 6), (0, 0)))
    gain_row = onorm_gain.reshape(1, DV)
    gated, inverse, update = mixer_forward(place, projected, taps, rates, gain_row)

    mixed_parts = [gated[0]] + [swapped(gated[step], "seq", step) for step in range(1, seqs)]
    mixed_in = jnp.concatenate(settled(mixed_parts, seq), -1).reshape(flat, VD)
    flat_in = tokens.reshape(flat, D).astype(F32)
    middle = flat_in + sum(
        dot(left, right) for left, right in zip(blocks(mixed_in, shards), out_parts)
    )
    middle_scale = rms_parts(middle)
    renormed = (middle * middle_scale * gains[1]).astype(BF16)

    upstream = cotangent.reshape(flat, D)
    pair_up = jnp.concatenate(around(upstream, "shard"), 0)
    hidden_grad = dot_rows(pair_up, w_down)
    pair_renormed = jnp.concatenate(around(renormed, "shard"), 0)
    gate_up = sum(dot(left, right) for left, right in zip(blocks(pair_renormed, shards), gu_parts))

    def feed_forward(gate_up_rows, grad_rows):
        width = gate_up_rows.shape[1] // 2
        gate, up = gate_up_rows[:, :width], gate_up_rows[:, width:]
        slope = jax.nn.sigmoid(gate)
        hidden_rows = (gate * slope * up).astype(BF16)
        gate_grad = grad_rows * up * (slope * (1.0 + gate * (1.0 - slope)))
        return hidden_rows, gate_grad.astype(BF16), (grad_rows * gate * slope).astype(BF16)

    hidden, gate_grad, up_grad = feed_forward(gate_up, hidden_grad)
    gate_up_grad = jnp.concatenate([gate_grad, up_grad], 1)

    def scattered(parts):
        return parts[0] + sum(
            swapped(parts[step], "shard", step) for step in range(1, len(parts))
        )

    column_parts = [dot_rows(gate_up_grad, part).reshape(shards, flat, depth) for part in gu_parts]
    rows_for = [
        jnp.concatenate([column_parts[step ^ at][step] for at in range(shards)], 1)
        for step in range(shards)
    ]
    renormed_grad = scattered(rows_for)
    renormed_grad = jnp.concatenate(
        settled([renormed_grad[:, at * depth : (at + 1) * depth] for at in range(shards)], shard), 1
    )
    middle_grad, gain2_grad = rms_back(middle, middle_scale, gains[1], renormed_grad)
    middle_grad = middle_grad + upstream.astype(F32)
    mixed_grad = middle_grad.astype(BF16)
    down_rows = dot(hidden, w_down).reshape(shards, flat, D)
    result = middle + scattered(list(down_rows))
    results = result.astype(BF16).reshape(micro, row, D)

    gated_grad = [dot_rows(mixed_grad, part).astype(BF16) for part in out_parts]
    gated_grad = jnp.concatenate(settled(gated_grad, shard), 1)
    grad_parts = [
        swapped(part_of(gated_grad, jnp.bitwise_xor(seq, step), seqs, 1), "seq", step)
        if step
        else part_of(gated_grad, seq, seqs, 1)
        for step in range(seqs)
    ]
    grad_parts = jnp.stack(grad_parts).reshape(seqs, micro, row, value_width)
    dq, dk, dv, dg, small_grad = mixer_backward(
        place, projected, taps, rates, gain_row, inverse, update, grad_parts
    )
    rows_all = seqs * flat
    types = [item.reshape(rows_all, -1) for item in (dq, dk, dv, dg)]
    proj_grad = jnp.concatenate(types, 1)
    decay_grad = small_grad[:, :, 5, :length]
    write_grad = small_grad[:, :, 6, :length]
    shifted_grad = decay_grad * -jnp.exp(own_params[0]) * jax.nn.sigmoid(rate_shifted) * valid
    params_grad = jnp.stack(
        [jnp.sum(decay_grad * decays, (0, 2)), jnp.sum(shifted_grad, (0, 2))]
    )
    rate_grad = jnp.stack([shifted_grad, write_grad * written * (1.0 - written) * valid])
    rate_grad = jnp.transpose(rate_grad.reshape(2, micro, heads, seqs, row), (3, 1, 4, 0, 2))
    rate_grad = jnp.stack(settled(list(rate_grad), seq))
    wide_rates = jnp.zeros((seqs, micro, row, 2, HEADS), F32)
    wide_rates = lax.dynamic_update_slice_in_dim(wide_rates, rate_grad, seq * heads, 4)
    wide_rates = wide_rates.reshape(rows_all, 2 * HEADS)
    grad_ab = lax.dot_general(
        normed.astype(F32), wide_rates, (((0,), (0,)), ((), ())), precision=HIGHEST
    )
    ab_blocks = blocks(ab_full.astype(F32), shards, 0)
    normed_grad = [
        dot_rows(proj_grad, part)
        + lax.dot_general(wide_rates, ab, (((1,), (1,)), ((), ())), precision=HIGHEST)
        for part, ab in zip(in_parts, ab_blocks)
    ]
    normed_grad = jnp.concatenate(settled(normed_grad, shard), 1).reshape(seqs, flat, D)
    normed_grad = normed_grad[0] + sum(
        swapped(normed_grad[step].astype(BF16), "seq", step).astype(F32)
        for step in range(1, seqs)
    )
    inputs_grad, gain1_grad = rms_back(flat_in, rms_parts(flat_in), gains[0], normed_grad)
    input_grads = (inputs_grad + middle_grad).astype(BF16).reshape(micro, row, D)

    def type_part(index):
        return jnp.concatenate([part_of(item, index, shards, 1) for item in types], 1)

    pair_proj = jnp.concatenate(
        [type_part(shard)]
        + [
            swapped(type_part(jnp.bitwise_xor(shard, step)), "shard", step)
            for step in range(1, shards)
        ],
        0,
    )
    pair_normed = jnp.concatenate(around(normed, "shard"), 0)
    grad_in = dot_cols(pair_normed, pair_proj).astype(BF16)
    width = grad_in.shape[1]
    slice_rows = D // (owners * replicas)
    grad_in = grad_in.reshape(owners, replicas, slice_rows, width)
    grad_in = jnp.swapaxes(grad_in, 0, 1).reshape(replicas, owners * slice_rows, width)
    grad_in = lax.psum_scatter(grad_in, "replica", scatter_dimension=0, tiled=False)
    grad_in = lax.all_to_all(
        grad_in.reshape(owners, slice_rows, width), GROUP, split_axis=0, concat_axis=0, tiled=False
    )
    grad_in = lax.all_gather(grad_in, "replica", axis=0)
    grad_in = grad_in.reshape(replicas, shards, seqs, slice_rows, width)
    grad_in = jnp.transpose(grad_in, (0, 3, 2, 1, 4)).reshape(D // owners, seqs, shards, width)
    key_part, value_part = key_width // shards, value_width // shards
    edges = (0, key_part, 2 * key_part, 2 * key_part + value_part, width)
    grad_in = jnp.concatenate(
        [
            grad_in[..., low:high].reshape(D // owners, -1)
            for low, high in zip(edges[:-1], edges[1:])
        ],
        1,
    ).astype(F32)

    mixed_own = lax.all_to_all(mixed_in, GROUP, split_axis=1, concat_axis=0, tiled=True)
    mid_piece = lax.all_gather(mixed_grad, GROUP, axis=0, tiled=True)
    grad_out = lax.psum(dot_cols(mixed_own, mid_piece).astype(BF16), "replica").astype(F32)

    all_up = lax.all_gather(upstream, EVERY, axis=0, tiled=True)
    all_renormed = lax.all_gather(renormed, EVERY, axis=0, tiled=True)
    own_down = part_of(w_down, seq, seqs, 0)
    own_gu = [
        jnp.concatenate(
            [part_of(part[:, :ff_shard], seq, seqs, 1), part_of(part[:, ff_shard:], seq, seqs, 1)],
            1,
        )
        for part in gu_parts
    ]
    own_hidden_grad = dot_rows(all_up, own_down)
    own_gate_up = sum(
        dot(left, right) for left, right in zip(blocks(all_renormed, shards), own_gu)
    )
    own_hidden, own_gate_grad, own_up_grad = feed_forward(own_gate_up, own_hidden_grad)
    grad_down = dot_cols(own_hidden, all_up)
    grad_gu = jnp.concatenate(
        [dot_cols(all_renormed, own_gate_grad), dot_cols(all_renormed, own_up_grad)], 1
    ).astype(BF16)
    grad_gu = lax.all_to_all(
        grad_gu.reshape(owners, D // owners, 2 * (FF // owners)),
        GROUP,
        split_axis=0,
        concat_axis=0,
        tiled=False,
    )
    grad_gu = jnp.transpose(
        grad_gu.reshape(owners, D // owners, 2, FF // owners), (1, 2, 0, 3)
    ).reshape(D // owners, 2 * FF).astype(F32)

    taps_grad = jnp.sum(small_grad[:, :, :KERNEL], 0)
    conv_grad = jnp.zeros((KERNEL, CONVW), F32)
    for low, high, start in ((0, DK, 0), (DK, 2 * DK, KD), (2 * DK, 2 * DK + DV, 2 * KD)):
        rows_in = jnp.swapaxes(taps_grad[..., low:high], 0, 1).reshape(KERNEL, -1)
        conv_grad = lax.dynamic_update_slice_in_dim(
            conv_grad, rows_in, start + seq * rows_in.shape[1], 1
        )
    onorm_grad = jnp.sum(small_grad[:, :, 4, :DV], (0, 1))
    wide_params = lax.dynamic_update_slice_in_dim(
        jnp.zeros((2, HEADS), F32), params_grad, seq * heads, 1
    )
    params_total, onorm_total, gains_total, conv_total, ab_total = lax.psum(
        (wide_params, onorm_grad, jnp.stack([gain1_grad, gain2_grad]), conv_grad, grad_ab), EVERY
    )
    gains_own = part_of(gains_total, owner, owners, 1)
    ab_own = part_of(ab_total, owner, owners, 0)
    conv_own = part_of(conv_total, owner, owners, 1)
    return (
        results,
        input_grads,
        gains_own,
        grad_in,
        ab_own,
        conv_own,
        params_total,
        onorm_total,
        grad_out,
        grad_gu,
        grad_down,
    )


def solution(mesh):
    in_specs = (
        P(("shard", "replica"), "seq", None),
        P(("shard", "replica"), "seq", None),
        P(("shard", "replica")),
        P(None, "shard"),
        P("shard", None),
        P("shard", None),
        P(None, "shard"),
        P(),
        P(),
        P("shard", None),
        P("shard", None),
        P("shard", None),
    )
    out_specs = (
        P(("shard", "replica"), "seq", None),
        P(("shard", "replica"), "seq", None),
        P(None, ("shard", "seq")),
        P(("shard", "seq"), None),
        P(("shard", "seq"), None),
        P(None, ("shard", "seq")),
        P(),
        P(),
        P(("shard", "seq"), None),
        P(("shard", "seq"), None),
        P(("shard", "seq"), None),
    )
    return jax.shard_map(body, mesh=mesh, in_specs=in_specs, out_specs=out_specs, check_vma=False)
```

```python
import functools

import jax
import jax.numpy as jnp
from jax import lax
from jax.experimental import pallas as pl
from jax.experimental.pallas import tpu as pltpu
from jax.sharding import PartitionSpec as P

D = 2048
HEADS = 16
DK = 128
DV = 256
FF = 5632
KERNEL = 4
KD = 2048
VD = 4096
CONVW = 8192
PROJW = 12288
EPS = 1e-06
HIGHEST = lax.Precision.HIGHEST
LOWEST_DECAY = -104.0
F32 = jnp.float32
BF16 = jnp.bfloat16
EVERY = ("shard", "seq", "replica")
GROUP = ("shard", "seq")


def mm(left, right, dims=((1,), (0,))):
    return lax.dot_general(
        left.astype(BF16), right.astype(BF16), (dims, ((), ())), preferred_element_type=F32
    )


def split(value):
    high = value.astype(BF16)
    return high, (value - high.astype(F32)).astype(BF16)


def mm3s(left, right, dims=((1,), (0,))):
    return (
        mm(left[0], right[0], dims) + mm(left[0], right[1], dims) + mm(left[1], right[0], dims)
    )


def mm3(left, right, dims=((1,), (0,))):
    return mm3s(split(left), split(right), dims)


ROWS_ROWS = ((1,), (1,))
COLS_COLS = ((0,), (0,))


def delayed(value, steps, rows):
    if steps == 0:
        return value
    return jnp.where(rows >= steps, pltpu.roll(value, steps, 0), 0.0)


def advanced(value, steps, rows):
    if steps == 0:
        return value
    length = value.shape[0]
    return jnp.where(rows < length - steps, pltpu.roll(value, length - steps, 0), 0.0)


def convolved(source, taps, rows):
    mixed = taps[KERNEL - 1 : KERNEL] * source
    for offset in range(KERNEL - 1):
        mixed = mixed + taps[offset : offset + 1] * delayed(source, KERNEL - 1 - offset, rows)
    return mixed


def unit(value):
    scale = lax.rsqrt(jnp.sum(value * value, -1, keepdims=True) + EPS)
    return value * scale, scale


def decay_matrices(rates):
    length = rates.shape[1]
    row_ids = lax.broadcasted_iota(jnp.int32, (length, length), 0)
    col_ids = lax.broadcasted_iota(jnp.int32, (length, length), 1)
    decay_row = rates[0:1]
    rate_row = rates[1:2]
    diagonal = row_ids == col_ids
    running = jnp.sum(jnp.where(row_ids >= col_ids, decay_row, 0.0), 1, keepdims=True)
    running_row = jnp.sum(jnp.where(diagonal, running, 0.0), 0, keepdims=True)
    rate = jnp.sum(jnp.where(diagonal, rate_row, 0.0), 1, keepdims=True)
    spread = jnp.minimum(running - running_row, 0.0)
    weight = jnp.where(row_ids >= col_ids, jnp.exp(spread), 0.0)
    return row_ids, col_ids, rate, weight


def lower_inverses(systems, row_ids, col_ids):
    length = row_ids.shape[0]
    eye = (row_ids == col_ids).astype(F32)
    same = jnp.bitwise_xor(row_ids, col_ids)
    inverses = [eye - jnp.where(same < 2, system, 0.0) for system in systems]
    size = 2
    while size < length:
        level = (same >= size) & (same < 2 * size)
        halves = [split(inverse) for inverse in inverses]
        inner = [
            mm3s(split(jnp.where(level, system, 0.0)), half)
            for system, half in zip(systems, halves)
        ]
        inverses = [
            inverse - mm3s(half, split(item))
            for inverse, half, item in zip(inverses, halves, inner)
        ]
        size *= 2
    return inverses


def head_inputs(source, taps):
    rows = lax.broadcasted_iota(jnp.int32, (source.shape[0], 1), 0)
    cuts = (0, DK, 2 * DK, 2 * DK + DV)
    raw = [source[:, low:high].astype(BF16).astype(F32) for low, high in zip(cuts, cuts[1:])]
    mixed = [convolved(item, kernel, rows) for item, kernel in zip(raw, taps)]
    slopes = [jax.nn.sigmoid(item) for item in mixed]
    query_unit, query_scale = unit(mixed[0] * slopes[0])
    key_rows, key_scale = unit(mixed[1] * slopes[1])
    values = mixed[2] * slopes[2]
    queries = query_unit * DK ** (-0.5)
    return raw, rows, mixed, slopes, queries, key_rows, values, query_unit, query_scale, key_scale


def slot_rows(ref, place, slot, low, high):
    pieces = ref.shape[0]
    return jnp.concatenate(
        [ref[jnp.bitwise_xor(place, j), slot, :, low:high] for j in range(pieces)], 0
    )


def taps_of(refs, head):
    return [
        ref[:, head * width : (head + 1) * width].astype(F32)
        for ref, width in zip(refs, (DK, DK, DV))
    ]


def forward_kernel(
    place_ref, proj_ref, taps_q, taps_k, taps_v, rates_ref, gain_ref, *outs
):
    *gated_refs, inverse_ref, update_ref, kept = outs
    place = place_ref[0]
    micro, together = rates_ref.shape[0], rates_ref.shape[1]
    pairs = [(slot, head) for slot in range(micro) for head in range(together)]
    work = []
    for slot, head in pairs:
        source = slot_rows(proj_ref, place, slot, head * HEAD_WIDTH, (head + 1) * HEAD_WIDTH)
        items = head_inputs(source, taps_of((taps_q, taps_k, taps_v), head))
        queries, key_rows, values = items[4:7]
        row_ids, col_ids, rate, weight = decay_matrices(rates_ref[slot, head])
        system = jnp.where(
            row_ids > col_ids, rate * mm3(key_rows, key_rows, ROWS_ROWS) * weight, 0.0
        )
        scores = (mm(queries, key_rows, ROWS_ROWS) * weight).astype(BF16)
        gate = source[:, 2 * DK + DV :]
        work.append((system, scores, rate * values, gate * jax.nn.sigmoid(gate)))
    inverses = lower_inverses([item[0] for item in work], row_ids, col_ids)
    row = proj_ref.shape[2]
    for (slot, head), item, inverse in zip(pairs, work, inverses):
        update = mm3(inverse, item[2])
        outputs = mm(item[1], update)
        scaled = (
            outputs
            * lax.rsqrt(jnp.mean(outputs * outputs, -1, keepdims=True) + EPS)
            * gain_ref[...]
        )
        inverse_ref[slot, head] = inverse
        update_ref[slot, head] = update
        kept[...] = (scaled * item[3]).reshape(kept.shape)
        for step, ref in enumerate(gated_refs):
            ref[slot, :, head * DV : (head + 1) * DV] = kept[jnp.bitwise_xor(place, step)].astype(
                ref.dtype
            )


def unit_back(grad, direction, scale):
    return scale * (grad - direction * jnp.sum(grad * direction, -1, keepdims=True))


def backward_kernel(
    place_ref, proj_ref, taps_q, taps_k, taps_v, rates_ref, gain_ref, inverse_ref, update_ref,
    *refs,
):
    *grad_refs, dproj_ref, small_ref, taken, kept = refs
    place = place_ref[0]
    micro, together = rates_ref.shape[0], rates_ref.shape[1]
    small_ref[...] = jnp.zeros_like(small_ref)
    for slot in range(micro):
        for head in range(together):
            backward_head(
                place, slot, head, proj_ref, (taps_q, taps_k, taps_v), rates_ref, gain_ref,
                inverse_ref, update_ref, grad_refs, dproj_ref, small_ref,
                taken.at[slot, head], kept.at[slot, head],
            )


def backward_head(
    place, slot, head, proj_ref, taps_refs, rates_ref, gain_ref, inverse_ref, update_ref,
    grad_refs, dproj_ref, small_ref, taken, kept,
):
    source = slot_rows(proj_ref, place, slot, head * HEAD_WIDTH, (head + 1) * HEAD_WIDTH)
    taps = taps_of(taps_refs, head)
    raw, rows, mixed, slopes, queries, key_rows, values, query_unit, query_scale, key_scale = (
        head_inputs(source, taps)
    )
    for step, ref in enumerate(grad_refs):
        taken[jnp.bitwise_xor(place, step)] = ref[slot, :, head * DV : (head + 1) * DV]
    upstream = jnp.concatenate([taken[j] for j in range(len(grad_refs))], 0).astype(F32)
    row_ids, col_ids, rate, weight = decay_matrices(rates_ref[slot, head])
    inner = mm3(key_rows, key_rows, ROWS_ROWS)
    strict = row_ids > col_ids
    keyed = jnp.where(strict, inner * weight, 0.0)
    scores = mm(queries, key_rows, ROWS_ROWS) * weight
    inverse = inverse_ref[slot, head]
    update = update_ref[slot, head]
    outputs = mm(scores, update)
    gate = source[:, 2 * DK + DV :]
    gate_slope = jax.nn.sigmoid(gate)
    out_scale = lax.rsqrt(jnp.mean(outputs * outputs, -1, keepdims=True) + EPS)
    out_unit = outputs * out_scale
    gain = gain_ref[...]
    scaled_grad = upstream * (gate * gate_slope)
    gate_grad = upstream * out_unit * gain * (gate_slope * (1.0 + gate * (1.0 - gate_slope)))
    gain_grad = jnp.sum(scaled_grad * out_unit, 0, keepdims=True)
    unit_grad = scaled_grad * gain
    out_grad = out_scale * (
        unit_grad - out_unit * jnp.mean(unit_grad * out_unit, -1, keepdims=True)
    )
    scores_grad = jnp.where(row_ids >= col_ids, mm(out_grad, update, ROWS_ROWS), 0.0)
    update_grad = mm(scores, out_grad, COLS_COLS)
    target_grad = mm3(inverse, update_grad, COLS_COLS)
    system_grad = jnp.where(strict, -mm(target_grad, update, ROWS_ROWS), 0.0)
    value_grad = rate * target_grad
    keyed_grad = system_grad * keyed
    rate_grad = jnp.sum(target_grad * values, 1, keepdims=True) + jnp.sum(
        keyed_grad, 1, keepdims=True
    )
    spread_grad = keyed_grad * rate + scores_grad * scores
    inner_grad = system_grad * weight * rate
    raw_scores_grad = scores_grad * weight
    query_grad = mm(raw_scores_grad, key_rows) * DK ** (-0.5)
    key_grad = (
        mm(raw_scores_grad, queries, COLS_COLS)
        + mm(inner_grad, key_rows)
        + mm(inner_grad, key_rows, COLS_COLS)
    )
    diagonal = row_ids == col_ids
    column_sum = jnp.sum(spread_grad, 0, keepdims=True)
    running_grad = jnp.sum(spread_grad, 1, keepdims=True) - jnp.sum(
        jnp.where(diagonal, column_sum, 0.0), 1, keepdims=True
    )
    decay_grad = jnp.sum(jnp.where(row_ids >= col_ids, running_grad, 0.0), 0, keepdims=True)
    rate_grad_row = jnp.sum(jnp.where(diagonal, rate_grad, 0.0), 0, keepdims=True)
    active_grads = (
        unit_back(query_grad, query_unit, query_scale),
        unit_back(key_grad, key_rows, key_scale),
        value_grad,
    )
    cuts = (0, DK, 2 * DK, 2 * DK + DV, HEAD_WIDTH)
    for low, high, grad_out, plain, before, slope, kernel in zip(
        cuts, cuts[1:], active_grads, raw, mixed, slopes, taps
    ):
        mixed_grad = grad_out * (slope * (1.0 + before * (1.0 - slope)))
        total = kernel[KERNEL - 1 : KERNEL] * mixed_grad
        for offset in range(KERNEL):
            steps = KERNEL - 1 - offset
            if steps:
                total = total + kernel[offset : offset + 1] * advanced(mixed_grad, steps, rows)
            small_ref[slot, head, offset : offset + 1, low:high] = jnp.sum(
                mixed_grad * delayed(plain, steps, rows), 0, keepdims=True
            )
        kept[:, :, low:high] = total.reshape(kept.shape[:2] + (high - low,))
    kept[:, :, cuts[3] : cuts[4]] = gate_grad.reshape(kept.shape[:2] + (DV,))
    for step in range(kept.shape[0]):
        dproj_ref[step, slot, :, head * HEAD_WIDTH : (head + 1) * HEAD_WIDTH] = kept[
            jnp.bitwise_xor(place, step)
        ].astype(dproj_ref.dtype)
    small_ref[slot, head, 4:5, 0:DV] = gain_grad
    length = decay_grad.shape[1]
    small_ref[slot, head, 5:6, 0:length] = decay_grad
    small_ref[slot, head, 6:7, 0:length] = rate_grad_row


VMEM_LIMIT = 56 * 1024 * 1024
HEAD_WIDTH = 2 * DK + 2 * DV
SMALL_ROWS = 8


def mixer_specs(pieces, micro, row, heads, length, together):
    def slots(width):
        return pl.BlockSpec((micro, row, together * width), lambda h, place: (0, 0, h))

    def taps(width, first):
        at = first // (together * width)
        return pl.BlockSpec(
            (KERNEL, together * width),
            lambda h, place: (0, at + place[0] * (heads // together) + h),
        )

    proj = pl.BlockSpec(
        (pieces, micro, row, together * HEAD_WIDTH), lambda h, place: (0, 0, 0, h)
    )
    kernel = [taps(DK, 0), taps(DK, KD), taps(DV, 2 * KD)]
    rates = pl.BlockSpec((micro, together, SMALL_ROWS, length), lambda h, place: (0, h, 0, 0))
    gain = pl.BlockSpec((1, DV), lambda h, place: (0, 0))

    def square(width):
        return pl.BlockSpec((micro, together, length, width), lambda h, place: (0, h, 0, 0))

    return slots, proj, kernel, rates, gain, square


def mixer_forward(place, projected, taps, rates, gain, together):
    pieces, micro, row, _ = projected.shape
    heads, length = rates.shape[1], rates.shape[3]
    slots, proj, kernel, rate_spec, gain_spec, square = mixer_specs(
        pieces, micro, row, heads, length, together
    )
    return pl.pallas_call(
        forward_kernel,
        grid_spec=pltpu.PrefetchScalarGridSpec(
            num_scalar_prefetch=1,
            grid=(heads // together,),
            in_specs=[proj] + kernel + [rate_spec, gain_spec],
            out_specs=[slots(DV)] * pieces + [square(length), square(DV)],
            scratch_shapes=[pltpu.VMEM((pieces, row, DV), F32)],
        ),
        out_shape=[jax.ShapeDtypeStruct((micro, row, heads * DV), BF16)] * pieces
        + [
            jax.ShapeDtypeStruct((micro, heads, length, length), F32),
            jax.ShapeDtypeStruct((micro, heads, length, DV), F32),
        ],
        compiler_params=pltpu.CompilerParams(vmem_limit_bytes=VMEM_LIMIT),
        name="mixer_forward",
    )(place, projected, taps, taps, taps, rates, gain)


def mixer_backward(place, projected, taps, rates, gain, inverse, update, grads, together):
    pieces, micro, row, _ = projected.shape
    heads, length = rates.shape[1], rates.shape[3]
    slots, proj, kernel, rate_spec, gain_spec, square = mixer_specs(
        pieces, micro, row, heads, length, together
    )
    small_width = 2 * DK + DV
    return pl.pallas_call(
        backward_kernel,
        grid_spec=pltpu.PrefetchScalarGridSpec(
            num_scalar_prefetch=1,
            grid=(heads // together,),
            in_specs=[proj]
            + kernel
            + [rate_spec, gain_spec, square(length), square(DV)]
            + [slots(DV)] * pieces,
            out_specs=[
                proj,
                pl.BlockSpec(
                    (micro, together, SMALL_ROWS, small_width), lambda h, place: (0, h, 0, 0)
                ),
            ],
            scratch_shapes=[
                pltpu.VMEM((micro, together, pieces, row, DV), BF16),
                pltpu.VMEM((micro, together, pieces, row, HEAD_WIDTH), F32),
            ],
        ),
        out_shape=[
            jax.ShapeDtypeStruct((pieces, micro, row, heads * HEAD_WIDTH), BF16),
            jax.ShapeDtypeStruct((micro, heads, SMALL_ROWS, small_width), F32),
        ],
        compiler_params=pltpu.CompilerParams(vmem_limit_bytes=VMEM_LIMIT),
        name="mixer_backward",
    )(place, projected, taps, taps, taps, rates, gain, inverse, update, *grads)


def pick_kernel(place_ref, q_ref, k_ref, v_ref, g_ref, out_ref):
    at = 0
    for ref in (q_ref, k_ref, v_ref, g_ref):
        out_ref[:, at : at + ref.shape[1]] = ref[...]
        at += ref.shape[1]


def pick_heads(place, w_in, heads):
    depth = w_in.shape[0]

    def one(width, first):
        at = first // width
        return pl.BlockSpec((depth, width), lambda h, place: (0, at + place[0] * heads + h))

    return pl.pallas_call(
        pick_kernel,
        grid_spec=pltpu.PrefetchScalarGridSpec(
            num_scalar_prefetch=1,
            grid=(heads,),
            in_specs=[one(DK, 0), one(DK, KD), one(DV, 2 * KD), one(DV, CONVW)],
            out_specs=pl.BlockSpec((depth, HEAD_WIDTH), lambda h, place: (0, h)),
        ),
        out_shape=jax.ShapeDtypeStruct((depth, heads * HEAD_WIDTH), w_in.dtype),
        compiler_params=pltpu.CompilerParams(vmem_limit_bytes=VMEM_LIMIT),
        name="pick_heads",
    )(place, w_in, w_in, w_in, w_in)


def project_kernel(parts, pieces, place_ref, gain_ref, *refs):
    piece_refs, weight_refs = refs[:pieces], refs[pieces : pieces + parts]
    normed_ref, out_ref = refs[pieces + parts :]
    rows = piece_refs[0].shape[0]

    @pl.when(pl.program_id(0) == 0)
    def _():
        for at, ref in enumerate(piece_refs):
            values = ref[...].astype(F32)
            scale = lax.rsqrt(jnp.mean(values * values, -1, keepdims=True) + EPS)
            normed_ref[at * rows : (at + 1) * rows] = (values * scale * gain_ref[...]).astype(BF16)

    total = None
    for step, ref in enumerate(weight_refs):
        depth = ref.shape[0]
        at = pl.multiple_of(jnp.bitwise_xor(place_ref[0], step) * depth, 128)
        term = jnp.dot(normed_ref[:, pl.ds(at, depth)], ref[...], preferred_element_type=F32)
        total = term if total is None else total + term
    out_ref[...] = total


def project(shard_place, gain, piece_list, weights):
    rows, width = piece_list[0].shape
    columns = weights[0].shape[1]
    tile = HEAD_WIDTH
    pieces, parts = len(piece_list), len(weights)
    whole = pl.BlockSpec((rows, width), lambda j, place: (0, 0))
    return pl.pallas_call(
        functools.partial(project_kernel, parts, pieces),
        grid_spec=pltpu.PrefetchScalarGridSpec(
            num_scalar_prefetch=1,
            grid=(columns // tile,),
            in_specs=[pl.BlockSpec((1, width), lambda j, place: (0, 0))]
            + [whole] * pieces
            + [pl.BlockSpec((weights[0].shape[0], tile), lambda j, place: (0, j))] * parts,
            out_specs=[
                pl.BlockSpec((pieces * rows, width), lambda j, place: (0, 0)),
                pl.BlockSpec((pieces * rows, tile), lambda j, place: (0, j)),
            ],
        ),
        out_shape=[
            jax.ShapeDtypeStruct((pieces * rows, width), BF16),
            jax.ShapeDtypeStruct((pieces * rows, columns), F32),
        ],
        compiler_params=pltpu.CompilerParams(vmem_limit_bytes=VMEM_LIMIT),
        name="project",
    )(shard_place, gain, *piece_list, *weights)


def head_rows(places_ref, step, rows, group):
    width = min(rows, group)
    found = []
    for at in range(rows // width):
        first = jnp.bitwise_xor(places_ref[1], step) * rows + at * width
        whose = jnp.bitwise_xor(first // group, places_ref[0])
        found.append((whose, pl.multiple_of(first % group, 128) if width < group else 0, width))
    return found


def merge_kernel(parts, pieces, places_ref, gain_ref, tokens_ref, *refs):
    mixed_refs, weight_refs = refs[:pieces], refs[pieces : pieces + parts]
    middle_ref, normed_ref, *left_refs, gathered = refs[pieces + parts :]
    step_id = pl.program_id(0)
    group = mixed_refs[0].shape[1]

    @pl.when(step_id == 0)
    def _():
        for at, ref in enumerate(mixed_refs):
            gathered[at] = ref[...]
        height = left_refs[0].shape[1] // parts
        for at, ref in enumerate(left_refs):
            for part in range(parts):
                first = (part * pieces + jnp.bitwise_xor(places_ref[0], at)) * height
                whose = jnp.bitwise_xor(first // group, places_ref[0])
                ref[:, part * height : (part + 1) * height] = gathered[
                    whose, :, pl.ds(pl.multiple_of(first % group, 128), height)
                ]

    tile = weight_refs[0].shape[1]
    total = tokens_ref[...].astype(F32)
    for step, ref in enumerate(weight_refs):
        rows = ref.shape[0]
        for at, (whose, first, width) in enumerate(head_rows(places_ref, step, rows, group)):
            total = total + jnp.dot(
                gathered[whose, :, pl.ds(first, width)],
                ref[at * width : (at + 1) * width],
                preferred_element_type=F32,
            )
    middle_ref[:, pl.ds(pl.multiple_of(step_id * tile, 128), tile)] = total

    @pl.when(step_id == pl.num_programs(0) - 1)
    def _():
        values = middle_ref[...]
        scale = lax.rsqrt(jnp.mean(values * values, -1, keepdims=True) + EPS)
        normed_ref[...] = (values * scale * gain_ref[...]).astype(BF16)


def merge(places, gain, tokens, mixed, weights):
    rows, width = tokens.shape
    tile = 512
    pieces, parts = len(mixed), len(weights)
    group = mixed[0].shape[1]
    whole = pl.BlockSpec((rows, width), lambda j, place: (0, 0))
    return pl.pallas_call(
        functools.partial(merge_kernel, parts, pieces),
        grid_spec=pltpu.PrefetchScalarGridSpec(
            num_scalar_prefetch=1,
            grid=(width // tile,),
            in_specs=[
                pl.BlockSpec((1, width), lambda j, place: (0, 0)),
                pl.BlockSpec((rows, tile), lambda j, place: (0, j)),
            ]
            + [pl.BlockSpec((rows, group), lambda j, place: (0, 0))] * pieces
            + [pl.BlockSpec((weights[0].shape[0], tile), lambda j, place: (0, j))] * parts,
            out_specs=[whole, whole]
            + [pl.BlockSpec((rows, group), lambda j, place: (0, 0))] * pieces,
            scratch_shapes=[pltpu.VMEM((pieces, rows, group), BF16)],
        ),
        out_shape=[
            jax.ShapeDtypeStruct((rows, width), F32),
            jax.ShapeDtypeStruct((rows, width), BF16),
        ]
        + [jax.ShapeDtypeStruct((rows, group), BF16)] * pieces,
        compiler_params=pltpu.CompilerParams(vmem_limit_bytes=VMEM_LIMIT),
        name="merge_heads",
    )(places, gain, tokens, *mixed, *weights)


def feed_kernel(parts, places_ref, *refs):
    normed_refs, grad_ref = refs[:parts], refs[parts]
    gate_refs, wide_refs = refs[parts + 1 : 2 * parts + 1], refs[2 * parts + 1 : 3 * parts + 1]
    outs, hidden_ref = refs[3 * parts + 1 : 4 * parts + 1], refs[4 * parts + 1]
    normed_all, grad_all = refs[4 * parts + 2 :]
    step_id = pl.program_id(0)
    rows, depth = normed_refs[0].shape[0], gate_refs[0].shape[0]

    @pl.when(step_id == 0)
    def _():
        for at in range(parts):
            where = slice(at * rows, (at + 1) * rows)
            for step in range(parts):
                first = pl.multiple_of(jnp.bitwise_xor(places_ref[1], step) * depth, 128)
                normed_all[step, where] = normed_refs[at][:, pl.ds(first, depth)]
        grad_all[...] = jnp.zeros_like(grad_all)

    gate, wide = None, None
    for step in range(parts):
        left = normed_all[step]
        one = jnp.dot(left, gate_refs[step][...], preferred_element_type=F32)
        two = jnp.dot(left, wide_refs[step][...], preferred_element_type=F32)
        gate, wide = (one, two) if gate is None else (gate + one, wide + two)
    hidden_grad = grad_ref[...]
    slope = jax.nn.sigmoid(gate)
    hidden_ref[...] = (gate * slope * wide).astype(BF16)
    gate_grad = (hidden_grad * wide * (slope * (1.0 + gate * (1.0 - slope)))).astype(BF16)
    wide_grad = (hidden_grad * gate * slope).astype(BF16)
    for step in range(parts):
        grad_all[step] += mm(gate_grad, gate_refs[step][...], ROWS_ROWS) + mm(
            wide_grad, wide_refs[step][...], ROWS_ROWS
        )

    @pl.when(step_id == pl.num_programs(0) - 1)
    def _():
        for at in range(parts):
            where = slice(at * rows, (at + 1) * rows)
            for step in range(parts):
                outs[at][step ^ at] = grad_all[step, where]


def feed(places, normed, hidden_grad, weights):
    rows, width = normed[0].shape
    parts = len(weights)
    depth = weights[0].shape[0]
    shard_columns = hidden_grad.shape[1]
    tile = 256 if shard_columns % 256 == 0 else shard_columns
    if tile == 256:
        sources = [(part, part) for part in weights]
        columns = weights[0].shape[1] // 2
        gate_at = lambda j, place: (0, place[1] * (shard_columns // tile) + j)
        wide_at = lambda j, place: (
            0,
            columns // tile + place[1] * (shard_columns // tile) + j,
        )
    else:
        shard = lax.axis_index("shard")
        sources = [
            (
                part_of(part[:, : part.shape[1] // 2], shard, parts, 1),
                part_of(part[:, part.shape[1] // 2 :], shard, parts, 1),
            )
            for part in weights
        ]
        gate_at = wide_at = lambda j, place: (0, j)
    whole = pl.BlockSpec((rows, width), lambda j, place: (0, 0))
    narrow = pl.BlockSpec((parts * rows, tile), lambda j, place: (0, j))
    return pl.pallas_call(
        functools.partial(feed_kernel, parts),
        grid_spec=pltpu.PrefetchScalarGridSpec(
            num_scalar_prefetch=1,
            grid=(shard_columns // tile,),
            in_specs=[whole] * parts
            + [narrow]
            + [pl.BlockSpec((depth, tile), gate_at)] * parts
            + [pl.BlockSpec((depth, tile), wide_at)] * parts,
            out_specs=[pl.BlockSpec((parts, rows, depth), lambda j, place: (0, 0, 0))] * parts
            + [narrow],
            scratch_shapes=[
                pltpu.VMEM((parts, parts * rows, depth), BF16),
                pltpu.VMEM((parts, parts * rows, depth), F32),
            ],
        ),
        out_shape=[jax.ShapeDtypeStruct((parts, rows, depth), F32)] * parts
        + [jax.ShapeDtypeStruct((parts * rows, shard_columns), BF16)],
        compiler_params=pltpu.CompilerParams(vmem_limit_bytes=VMEM_LIMIT),
        name="feed_forward",
    )(
        places,
        *normed,
        hidden_grad,
        *[source[0] for source in sources],
        *[source[1] for source in sources],
    )


def unmerge_kernel(parts, pieces, places_ref, gain_ref, middle_ref, up_ref, *refs):
    grad_refs, weight_refs = refs[:parts], refs[parts : 2 * parts]
    grad_out, sent_out, gain_out = refs[2 * parts : 2 * parts + 3]
    piece_outs = refs[2 * parts + 3 : 2 * parts + 3 + pieces]
    gathered = refs[-1]
    step_id = pl.program_id(0)
    depth = grad_refs[0].shape[2]

    @pl.when(step_id == 0)
    def _():
        for step in range(parts):
            first = pl.multiple_of(jnp.bitwise_xor(places_ref[1], step) * depth, 128)
            total = grad_refs[0][step]
            for ref in grad_refs[1:]:
                total = total + ref[step]
            grad_out[:, pl.ds(first, depth)] = total
        values, grad, gain = middle_ref[...], grad_out[...], gain_ref[...]
        scale = lax.rsqrt(jnp.mean(values * values, -1, keepdims=True) + EPS)
        unit_rows = values * scale
        weighted = grad * gain
        inner = jnp.mean(weighted * unit_rows, -1, keepdims=True)
        gain_out[...] = jnp.sum(grad * unit_rows, 0, keepdims=True)
        total = scale * (weighted - unit_rows * inner) + up_ref[...].astype(F32)
        grad_out[...] = total
        sent_out[...] = total.astype(BF16)

    count = pl.num_programs(0)
    group = gathered.shape[2]
    for step, ref in enumerate(weight_refs):
        width = ref.shape[0]
        first = jnp.bitwise_xor(places_ref[1], step) * (width * count) + step_id * width
        whose = jnp.bitwise_xor(first // group, places_ref[0])
        at = pl.multiple_of(first % group, 128) if width < group else 0
        gathered[whose, :, pl.ds(at, width)] = mm(sent_out[...], ref[...], ROWS_ROWS).astype(BF16)

    @pl.when(step_id == count - 1)
    def _():
        for at, ref in enumerate(piece_outs):
            ref[...] = gathered[at]


def unmerge(places, gain, middle, upstream, grads, weights, pieces):
    rows, width = middle.shape
    parts = len(weights)
    depth = grads[0].shape[2]
    group = VD // pieces
    tile = min(weights[0].shape[0], group)
    whole = pl.BlockSpec((rows, width), lambda j, place: (0, 0))
    one_row = pl.BlockSpec((1, width), lambda j, place: (0, 0))
    return pl.pallas_call(
        functools.partial(unmerge_kernel, parts, pieces),
        grid_spec=pltpu.PrefetchScalarGridSpec(
            num_scalar_prefetch=1,
            grid=(weights[0].shape[0] // tile,),
            in_specs=[one_row, whole, whole]
            + [pl.BlockSpec((parts, rows, depth), lambda j, place: (0, 0, 0))] * parts
            + [pl.BlockSpec((tile, width), lambda j, place: (j, 0))] * parts,
            out_specs=[whole, whole, one_row]
            + [pl.BlockSpec((rows, group), lambda j, place: (0, 0))] * pieces,
            scratch_shapes=[pltpu.VMEM((pieces, rows, group), BF16)],
        ),
        out_shape=[
            jax.ShapeDtypeStruct((rows, width), F32),
            jax.ShapeDtypeStruct((rows, width), BF16),
            jax.ShapeDtypeStruct((1, width), F32),
        ]
        + [jax.ShapeDtypeStruct((rows, group), BF16)] * pieces,
        compiler_params=pltpu.CompilerParams(vmem_limit_bytes=VMEM_LIMIT),
        name="split_heads",
    )(places, gain, middle, upstream, *grads, *weights)


def outer_kernel(parts, places_ref, *refs):
    left_refs, right_refs, out_refs = refs[:parts], refs[parts : 2 * parts], refs[2 * parts :]
    total = None
    for left, right in zip(left_refs, right_refs):
        term = mm(left[...], right[...], COLS_COLS)
        total = term if total is None else total + term
    (out_ref,) = out_refs
    chunks, several, height, _ = out_ref.shape
    for one in range(several):
        for at in range(chunks):
            first = (one * chunks + at) * height
            out_ref[at, one] = total[first : first + height].astype(out_ref.dtype)


def outer_products(places, lefts, own_right, rights, owners, chunks):
    rows, width = lefts[0].shape
    parts = len(lefts)
    columns = own_right.shape[1] // parts
    own = width // owners
    tile = max(own, 256)
    fixed = pl.BlockSpec((rows, columns), lambda j, place: (0, 0))
    return pl.pallas_call(
        functools.partial(outer_kernel, parts),
        grid_spec=pltpu.PrefetchScalarGridSpec(
            num_scalar_prefetch=1,
            grid=(width // tile,),
            in_specs=[pl.BlockSpec((rows, tile), lambda j, place: (0, j))] * parts
            + [pl.BlockSpec((rows, columns), lambda j, place: (0, place[1]))]
            + [fixed] * (parts - 1),
            out_specs=pl.BlockSpec(
                (chunks, tile // own, own // chunks, columns), lambda j, place: (0, j, 0, 0)
            ),
        ),
        out_shape=jax.ShapeDtypeStruct((chunks, owners, own // chunks, columns), BF16),
        compiler_params=pltpu.CompilerParams(vmem_limit_bytes=VMEM_LIMIT),
        name="outer_products",
    )(places, *lefts, own_right, *rights)


def rows_kernel(pieces, places_ref, *refs):
    left_refs, right_refs, out_ref, left, right = (
        refs[:pieces], refs[pieces : 2 * pieces], refs[2 * pieces], refs[-2], refs[-1],
    )
    rows = left_refs[0].shape[0]

    @pl.when(pl.program_id(0) == 0)
    def _():
        for at, ref in enumerate(left_refs):
            left[at * rows : (at + 1) * rows] = ref[...]

    for at, ref in enumerate(right_refs):
        right[at * rows : (at + 1) * rows] = ref[...]
    parts, height, _ = out_ref.shape
    for step in range(parts):
        first = pl.multiple_of(jnp.bitwise_xor(places_ref[1], step) * height, 128)
        out_ref[step] = mm(left[:, pl.ds(first, height)], right[...], COLS_COLS).astype(
            out_ref.dtype
        )


def own_rows(places, lefts, rights, parts):
    pieces = len(lefts)
    rows, columns = lefts[0].shape
    height = columns // parts
    width = rights[0].shape[1]
    tile = 512
    return pl.pallas_call(
        functools.partial(rows_kernel, pieces),
        grid_spec=pltpu.PrefetchScalarGridSpec(
            num_scalar_prefetch=1,
            grid=(width // tile,),
            in_specs=[pl.BlockSpec((rows, columns), lambda j, place: (0, 0))] * pieces
            + [pl.BlockSpec((rows, tile), lambda j, place: (0, j))] * pieces,
            out_specs=pl.BlockSpec((parts, height, tile), lambda j, place: (0, 0, j)),
            scratch_shapes=[
                pltpu.VMEM((pieces * rows, columns), BF16),
                pltpu.VMEM((pieces * rows, tile), BF16),
            ],
        ),
        out_shape=jax.ShapeDtypeStruct((parts, height, width), BF16),
        compiler_params=pltpu.CompilerParams(vmem_limit_bytes=VMEM_LIMIT),
        name="own_rows",
    )(places, *lefts, *rights)


def again_kernel(parts, places_ref, normed_ref, up_ref, *refs):
    gate_refs, wide_refs, down_ref = refs[:parts], refs[parts : 2 * parts], refs[2 * parts]
    hidden_ref, gate_out, wide_out = refs[-3:]
    depth = gate_refs[0].shape[0]
    gate, wide = None, None
    for step in range(parts):
        first = pl.multiple_of(jnp.bitwise_xor(places_ref[1], step) * depth, 128)
        left = normed_ref[:, pl.ds(first, depth)]
        one, two = mm(left, gate_refs[step][...]), mm(left, wide_refs[step][...])
        gate, wide = (one, two) if gate is None else (gate + one, wide + two)
    hidden_grad = mm(up_ref[...], down_ref[...], ROWS_ROWS)
    slope = jax.nn.sigmoid(gate)
    hidden_ref[...] = (gate * slope * wide).astype(BF16)
    gate_out[...] = (hidden_grad * wide * (slope * (1.0 + gate * (1.0 - slope)))).astype(BF16)
    wide_out[...] = (hidden_grad * gate * slope).astype(BF16)


def feed_again(places, normed, upstream, gates, wides, down, part, cut, before=()):
    width = normed.shape[1]
    count = normed.shape[0] // cut
    parts = len(gates)
    depth, columns = gates[0].shape
    tile = 256
    rows = pl.BlockSpec((tile, width), lambda j, place: (part * (count // tile) + j, 0))
    narrow = pl.BlockSpec((tile, columns), lambda j, place: (part * (count // tile) + j, 0))
    carried = 1 + 2 + 2 * parts + 1
    fixed = pl.BlockSpec((depth, columns), lambda j, place: (0, 0))
    return pl.pallas_call(
        functools.partial(again_kernel, parts),
        grid_spec=pltpu.PrefetchScalarGridSpec(
            num_scalar_prefetch=1,
            grid=(count // tile,),
            in_specs=[rows, rows]
            + [fixed] * (2 * parts)
            + [pl.BlockSpec((columns, width), lambda j, place: (0, 0))]
            + [pl.BlockSpec(memory_space=pl.ANY)] * len(before),
            out_specs=[narrow] * 3,
        ),
        out_shape=[jax.ShapeDtypeStruct((normed.shape[0], columns), BF16)] * 3,
        input_output_aliases={carried + at: at for at in range(len(before))},
        compiler_params=pltpu.CompilerParams(vmem_limit_bytes=VMEM_LIMIT),
        name="feed_again",
    )(places, normed, upstream, *gates, *wides, down, *before)


def place_in_kernel(columns_of, head_of, in_ref, out_ref, held, sems):
    step_id = pl.program_id(0)
    slot = lax.rem(step_id, 2)

    def copies(which, where):
        found = []
        for number, (low, width, first) in enumerate(columns_of):
            at = pl.multiple_of(first + head_of(which) * width, 128)
            found.append(
                pltpu.make_async_copy(
                    held.at[where, :, pl.ds(low, width)],
                    out_ref.at[:, pl.ds(at, width)],
                    sems.at[where, number],
                )
            )
        return found

    @pl.when(step_id >= 2)
    def _():
        for copy in copies(step_id - 2, slot):
            copy.wait()

    held[slot] = in_ref[:, 0].astype(F32).reshape(held.shape[1:])
    for copy in copies(step_id, slot):
        copy.start()

    @pl.when(step_id == pl.num_programs(0) - 1)
    def _():
        for copy in copies(step_id - 1, 1 - slot) + copies(step_id, slot):
            copy.wait()


def place_in(value, seqs):
    blocks, sources, rows, columns = value.shape
    heads = HEADS // seqs
    per_source = columns // HEAD_WIDTH
    columns_of = [(0, DK, 0), (DK, DK, KD), (2 * DK, DV, 2 * KD), (2 * DK + DV, DV, CONVW)]

    def head_of(step):
        source = step // per_source
        return source % seqs * heads + source // seqs * per_source + step % per_source

    return pl.pallas_call(
        functools.partial(place_in_kernel, columns_of, head_of),
        grid=(sources * per_source,),
        in_specs=[
            pl.BlockSpec(
                (blocks, 1, rows, HEAD_WIDTH), lambda h: (0, h // per_source, 0, h % per_source)
            )
        ],
        out_specs=pl.BlockSpec(memory_space=pl.ANY),
        out_shape=jax.ShapeDtypeStruct((blocks * rows, PROJW), F32),
        scratch_shapes=[
            pltpu.VMEM((2, blocks * rows, HEAD_WIDTH), F32),
            pltpu.SemaphoreType.DMA((2, len(columns_of))),
        ],
        compiler_params=pltpu.CompilerParams(vmem_limit_bytes=VMEM_LIMIT),
        name="place_w_in",
    )(value)


def place_gu_kernel(half, gate_ref, wide_ref, out_ref):
    def put(ref):
        width = ref.shape[2]
        for at in range(ref.shape[0]):
            out_ref[:, at * width : (at + 1) * width] = ref[at].astype(F32)

    @pl.when(pl.program_id(0) < half)
    def _():
        put(gate_ref)

    @pl.when(pl.program_id(0) >= half)
    def _():
        put(wide_ref)


def place_gu(gate, wide):
    sources, rows, width = gate.shape
    together = 1
    while together * width % 128:
        together *= 2
    half = sources // together
    return pl.pallas_call(
        functools.partial(place_gu_kernel, half),
        grid=(2 * half,),
        in_specs=[
            pl.BlockSpec((together, rows, width), lambda j: (jnp.minimum(j, half - 1), 0, 0)),
            pl.BlockSpec((together, rows, width), lambda j: (jnp.maximum(j - half, 0), 0, 0)),
        ],
        out_specs=pl.BlockSpec((rows, together * width), lambda j: (0, j)),
        out_shape=jax.ShapeDtypeStruct((rows, 2 * sources * width), F32),
        compiler_params=pltpu.CompilerParams(vmem_limit_bytes=VMEM_LIMIT),
        name="place_w_gu",
    )(gate, wide)


def line_first(value):
    return lax.ppermute(value, "replica", [(0, 1), (3, 2)])


def line_second(value):
    return lax.ppermute(value, "replica", [(1, 2), (2, 1)])


def line_third(value):
    return lax.ppermute(value, "replica", [(1, 0), (2, 3)])


def added(left, right):
    return (left.astype(F32) + right.astype(F32)).astype(BF16)


def pinned(*values):
    return lax.optimization_barrier(values)


def line_sum(value):
    value = added(value, line_first(value))
    value = added(value, line_second(value))
    return settled_pair((value, line_third(value)))


def settled_pair(pair):
    place = lax.axis_index("replica")
    return jnp.where((place == 1) | (place == 2), pair[0], pair[1]).astype(F32)


def swapped(value, axis, step):
    count = lax.axis_size(axis)
    return lax.ppermute(value, axis, [(source, source ^ step) for source in range(count)])


def around(value, axis):
    return [value] + [swapped(value, axis, step) for step in range(1, lax.axis_size(axis))]


def settled(parts, index):
    stacked = jnp.stack(parts)
    return [
        lax.dynamic_index_in_dim(stacked, jnp.bitwise_xor(index, at), 0, keepdims=False)
        for at in range(len(parts))
    ]


def part_of(value, index, count, axis):
    width = value.shape[axis] // count
    return lax.dynamic_slice_in_dim(value, index * width, width, axis)


def dot(left, right):
    return jnp.dot(left, right, preferred_element_type=F32)


def dot_rows(left, right):
    return lax.dot_general(left, right, (((1,), (1,)), ((), ())), preferred_element_type=F32)


def dot_cols(left, right):
    return lax.dot_general(left, right, (((0,), (0,)), ((), ())), preferred_element_type=F32)


def rms_parts(values):
    return lax.rsqrt(jnp.mean(values * values, -1, keepdims=True) + EPS)


def rms_back(values, scale, gain, grad):
    weighted = grad * gain
    unit_rows = values * scale
    inner = jnp.mean(weighted * unit_rows, -1, keepdims=True)
    return scale * (weighted - unit_rows * inner), jnp.sum(grad * unit_rows, 0)


def body(
    tokens,
    cotangent,
    lengths,
    norm_gains,
    w_in,
    w_ab,
    conv_weight,
    gate_params,
    onorm_gain,
    w_o,
    w_gu,
    w_down,
):
    shards, seqs, replicas = (lax.axis_size(name) for name in EVERY)
    shard, seq = lax.axis_index("shard"), lax.axis_index("seq")
    owners = shards * seqs
    owner = shard * seqs + seq
    micro, row = tokens.shape[0], tokens.shape[1]
    flat = micro * row
    length = row * seqs
    heads = HEADS // seqs
    depth = D // shards
    seq_place = jnp.reshape(seq, (1,)).astype(jnp.int32)
    shard_place = jnp.reshape(shard, (1,)).astype(jnp.int32)
    places = jnp.stack([seq, shard]).astype(jnp.int32)

    def blocks(value, count, axis=1):
        return [part_of(value, jnp.bitwise_xor(shard, step), count, axis) for step in range(count)]

    flat_tokens = tokens.reshape(flat, D)
    in_own = pick_heads(seq_place, w_in, heads)
    sent_tokens, in_own = pinned(flat_tokens, in_own)
    pieces = around(sent_tokens, "seq")
    gain_parts = around(norm_gains, "shard")
    in_parts = around(in_own, "shard")
    taps_parts = around(conv_weight, "shard")
    ab_parts = around(w_ab, "shard")
    gains = jnp.concatenate(settled(gain_parts, shard), 1).astype(F32)
    gain_first, gain_second = gains[:1], gains[1:]
    taps = jnp.concatenate(settled(taps_parts, shard), 1)
    upstream = cotangent.reshape(flat, D)
    up_parts = around(upstream, "shard")
    hidden_grad = dot_rows(jnp.concatenate(up_parts, 0), w_down)
    own_out, own_gu, late_up, hidden_grad, *arrived = pinned(
        w_o, w_gu, upstream, hidden_grad, *pieces, *in_parts
    )
    pieces, in_parts = arrived[:seqs], arrived[seqs:]
    all_up = lax.all_gather(late_up, EVERY, axis=0, tiled=True)
    out_parts = around(own_out, "shard")
    gu_parts = around(own_gu, "shard")

    normed, projected = project(shard_place, gain_first, pieces, in_parts)
    rate_in = sum(dot(left, right) for left, right in zip(blocks(normed, shards), ab_parts))
    rate_in = part_of(rate_in.reshape(seqs, micro, row, 2, HEADS), seq, seqs, 4)
    rate_in = jnp.stack(settled(list(rate_in), seq))
    rate_in = jnp.transpose(rate_in, (3, 1, 4, 0, 2)).reshape(2, micro, heads, length)
    position = jnp.arange(length, dtype=jnp.int32)
    valid = (position[None, :] < lengths[:, None]).astype(F32)[:, None, :]
    own_params = part_of(gate_params, seq, seqs, 1)[:, None, :, None]
    rate_shifted = rate_in[0] + own_params[1]
    decays = -jnp.exp(own_params[0]) * jax.nn.softplus(rate_shifted) * valid
    written = jax.nn.sigmoid(rate_in[1])
    rates = jnp.stack([jnp.maximum(decays, LOWEST_DECAY), written * valid], 2)
    rates = jnp.pad(rates, ((0, 0), (0, 0), (0, SMALL_ROWS - 2), (0, 0)))
    gain_row = onorm_gain.reshape(1, DV)
    projected = projected.reshape(seqs, micro, row, -1)
    *gated, inverse, update = mixer_forward(seq_place, projected, taps, rates, gain_row, 2)
    gated = [item.reshape(flat, heads * DV) for item in gated]

    mixed_parts = [gated[0]] + [swapped(gated[step], "seq", step) for step in range(1, seqs)]
    arrived = pinned(*mixed_parts, *gu_parts)
    mixed_parts, gu_parts = list(arrived[:seqs]), list(arrived[seqs:])
    middle, renormed, *mixed_left = merge(
        places, gain_second, flat_tokens, mixed_parts, out_parts
    )
    all_renormed = lax.all_gather(renormed, EVERY, axis=0, tiled=True)

    mixed_left = [
        swapped(item, "seq", step) if step else item for step, item in enumerate(mixed_left)
    ]
    fed = feed(places, around(renormed, "shard"), hidden_grad, gu_parts)
    pair = len(fed)
    fed = list(pinned(*fed, *mixed_left))
    fed, mixed_left = fed[:pair], fed[pair:]
    grads_back = [fed[0]] + [swapped(fed[step], "shard", step) for step in range(1, shards)]
    middle_grad, mixed_grad, gain2_grad, *gated_grad = unmerge(
        places, gain_second, middle, upstream, grads_back, out_parts, seqs
    )
    hidden = fed[shards]

    ff_own = FF // owners
    own_down = part_of(w_down, seq, seqs, 0)
    own_gate = [part_of(part, owner, 2 * owners, 1) for part in gu_parts]
    own_wide = [part_of(part, owners + owner, 2 * owners, 1) for part in gu_parts]

    gated_grad = [
        swapped(item, "seq", step) if step else item for step, item in enumerate(gated_grad)
    ]
    mixed_grad, own_down, *others = pinned(
        mixed_grad, own_down, *own_gate, *own_wide, *mixed_left, *gated_grad
    )
    own_gate, own_wide = others[:shards], others[shards : 2 * shards]
    mixed_left, gated_grad = others[2 * shards : 2 * shards + seqs], others[2 * shards + seqs :]
    gated_grad = [item.reshape(micro, row, heads * DV) for item in gated_grad]
    mid_pieces = around(mixed_grad, "seq")
    proj_grad, small_grad = mixer_backward(
        seq_place, projected, taps, rates, gain_row, inverse, update, gated_grad, 1
    )
    proj_grad, *mid_pieces = pinned(proj_grad, *mid_pieces)
    rows_all = seqs * flat
    proj_grad = proj_grad.reshape(rows_all, -1)
    pair_proj = [
        swapped(part_of(proj_grad, jnp.bitwise_xor(shard, step), shards, 1), "shard", step)
        for step in range(1, shards)
    ]

    def to_group(value):
        return lax.all_to_all(value, GROUP, split_axis=0, concat_axis=0, tiled=False)

    pair_normed = around(normed, "shard")
    grad_in = outer_products(places, pair_normed, proj_grad, pair_proj, owners, replicas)
    width = grad_in.shape[3]
    proj_grad, small_grad, grad_in, *mid_pieces = pinned(
        proj_grad, small_grad, grad_in, *mid_pieces
    )

    grad_out = own_rows(places, mixed_left, mid_pieces, shards)
    grad_out = functools.reduce(
        added, [grad_out[0]] + [swapped(grad_out[step], "shard", step) for step in range(1, shards)]
    )

    def input_gradient_parts(proj_grad, small_grad):
        decay_grad = small_grad[:, :, 5, :length]
        write_grad = small_grad[:, :, 6, :length]
        shifted_grad = decay_grad * -jnp.exp(own_params[0]) * jax.nn.sigmoid(rate_shifted) * valid
        params_grad = jnp.stack(
            [jnp.sum(decay_grad * decays, (0, 2)), jnp.sum(shifted_grad, (0, 2))]
        )
        rate_grad = jnp.stack([shifted_grad, write_grad * written * (1.0 - written) * valid])
        rate_grad = jnp.transpose(rate_grad.reshape(2, micro, heads, seqs, row), (3, 1, 4, 0, 2))
        rate_grad = jnp.stack(settled(list(rate_grad), seq))
        rate_grad = rate_grad.reshape(rows_all, 2 * heads)
        grad_ab = lax.dot_general(
            rate_grad, normed.astype(F32), (((0,), (0,)), ((), ())), precision=HIGHEST
        )
        own_ab = [
            part_of(part.reshape(depth, 2, HEADS), seq, seqs, 2).reshape(depth, 2 * heads)
            for part in ab_parts
        ]
        normed_grad = [
            dot_rows(proj_grad, part)
            + lax.dot_general(
                rate_grad, ab.astype(F32), (((1,), (1,)), ((), ())), precision=HIGHEST
            )
            for part, ab in zip(in_parts, own_ab)
        ]
        return (*normed_grad, grad_ab, params_grad)

    def input_gradient(*normed_grad):
        *normed_grad, grad_ab, params_grad = normed_grad
        normed_grad = jnp.concatenate(settled(normed_grad, shard), 1).reshape(seqs, flat, D)
        normed_grad = normed_grad[0] + sum(
            swapped(normed_grad[step].astype(BF16), "seq", step).astype(F32)
            for step in range(1, seqs)
        )
        flat_in = flat_tokens.astype(F32)
        inputs_grad, gain1_grad = rms_back(flat_in, rms_parts(flat_in), gains[0], normed_grad)
        input_grads = (inputs_grad + middle_grad).astype(BF16).reshape(micro, row, D)
        return input_grads, gain1_grad, grad_ab, params_grad

    def to_group(value):
        return lax.all_to_all(value, GROUP, split_axis=0, concat_axis=0, tiled=False)

    def to_owners(value):
        return to_group(value.astype(BF16).reshape(owners, D // owners, ff_own))

    grad_out, proj_grad, small_grad = pinned(grad_out, proj_grad, small_grad)
    grad_out = lax.all_to_all(
        grad_out.reshape(replicas, -1, D), "replica", split_axis=0, concat_axis=0
    )
    normed_parts = input_gradient_parts(proj_grad, small_grad)
    grad_out, grad_in, all_renormed, all_up, *normed_parts = pinned(
        grad_out, grad_in, all_renormed, all_up, *normed_parts
    )
    grad_in = lax.psum_scatter(grad_in, "replica", scatter_dimension=0, tiled=False)
    input_grads, gain1_grad, grad_ab, params_grad = input_gradient(*normed_parts)
    gain2_grad = gain2_grad[0]
    taps_grad = jnp.sum(small_grad[:, :, :KERNEL], 0)
    conv_grad = jnp.concatenate(
        [
            jnp.swapaxes(taps_grad[..., low:high], 0, 1).reshape(KERNEL, -1)
            for low, high in ((0, DK), (DK, 2 * DK), (2 * DK, 2 * DK + DV))
        ],
        1,
    )
    onorm_grad = jnp.sum(small_grad[:, :, 4, :DV], (0, 1))
    loose = jnp.concatenate([onorm_grad, params_grad.reshape(-1)])
    loose = jnp.pad(loose, (0, D - loose.size))
    rows_ab = 2 * heads
    smalls = jnp.concatenate(
        [grad_ab, conv_grad, loose[None], gain1_grad[None], gain2_grad[None]], 0
    )
    step = 1
    while step < shards:
        smalls = smalls + swapped(smalls, "shard", step)
        step *= 2
    all_renormed, all_up, smalls, input_grads = pinned(
        all_renormed, all_up, smalls, input_grads
    )
    grad_out = jnp.sum(grad_out.astype(F32), 0).astype(BF16)
    own_hidden, gate_grad, wide_grad = feed_again(
        places, all_renormed, all_up, own_gate, own_wide, own_down, 0, 1
    )
    grad_gate = dot_cols(all_renormed, gate_grad).astype(BF16)
    grad_out, grad_in, grad_gate, wide_grad, own_hidden = pinned(
        grad_out, grad_in, grad_gate, wide_grad, own_hidden
    )
    grad_out = lax.all_gather(grad_out, "replica", axis=0, tiled=True)
    grad_in = to_group(grad_in)
    grad_wide = dot_cols(all_renormed, wide_grad).astype(BF16)
    grad_out, grad_in, grad_gate, grad_wide, own_hidden, hidden, smalls = pinned(
        grad_out, grad_in, grad_gate, grad_wide, own_hidden, hidden, smalls
    )
    grad_in = lax.all_gather(grad_in, "replica", axis=0)
    grad_gate = to_owners(grad_gate)
    grad_down = dot_cols(own_hidden, all_up)
    grad_wide, grad_gate = pinned(grad_wide, grad_gate)
    grad_wide = to_owners(grad_wide)
    step = 1
    while step < replicas:
        smalls = smalls + swapped(smalls, "replica", step)
        step *= 2
    rows_down = dot(hidden, w_down).reshape(shards, flat, D)
    result = (
        middle
        + rows_down[0]
        + sum(swapped(rows_down[step], "shard", step) for step in range(1, shards))
    )
    results = result.astype(BF16).reshape(micro, row, D)
    grad_out = grad_out.astype(F32)
    every = jnp.stack(settled(around(smalls, "seq"), seq))
    grad_gu = place_gu(grad_gate, grad_wide)
    if width % HEAD_WIDTH == 0:
        grad_in = place_in(grad_in, seqs)
    else:
        grad_in = grad_in.reshape(replicas, shards, seqs, -1, width)
        grad_in = jnp.transpose(grad_in, (0, 3, 2, 1, 4)).reshape(D // owners, HEADS, HEAD_WIDTH)
        cuts = (0, DK, 2 * DK, 2 * DK + DV, HEAD_WIDTH)
        grad_in = jnp.concatenate(
            [
                grad_in[..., low:high].reshape(D // owners, -1)
                for low, high in zip(cuts[:-1], cuts[1:])
            ],
            1,
        ).astype(F32)

    ab_total = jnp.transpose(every[:, :rows_ab].reshape(seqs, 2, heads, D), (3, 1, 0, 2))
    ab_total = ab_total.reshape(D, 2 * HEADS)
    conv_all = every[:, rows_ab : rows_ab + KERNEL]
    conv_total = jnp.concatenate(
        [
            jnp.swapaxes(conv_all[..., low:high], 0, 1).reshape(KERNEL, -1)
            for low, high in (
                (0, heads * DK),
                (heads * DK, 2 * heads * DK),
                (2 * heads * DK, heads * (2 * DK + DV)),
            )
        ],
        1,
    )
    loose_all = every[:, rows_ab + KERNEL]
    onorm_total = jnp.sum(loose_all[:, :DV], 0)
    params_total = loose_all[:, DV : DV + 2 * heads].reshape(seqs, 2, heads)
    params_total = jnp.swapaxes(params_total, 0, 1).reshape(2, HEADS)
    gains_total = jnp.sum(every[:, rows_ab + KERNEL + 1 : rows_ab + KERNEL + 3], 0)
    gains_own = part_of(gains_total, owner, owners, 1)
    ab_own = part_of(ab_total, owner, owners, 0)
    conv_own = part_of(conv_total, owner, owners, 1)
    return (
        results,
        input_grads,
        gains_own,
        grad_in,
        ab_own,
        conv_own,
        params_total,
        onorm_total,
        grad_out,
        grad_gu,
        grad_down,
    )


def solution(mesh):
    in_specs = (
        P(("shard", "replica"), "seq", None),
        P(("shard", "replica"), "seq", None),
        P(("shard", "replica")),
        P(None, "shard"),
        P("shard", None),
        P("shard", None),
        P(None, "shard"),
        P(),
        P(),
        P("shard", None),
        P("shard", None),
        P("shard", None),
    )
    out_specs = (
        P(("shard", "replica"), "seq", None),
        P(("shard", "replica"), "seq", None),
        P(None, ("shard", "seq")),
        P(("shard", "seq"), None),
        P(("shard", "seq"), None),
        P(None, ("shard", "seq")),
        P(),
        P(),
        P(("shard", "seq"), None),
        P(("shard", "seq"), None),
        P(("shard", "seq"), None),
    )
    return jax.shard_map(body, mesh=mesh, in_specs=in_specs, out_specs=out_specs, check_vma=False)
```

```python
import functools

import jax
import jax.numpy as jnp
from jax import lax
from jax.experimental import pallas as pl
from jax.experimental.pallas import tpu as pltpu
from jax.sharding import PartitionSpec as P

D = 2048
HEADS = 16
DK = 128
DV = 256
FF = 5632
KERNEL = 4
KD = 2048
VD = 4096
CONVW = 8192
PROJW = 12288
EPS = 1e-06
HIGHEST = lax.Precision.HIGHEST
LOWEST_DECAY = -104.0
F32 = jnp.float32
BF16 = jnp.bfloat16
EVERY = ("shard", "seq", "replica")
GROUP = ("shard", "seq")


def mm(left, right, dims=((1,), (0,))):
    return lax.dot_general(
        left.astype(BF16), right.astype(BF16), (dims, ((), ())), preferred_element_type=F32
    )


def split(value):
    high = value.astype(BF16)
    return high, (value - high.astype(F32)).astype(BF16)


def mm3s(left, right, dims=((1,), (0,))):
    return (
        mm(left[0], right[0], dims) + mm(left[0], right[1], dims) + mm(left[1], right[0], dims)
    )


def mm3(left, right, dims=((1,), (0,))):
    return mm3s(split(left), split(right), dims)


ROWS_ROWS = ((1,), (1,))
COLS_COLS = ((0,), (0,))


def delayed(value, steps, rows):
    if steps == 0:
        return value
    return jnp.where(rows >= steps, pltpu.roll(value, steps, 0), 0.0)


def advanced(value, steps, rows):
    if steps == 0:
        return value
    length = value.shape[0]
    return jnp.where(rows < length - steps, pltpu.roll(value, length - steps, 0), 0.0)


def convolved(source, taps, rows):
    mixed = taps[KERNEL - 1 : KERNEL] * source
    for offset in range(KERNEL - 1):
        mixed = mixed + taps[offset : offset + 1] * delayed(source, KERNEL - 1 - offset, rows)
    return mixed


def unit(value):
    scale = lax.rsqrt(jnp.sum(value * value, -1, keepdims=True) + EPS)
    return value * scale, scale


def decay_matrices(rates):
    length = rates.shape[1]
    row_ids = lax.broadcasted_iota(jnp.int32, (length, length), 0)
    col_ids = lax.broadcasted_iota(jnp.int32, (length, length), 1)
    decay_row = rates[0:1]
    rate_row = rates[1:2]
    diagonal = row_ids == col_ids
    running = jnp.sum(jnp.where(row_ids >= col_ids, decay_row, 0.0), 1, keepdims=True)
    running_row = jnp.sum(jnp.where(diagonal, running, 0.0), 0, keepdims=True)
    rate = jnp.sum(jnp.where(diagonal, rate_row, 0.0), 1, keepdims=True)
    spread = jnp.minimum(running - running_row, 0.0)
    weight = jnp.where(row_ids >= col_ids, jnp.exp(spread), 0.0)
    return row_ids, col_ids, rate, weight


def lower_inverses(systems, row_ids, col_ids):
    length = row_ids.shape[0]
    eye = (row_ids == col_ids).astype(F32)
    same = jnp.bitwise_xor(row_ids, col_ids)
    inverses = [eye - jnp.where(same < 2, system, 0.0) for system in systems]
    size = 2
    while size < length:
        level = (same >= size) & (same < 2 * size)
        halves = [split(inverse) for inverse in inverses]
        inner = [
            mm3s(split(jnp.where(level, system, 0.0)), half)
            for system, half in zip(systems, halves)
        ]
        inverses = [
            inverse - mm3s(half, split(item))
            for inverse, half, item in zip(inverses, halves, inner)
        ]
        size *= 2
    return inverses


def head_inputs(source, taps):
    rows = lax.broadcasted_iota(jnp.int32, (source.shape[0], 1), 0)
    cuts = (0, DK, 2 * DK, 2 * DK + DV)
    raw = [source[:, low:high].astype(BF16).astype(F32) for low, high in zip(cuts, cuts[1:])]
    mixed = [convolved(item, kernel, rows) for item, kernel in zip(raw, taps)]
    slopes = [jax.nn.sigmoid(item) for item in mixed]
    query_unit, query_scale = unit(mixed[0] * slopes[0])
    key_rows, key_scale = unit(mixed[1] * slopes[1])
    values = mixed[2] * slopes[2]
    queries = query_unit * DK ** (-0.5)
    return raw, rows, mixed, slopes, queries, key_rows, values, query_unit, query_scale, key_scale


def slot_rows(ref, place, slot, low, high):
    pieces = ref.shape[0]
    return jnp.concatenate(
        [ref[jnp.bitwise_xor(place, j), slot, :, low:high] for j in range(pieces)], 0
    )


def taps_of(refs, head):
    return [
        ref[:, head * width : (head + 1) * width].astype(F32)
        for ref, width in zip(refs, (DK, DK, DV))
    ]


def forward_kernel(
    place_ref, proj_ref, taps_q, taps_k, taps_v, rates_ref, gain_ref, *outs
):
    *gated_refs, inverse_ref, update_ref, kept = outs
    place = place_ref[0]
    micro, together = rates_ref.shape[0], rates_ref.shape[1]
    pairs = [(slot, head) for slot in range(micro) for head in range(together)]
    work = []
    for slot, head in pairs:
        source = slot_rows(proj_ref, place, slot, head * HEAD_WIDTH, (head + 1) * HEAD_WIDTH)
        items = head_inputs(source, taps_of((taps_q, taps_k, taps_v), head))
        queries, key_rows, values = items[4:7]
        row_ids, col_ids, rate, weight = decay_matrices(rates_ref[slot, head])
        system = jnp.where(
            row_ids > col_ids, rate * mm3(key_rows, key_rows, ROWS_ROWS) * weight, 0.0
        )
        scores = (mm(queries, key_rows, ROWS_ROWS) * weight).astype(BF16)
        gate = source[:, 2 * DK + DV :]
        work.append((system, scores, rate * values, gate * jax.nn.sigmoid(gate)))
    inverses = lower_inverses([item[0] for item in work], row_ids, col_ids)
    row = proj_ref.shape[2]
    for (slot, head), item, inverse in zip(pairs, work, inverses):
        update = mm3(inverse, item[2])
        outputs = mm(item[1], update)
        scaled = (
            outputs
            * lax.rsqrt(jnp.mean(outputs * outputs, -1, keepdims=True) + EPS)
            * gain_ref[...]
        )
        inverse_ref[slot, head] = inverse
        update_ref[slot, head] = update
        kept[...] = (scaled * item[3]).reshape(kept.shape)
        for step, ref in enumerate(gated_refs):
            ref[slot, :, head * DV : (head + 1) * DV] = kept[jnp.bitwise_xor(place, step)].astype(
                ref.dtype
            )


def unit_back(grad, direction, scale):
    return scale * (grad - direction * jnp.sum(grad * direction, -1, keepdims=True))


def backward_kernel(
    place_ref, proj_ref, taps_q, taps_k, taps_v, rates_ref, gain_ref, inverse_ref, update_ref,
    *refs,
):
    *grad_refs, dproj_ref, small_ref, taken, kept = refs
    place = place_ref[0]
    micro, together = rates_ref.shape[0], rates_ref.shape[1]
    small_ref[...] = jnp.zeros_like(small_ref)
    for slot in range(micro):
        for head in range(together):
            backward_head(
                place, slot, head, proj_ref, (taps_q, taps_k, taps_v), rates_ref, gain_ref,
                inverse_ref, update_ref, grad_refs, dproj_ref, small_ref,
                taken.at[slot, head], kept.at[slot, head],
            )


def backward_head(
    place, slot, head, proj_ref, taps_refs, rates_ref, gain_ref, inverse_ref, update_ref,
    grad_refs, dproj_ref, small_ref, taken, kept,
):
    source = slot_rows(proj_ref, place, slot, head * HEAD_WIDTH, (head + 1) * HEAD_WIDTH)
    taps = taps_of(taps_refs, head)
    raw, rows, mixed, slopes, queries, key_rows, values, query_unit, query_scale, key_scale = (
        head_inputs(source, taps)
    )
    for step, ref in enumerate(grad_refs):
        taken[jnp.bitwise_xor(place, step)] = ref[slot, :, head * DV : (head + 1) * DV]
    upstream = jnp.concatenate([taken[j] for j in range(len(grad_refs))], 0).astype(F32)
    row_ids, col_ids, rate, weight = decay_matrices(rates_ref[slot, head])
    inner = mm3(key_rows, key_rows, ROWS_ROWS)
    strict = row_ids > col_ids
    keyed = jnp.where(strict, inner * weight, 0.0)
    scores = mm(queries, key_rows, ROWS_ROWS) * weight
    inverse = inverse_ref[slot, head]
    update = update_ref[slot, head]
    outputs = mm(scores, update)
    gate = source[:, 2 * DK + DV :]
    gate_slope = jax.nn.sigmoid(gate)
    out_scale = lax.rsqrt(jnp.mean(outputs * outputs, -1, keepdims=True) + EPS)
    out_unit = outputs * out_scale
    gain = gain_ref[...]
    scaled_grad = upstream * (gate * gate_slope)
    gate_grad = upstream * out_unit * gain * (gate_slope * (1.0 + gate * (1.0 - gate_slope)))
    gain_grad = jnp.sum(scaled_grad * out_unit, 0, keepdims=True)
    unit_grad = scaled_grad * gain
    out_grad = out_scale * (
        unit_grad - out_unit * jnp.mean(unit_grad * out_unit, -1, keepdims=True)
    )
    scores_grad = jnp.where(row_ids >= col_ids, mm(out_grad, update, ROWS_ROWS), 0.0)
    update_grad = mm(scores, out_grad, COLS_COLS)
    target_grad = mm3(inverse, update_grad, COLS_COLS)
    system_grad = jnp.where(strict, -mm(target_grad, update, ROWS_ROWS), 0.0)
    value_grad = rate * target_grad
    keyed_grad = system_grad * keyed
    rate_grad = jnp.sum(target_grad * values, 1, keepdims=True) + jnp.sum(
        keyed_grad, 1, keepdims=True
    )
    spread_grad = keyed_grad * rate + scores_grad * scores
    inner_grad = system_grad * weight * rate
    raw_scores_grad = scores_grad * weight
    query_grad = mm(raw_scores_grad, key_rows) * DK ** (-0.5)
    key_grad = (
        mm(raw_scores_grad, queries, COLS_COLS)
        + mm(inner_grad, key_rows)
        + mm(inner_grad, key_rows, COLS_COLS)
    )
    diagonal = row_ids == col_ids
    column_sum = jnp.sum(spread_grad, 0, keepdims=True)
    running_grad = jnp.sum(spread_grad, 1, keepdims=True) - jnp.sum(
        jnp.where(diagonal, column_sum, 0.0), 1, keepdims=True
    )
    decay_grad = jnp.sum(jnp.where(row_ids >= col_ids, running_grad, 0.0), 0, keepdims=True)
    rate_grad_row = jnp.sum(jnp.where(diagonal, rate_grad, 0.0), 0, keepdims=True)
    active_grads = (
        unit_back(query_grad, query_unit, query_scale),
        unit_back(key_grad, key_rows, key_scale),
        value_grad,
    )
    cuts = (0, DK, 2 * DK, 2 * DK + DV, HEAD_WIDTH)
    for low, high, grad_out, plain, before, slope, kernel in zip(
        cuts, cuts[1:], active_grads, raw, mixed, slopes, taps
    ):
        mixed_grad = grad_out * (slope * (1.0 + before * (1.0 - slope)))
        total = kernel[KERNEL - 1 : KERNEL] * mixed_grad
        for offset in range(KERNEL):
            steps = KERNEL - 1 - offset
            if steps:
                total = total + kernel[offset : offset + 1] * advanced(mixed_grad, steps, rows)
            small_ref[slot, head, offset : offset + 1, low:high] = jnp.sum(
                mixed_grad * delayed(plain, steps, rows), 0, keepdims=True
            )
        kept[:, :, low:high] = total.reshape(kept.shape[:2] + (high - low,))
    kept[:, :, cuts[3] : cuts[4]] = gate_grad.reshape(kept.shape[:2] + (DV,))
    for step in range(kept.shape[0]):
        dproj_ref[step, slot, :, head * HEAD_WIDTH : (head + 1) * HEAD_WIDTH] = kept[
            jnp.bitwise_xor(place, step)
        ].astype(dproj_ref.dtype)
    small_ref[slot, head, 4:5, 0:DV] = gain_grad
    length = decay_grad.shape[1]
    small_ref[slot, head, 5:6, 0:length] = decay_grad
    small_ref[slot, head, 6:7, 0:length] = rate_grad_row


VMEM_LIMIT = 56 * 1024 * 1024
HEAD_WIDTH = 2 * DK + 2 * DV
SMALL_ROWS = 8


def mixer_specs(pieces, micro, row, heads, length, together):
    def slots(width):
        return pl.BlockSpec((micro, row, together * width), lambda h, place: (0, 0, h))

    def taps(width, first):
        at = first // (together * width)
        return pl.BlockSpec(
            (KERNEL, together * width),
            lambda h, place: (0, at + place[0] * (heads // together) + h),
        )

    proj = pl.BlockSpec(
        (pieces, micro, row, together * HEAD_WIDTH), lambda h, place: (0, 0, 0, h)
    )
    kernel = [taps(DK, 0), taps(DK, KD), taps(DV, 2 * KD)]
    rates = pl.BlockSpec((micro, together, SMALL_ROWS, length), lambda h, place: (0, h, 0, 0))
    gain = pl.BlockSpec((1, DV), lambda h, place: (0, 0))

    def square(width):
        return pl.BlockSpec((micro, together, length, width), lambda h, place: (0, h, 0, 0))

    return slots, proj, kernel, rates, gain, square


def mixer_forward(place, projected, taps, rates, gain, together):
    pieces, micro, row, _ = projected.shape
    heads, length = rates.shape[1], rates.shape[3]
    slots, proj, kernel, rate_spec, gain_spec, square = mixer_specs(
        pieces, micro, row, heads, length, together
    )
    return pl.pallas_call(
        forward_kernel,
        grid_spec=pltpu.PrefetchScalarGridSpec(
            num_scalar_prefetch=1,
            grid=(heads // together,),
            in_specs=[proj] + kernel + [rate_spec, gain_spec],
            out_specs=[slots(DV)] * pieces + [square(length), square(DV)],
            scratch_shapes=[pltpu.VMEM((pieces, row, DV), F32)],
        ),
        out_shape=[jax.ShapeDtypeStruct((micro, row, heads * DV), BF16)] * pieces
        + [
            jax.ShapeDtypeStruct((micro, heads, length, length), F32),
            jax.ShapeDtypeStruct((micro, heads, length, DV), F32),
        ],
        compiler_params=pltpu.CompilerParams(vmem_limit_bytes=VMEM_LIMIT),
        name="mixer_forward",
    )(place, projected, taps, taps, taps, rates, gain)


def mixer_backward(place, projected, taps, rates, gain, inverse, update, grads, together):
    pieces, micro, row, _ = projected.shape
    heads, length = rates.shape[1], rates.shape[3]
    slots, proj, kernel, rate_spec, gain_spec, square = mixer_specs(
        pieces, micro, row, heads, length, together
    )
    small_width = 2 * DK + DV
    return pl.pallas_call(
        backward_kernel,
        grid_spec=pltpu.PrefetchScalarGridSpec(
            num_scalar_prefetch=1,
            grid=(heads // together,),
            in_specs=[proj]
            + kernel
            + [rate_spec, gain_spec, square(length), square(DV)]
            + [slots(DV)] * pieces,
            out_specs=[
                proj,
                pl.BlockSpec(
                    (micro, together, SMALL_ROWS, small_width), lambda h, place: (0, h, 0, 0)
                ),
            ],
            scratch_shapes=[
                pltpu.VMEM((micro, together, pieces, row, DV), BF16),
                pltpu.VMEM((micro, together, pieces, row, HEAD_WIDTH), F32),
            ],
        ),
        out_shape=[
            jax.ShapeDtypeStruct((pieces, micro, row, heads * HEAD_WIDTH), BF16),
            jax.ShapeDtypeStruct((micro, heads, SMALL_ROWS, small_width), F32),
        ],
        compiler_params=pltpu.CompilerParams(vmem_limit_bytes=VMEM_LIMIT),
        name="mixer_backward",
    )(place, projected, taps, taps, taps, rates, gain, inverse, update, *grads)


def pick_kernel(place_ref, q_ref, k_ref, v_ref, g_ref, out_ref):
    at = 0
    for ref in (q_ref, k_ref, v_ref, g_ref):
        out_ref[:, at : at + ref.shape[1]] = ref[...]
        at += ref.shape[1]


def pick_heads(place, w_in, heads):
    depth = w_in.shape[0]

    def one(width, first):
        at = first // width
        return pl.BlockSpec((depth, width), lambda h, place: (0, at + place[0] * heads + h))

    return pl.pallas_call(
        pick_kernel,
        grid_spec=pltpu.PrefetchScalarGridSpec(
            num_scalar_prefetch=1,
            grid=(heads,),
            in_specs=[one(DK, 0), one(DK, KD), one(DV, 2 * KD), one(DV, CONVW)],
            out_specs=pl.BlockSpec((depth, HEAD_WIDTH), lambda h, place: (0, h)),
        ),
        out_shape=jax.ShapeDtypeStruct((depth, heads * HEAD_WIDTH), w_in.dtype),
        compiler_params=pltpu.CompilerParams(vmem_limit_bytes=VMEM_LIMIT),
        name="pick_heads",
    )(place, w_in, w_in, w_in, w_in)


def project_kernel(parts, pieces, place_ref, gain_ref, *refs):
    piece_refs, weight_refs = refs[:pieces], refs[pieces : pieces + parts]
    normed_ref, out_ref = refs[pieces + parts :]
    rows = piece_refs[0].shape[0]

    @pl.when(pl.program_id(0) == 0)
    def _():
        for at, ref in enumerate(piece_refs):
            values = ref[...].astype(F32)
            scale = lax.rsqrt(jnp.mean(values * values, -1, keepdims=True) + EPS)
            normed_ref[at * rows : (at + 1) * rows] = (values * scale * gain_ref[...]).astype(BF16)

    total = None
    for step, ref in enumerate(weight_refs):
        depth = ref.shape[0]
        at = pl.multiple_of(jnp.bitwise_xor(place_ref[0], step) * depth, 128)
        term = jnp.dot(normed_ref[:, pl.ds(at, depth)], ref[...], preferred_element_type=F32)
        total = term if total is None else total + term
    out_ref[...] = total


def project(shard_place, gain, piece_list, weights):
    rows, width = piece_list[0].shape
    columns = weights[0].shape[1]
    tile = HEAD_WIDTH
    pieces, parts = len(piece_list), len(weights)
    whole = pl.BlockSpec((rows, width), lambda j, place: (0, 0))
    return pl.pallas_call(
        functools.partial(project_kernel, parts, pieces),
        grid_spec=pltpu.PrefetchScalarGridSpec(
            num_scalar_prefetch=1,
            grid=(columns // tile,),
            in_specs=[pl.BlockSpec((1, width), lambda j, place: (0, 0))]
            + [whole] * pieces
            + [pl.BlockSpec((weights[0].shape[0], tile), lambda j, place: (0, j))] * parts,
            out_specs=[
                pl.BlockSpec((pieces * rows, width), lambda j, place: (0, 0)),
                pl.BlockSpec((pieces * rows, tile), lambda j, place: (0, j)),
            ],
        ),
        out_shape=[
            jax.ShapeDtypeStruct((pieces * rows, width), BF16),
            jax.ShapeDtypeStruct((pieces * rows, columns), F32),
        ],
        compiler_params=pltpu.CompilerParams(vmem_limit_bytes=VMEM_LIMIT),
        name="project",
    )(shard_place, gain, *piece_list, *weights)


def head_rows(places_ref, step, rows, group):
    width = min(rows, group)
    found = []
    for at in range(rows // width):
        first = jnp.bitwise_xor(places_ref[1], step) * rows + at * width
        whose = jnp.bitwise_xor(first // group, places_ref[0])
        found.append((whose, pl.multiple_of(first % group, 128) if width < group else 0, width))
    return found


def merge_kernel(parts, pieces, places_ref, gain_ref, tokens_ref, *refs):
    mixed_refs, weight_refs = refs[:pieces], refs[pieces : pieces + parts]
    middle_ref, normed_ref, *left_refs, gathered = refs[pieces + parts :]
    step_id = pl.program_id(0)
    group = mixed_refs[0].shape[1]

    @pl.when(step_id == 0)
    def _():
        for at, ref in enumerate(mixed_refs):
            gathered[at] = ref[...]
        height = left_refs[0].shape[1] // parts
        for at, ref in enumerate(left_refs):
            for part in range(parts):
                first = (part * pieces + jnp.bitwise_xor(places_ref[0], at)) * height
                whose = jnp.bitwise_xor(first // group, places_ref[0])
                ref[:, part * height : (part + 1) * height] = gathered[
                    whose, :, pl.ds(pl.multiple_of(first % group, 128), height)
                ]

    tile = weight_refs[0].shape[1]
    total = tokens_ref[...].astype(F32)
    for step, ref in enumerate(weight_refs):
        rows = ref.shape[0]
        for at, (whose, first, width) in enumerate(head_rows(places_ref, step, rows, group)):
            total = total + jnp.dot(
                gathered[whose, :, pl.ds(first, width)],
                ref[at * width : (at + 1) * width],
                preferred_element_type=F32,
            )
    middle_ref[:, pl.ds(pl.multiple_of(step_id * tile, 128), tile)] = total

    @pl.when(step_id == pl.num_programs(0) - 1)
    def _():
        values = middle_ref[...]
        scale = lax.rsqrt(jnp.mean(values * values, -1, keepdims=True) + EPS)
        normed_ref[...] = (values * scale * gain_ref[...]).astype(BF16)


def merge(places, gain, tokens, mixed, weights):
    rows, width = tokens.shape
    tile = 512
    pieces, parts = len(mixed), len(weights)
    group = mixed[0].shape[1]
    whole = pl.BlockSpec((rows, width), lambda j, place: (0, 0))
    return pl.pallas_call(
        functools.partial(merge_kernel, parts, pieces),
        grid_spec=pltpu.PrefetchScalarGridSpec(
            num_scalar_prefetch=1,
            grid=(width // tile,),
            in_specs=[
                pl.BlockSpec((1, width), lambda j, place: (0, 0)),
                pl.BlockSpec((rows, tile), lambda j, place: (0, j)),
            ]
            + [pl.BlockSpec((rows, group), lambda j, place: (0, 0))] * pieces
            + [pl.BlockSpec((weights[0].shape[0], tile), lambda j, place: (0, j))] * parts,
            out_specs=[whole, whole]
            + [pl.BlockSpec((rows, group), lambda j, place: (0, 0))] * pieces,
            scratch_shapes=[pltpu.VMEM((pieces, rows, group), BF16)],
        ),
        out_shape=[
            jax.ShapeDtypeStruct((rows, width), F32),
            jax.ShapeDtypeStruct((rows, width), BF16),
        ]
        + [jax.ShapeDtypeStruct((rows, group), BF16)] * pieces,
        compiler_params=pltpu.CompilerParams(vmem_limit_bytes=VMEM_LIMIT),
        name="merge_heads",
    )(places, gain, tokens, *mixed, *weights)


def feed_kernel(parts, places_ref, *refs):
    normed_refs, grad_ref = refs[:parts], refs[parts]
    gate_refs, wide_refs = refs[parts + 1 : 2 * parts + 1], refs[2 * parts + 1 : 3 * parts + 1]
    outs, hidden_ref = refs[3 * parts + 1 : 4 * parts + 1], refs[4 * parts + 1]
    normed_all, grad_all = refs[4 * parts + 2 :]
    step_id = pl.program_id(0)
    rows, depth = normed_refs[0].shape[0], gate_refs[0].shape[0]

    @pl.when(step_id == 0)
    def _():
        for at in range(parts):
            where = slice(at * rows, (at + 1) * rows)
            for step in range(parts):
                first = pl.multiple_of(jnp.bitwise_xor(places_ref[1], step) * depth, 128)
                normed_all[step, where] = normed_refs[at][:, pl.ds(first, depth)]
        grad_all[...] = jnp.zeros_like(grad_all)

    gate, wide = None, None
    for step in range(parts):
        left = normed_all[step]
        one = jnp.dot(left, gate_refs[step][...], preferred_element_type=F32)
        two = jnp.dot(left, wide_refs[step][...], preferred_element_type=F32)
        gate, wide = (one, two) if gate is None else (gate + one, wide + two)
    hidden_grad = grad_ref[...]
    slope = jax.nn.sigmoid(gate)
    hidden_ref[...] = (gate * slope * wide).astype(BF16)
    gate_grad = (hidden_grad * wide * (slope * (1.0 + gate * (1.0 - slope)))).astype(BF16)
    wide_grad = (hidden_grad * gate * slope).astype(BF16)
    for step in range(parts):
        grad_all[step] += mm(gate_grad, gate_refs[step][...], ROWS_ROWS) + mm(
            wide_grad, wide_refs[step][...], ROWS_ROWS
        )

    @pl.when(step_id == pl.num_programs(0) - 1)
    def _():
        for at in range(parts):
            where = slice(at * rows, (at + 1) * rows)
            for step in range(parts):
                outs[at][step ^ at] = grad_all[step, where]


def feed(places, normed, hidden_grad, weights):
    rows, width = normed[0].shape
    parts = len(weights)
    depth = weights[0].shape[0]
    shard_columns = hidden_grad.shape[1]
    tile = 256 if shard_columns % 256 == 0 else shard_columns
    if tile == 256:
        sources = [(part, part) for part in weights]
        columns = weights[0].shape[1] // 2
        gate_at = lambda j, place: (0, place[1] * (shard_columns // tile) + j)
        wide_at = lambda j, place: (
            0,
            columns // tile + place[1] * (shard_columns // tile) + j,
        )
    else:
        shard = lax.axis_index("shard")
        sources = [
            (
                part_of(part[:, : part.shape[1] // 2], shard, parts, 1),
                part_of(part[:, part.shape[1] // 2 :], shard, parts, 1),
            )
            for part in weights
        ]
        gate_at = wide_at = lambda j, place: (0, j)
    whole = pl.BlockSpec((rows, width), lambda j, place: (0, 0))
    narrow = pl.BlockSpec((parts * rows, tile), lambda j, place: (0, j))
    return pl.pallas_call(
        functools.partial(feed_kernel, parts),
        grid_spec=pltpu.PrefetchScalarGridSpec(
            num_scalar_prefetch=1,
            grid=(shard_columns // tile,),
            in_specs=[whole] * parts
            + [narrow]
            + [pl.BlockSpec((depth, tile), gate_at)] * parts
            + [pl.BlockSpec((depth, tile), wide_at)] * parts,
            out_specs=[pl.BlockSpec((parts, rows, depth), lambda j, place: (0, 0, 0))] * parts
            + [narrow],
            scratch_shapes=[
                pltpu.VMEM((parts, parts * rows, depth), BF16),
                pltpu.VMEM((parts, parts * rows, depth), F32),
            ],
        ),
        out_shape=[jax.ShapeDtypeStruct((parts, rows, depth), F32)] * parts
        + [jax.ShapeDtypeStruct((parts * rows, shard_columns), BF16)],
        compiler_params=pltpu.CompilerParams(vmem_limit_bytes=VMEM_LIMIT),
        name="feed_forward",
    )(
        places,
        *normed,
        hidden_grad,
        *[source[0] for source in sources],
        *[source[1] for source in sources],
    )


def unmerge_kernel(parts, pieces, places_ref, gain_ref, middle_ref, up_ref, *refs):
    grad_refs, weight_refs = refs[:parts], refs[parts : 2 * parts]
    grad_out, sent_out, gain_out = refs[2 * parts : 2 * parts + 3]
    piece_outs = refs[2 * parts + 3 : 2 * parts + 3 + pieces]
    gathered = refs[-1]
    step_id = pl.program_id(0)
    depth = grad_refs[0].shape[2]

    @pl.when(step_id == 0)
    def _():
        for step in range(parts):
            first = pl.multiple_of(jnp.bitwise_xor(places_ref[1], step) * depth, 128)
            total = grad_refs[0][step]
            for ref in grad_refs[1:]:
                total = total + ref[step]
            grad_out[:, pl.ds(first, depth)] = total
        values, grad, gain = middle_ref[...], grad_out[...], gain_ref[...]
        scale = lax.rsqrt(jnp.mean(values * values, -1, keepdims=True) + EPS)
        unit_rows = values * scale
        weighted = grad * gain
        inner = jnp.mean(weighted * unit_rows, -1, keepdims=True)
        gain_out[...] = jnp.sum(grad * unit_rows, 0, keepdims=True)
        total = scale * (weighted - unit_rows * inner) + up_ref[...].astype(F32)
        grad_out[...] = total
        sent_out[...] = total.astype(BF16)

    count = pl.num_programs(0)
    group = gathered.shape[2]
    for step, ref in enumerate(weight_refs):
        width = ref.shape[0]
        first = jnp.bitwise_xor(places_ref[1], step) * (width * count) + step_id * width
        whose = jnp.bitwise_xor(first // group, places_ref[0])
        at = pl.multiple_of(first % group, 128) if width < group else 0
        gathered[whose, :, pl.ds(at, width)] = mm(sent_out[...], ref[...], ROWS_ROWS).astype(BF16)

    @pl.when(step_id == count - 1)
    def _():
        for at, ref in enumerate(piece_outs):
            ref[...] = gathered[at]


def unmerge(places, gain, middle, upstream, grads, weights, pieces):
    rows, width = middle.shape
    parts = len(weights)
    depth = grads[0].shape[2]
    group = VD // pieces
    tile = min(weights[0].shape[0], group)
    whole = pl.BlockSpec((rows, width), lambda j, place: (0, 0))
    one_row = pl.BlockSpec((1, width), lambda j, place: (0, 0))
    return pl.pallas_call(
        functools.partial(unmerge_kernel, parts, pieces),
        grid_spec=pltpu.PrefetchScalarGridSpec(
            num_scalar_prefetch=1,
            grid=(weights[0].shape[0] // tile,),
            in_specs=[one_row, whole, whole]
            + [pl.BlockSpec((parts, rows, depth), lambda j, place: (0, 0, 0))] * parts
            + [pl.BlockSpec((tile, width), lambda j, place: (j, 0))] * parts,
            out_specs=[whole, whole, one_row]
            + [pl.BlockSpec((rows, group), lambda j, place: (0, 0))] * pieces,
            scratch_shapes=[pltpu.VMEM((pieces, rows, group), BF16)],
        ),
        out_shape=[
            jax.ShapeDtypeStruct((rows, width), F32),
            jax.ShapeDtypeStruct((rows, width), BF16),
            jax.ShapeDtypeStruct((1, width), F32),
        ]
        + [jax.ShapeDtypeStruct((rows, group), BF16)] * pieces,
        compiler_params=pltpu.CompilerParams(vmem_limit_bytes=VMEM_LIMIT),
        name="split_heads",
    )(places, gain, middle, upstream, *grads, *weights)


def outer_kernel(parts, places_ref, *refs):
    left_refs, right_refs, out_refs = refs[:parts], refs[parts : 2 * parts], refs[2 * parts :]
    total = None
    for left, right in zip(left_refs, right_refs):
        term = mm(left[...], right[...], COLS_COLS)
        total = term if total is None else total + term
    (out_ref,) = out_refs
    chunks, several, height, _ = out_ref.shape
    for one in range(several):
        for at in range(chunks):
            first = (one * chunks + at) * height
            out_ref[at, one] = total[first : first + height].astype(out_ref.dtype)


def outer_products(places, lefts, own_right, rights, owners, chunks):
    rows, width = lefts[0].shape
    parts = len(lefts)
    columns = own_right.shape[1] // parts
    own = width // owners
    tile = max(own, 256)
    fixed = pl.BlockSpec((rows, columns), lambda j, place: (0, 0))
    return pl.pallas_call(
        functools.partial(outer_kernel, parts),
        grid_spec=pltpu.PrefetchScalarGridSpec(
            num_scalar_prefetch=1,
            grid=(width // tile,),
            in_specs=[pl.BlockSpec((rows, tile), lambda j, place: (0, j))] * parts
            + [pl.BlockSpec((rows, columns), lambda j, place: (0, place[1]))]
            + [fixed] * (parts - 1),
            out_specs=pl.BlockSpec(
                (chunks, tile // own, own // chunks, columns), lambda j, place: (0, j, 0, 0)
            ),
        ),
        out_shape=jax.ShapeDtypeStruct((chunks, owners, own // chunks, columns), BF16),
        compiler_params=pltpu.CompilerParams(vmem_limit_bytes=VMEM_LIMIT),
        name="outer_products",
    )(places, *lefts, own_right, *rights)


def rows_kernel(pieces, places_ref, *refs):
    left_refs, right_refs, out_ref, left, right = (
        refs[:pieces], refs[pieces : 2 * pieces], refs[2 * pieces], refs[-2], refs[-1],
    )
    rows = left_refs[0].shape[0]

    @pl.when(pl.program_id(0) == 0)
    def _():
        for at, ref in enumerate(left_refs):
            left[at * rows : (at + 1) * rows] = ref[...]

    for at, ref in enumerate(right_refs):
        right[at * rows : (at + 1) * rows] = ref[...]
    parts, height, _ = out_ref.shape
    for step in range(parts):
        first = pl.multiple_of(jnp.bitwise_xor(places_ref[1], step) * height, 128)
        out_ref[step] = mm(left[:, pl.ds(first, height)], right[...], COLS_COLS).astype(
            out_ref.dtype
        )


def own_rows(places, lefts, rights, parts):
    pieces = len(lefts)
    rows, columns = lefts[0].shape
    height = columns // parts
    width = rights[0].shape[1]
    tile = 512
    return pl.pallas_call(
        functools.partial(rows_kernel, pieces),
        grid_spec=pltpu.PrefetchScalarGridSpec(
            num_scalar_prefetch=1,
            grid=(width // tile,),
            in_specs=[pl.BlockSpec((rows, columns), lambda j, place: (0, 0))] * pieces
            + [pl.BlockSpec((rows, tile), lambda j, place: (0, j))] * pieces,
            out_specs=pl.BlockSpec((parts, height, tile), lambda j, place: (0, 0, j)),
            scratch_shapes=[
                pltpu.VMEM((pieces * rows, columns), BF16),
                pltpu.VMEM((pieces * rows, tile), BF16),
            ],
        ),
        out_shape=jax.ShapeDtypeStruct((parts, height, width), BF16),
        compiler_params=pltpu.CompilerParams(vmem_limit_bytes=VMEM_LIMIT),
        name="own_rows",
    )(places, *lefts, *rights)


def again_kernel(parts, places_ref, normed_ref, up_ref, *refs):
    gate_refs, wide_refs, down_ref = refs[:parts], refs[parts : 2 * parts], refs[2 * parts]
    hidden_ref, gate_out, wide_out = refs[-3:]
    depth = gate_refs[0].shape[0]
    gate, wide = None, None
    for step in range(parts):
        first = pl.multiple_of(jnp.bitwise_xor(places_ref[1], step) * depth, 128)
        left = normed_ref[:, pl.ds(first, depth)]
        one, two = mm(left, gate_refs[step][...]), mm(left, wide_refs[step][...])
        gate, wide = (one, two) if gate is None else (gate + one, wide + two)
    hidden_grad = mm(up_ref[...], down_ref[...], ROWS_ROWS)
    slope = jax.nn.sigmoid(gate)
    hidden_ref[...] = (gate * slope * wide).astype(BF16)
    gate_out[...] = (hidden_grad * wide * (slope * (1.0 + gate * (1.0 - slope)))).astype(BF16)
    wide_out[...] = (hidden_grad * gate * slope).astype(BF16)


def feed_again(places, normed, upstream, gates, wides, down, step, before=()):
    count, width = normed.shape
    parts = len(gates)
    depth, columns = gates[0].shape
    tile = 256
    tiles = count // tile
    there = lambda j, place: (jnp.bitwise_xor(place[1], step) * tiles + j, 0)
    here = lambda j, place: (j, 0)
    fixed = pl.BlockSpec((depth, columns), lambda j, place: (0, 0))
    carried = 1 + 2 + 2 * parts + 1
    return pl.pallas_call(
        functools.partial(again_kernel, parts),
        grid_spec=pltpu.PrefetchScalarGridSpec(
            num_scalar_prefetch=1,
            grid=(tiles,),
            in_specs=[pl.BlockSpec((tile, width), here), pl.BlockSpec((tile, width), there)]
            + [fixed] * (2 * parts)
            + [pl.BlockSpec((columns, width), lambda j, place: (0, 0))]
            + [pl.BlockSpec(memory_space=pl.ANY)] * len(before),
            out_specs=[pl.BlockSpec((tile, columns), there)]
            + [pl.BlockSpec((tile, columns), here)] * 2,
        ),
        out_shape=[
            jax.ShapeDtypeStruct((upstream.shape[0], columns), BF16),
            jax.ShapeDtypeStruct((count, columns), BF16),
            jax.ShapeDtypeStruct((count, columns), BF16),
        ],
        input_output_aliases={carried + at: at for at in range(len(before))},
        compiler_params=pltpu.CompilerParams(vmem_limit_bytes=VMEM_LIMIT),
        name="feed_again",
    )(places, normed, upstream, *gates, *wides, down, *before)


def place_in_kernel(columns_of, head_of, in_ref, out_ref, held, sems):
    step_id = pl.program_id(0)
    slot = lax.rem(step_id, 2)

    def copies(which, where):
        found = []
        for number, (low, width, first) in enumerate(columns_of):
            at = pl.multiple_of(first + head_of(which) * width, 128)
            found.append(
                pltpu.make_async_copy(
                    held.at[where, :, pl.ds(low, width)],
                    out_ref.at[:, pl.ds(at, width)],
                    sems.at[where, number],
                )
            )
        return found

    @pl.when(step_id >= 2)
    def _():
        for copy in copies(step_id - 2, slot):
            copy.wait()

    held[slot] = in_ref[:, 0].astype(F32).reshape(held.shape[1:])
    for copy in copies(step_id, slot):
        copy.start()

    @pl.when(step_id == pl.num_programs(0) - 1)
    def _():
        for copy in copies(step_id - 1, 1 - slot) + copies(step_id, slot):
            copy.wait()


def place_in(value, seqs):
    blocks, sources, rows, columns = value.shape
    heads = HEADS // seqs
    per_source = columns // HEAD_WIDTH
    columns_of = [(0, DK, 0), (DK, DK, KD), (2 * DK, DV, 2 * KD), (2 * DK + DV, DV, CONVW)]

    def head_of(step):
        source = step // per_source
        return source % seqs * heads + source // seqs * per_source + step % per_source

    return pl.pallas_call(
        functools.partial(place_in_kernel, columns_of, head_of),
        grid=(sources * per_source,),
        in_specs=[
            pl.BlockSpec(
                (blocks, 1, rows, HEAD_WIDTH), lambda h: (0, h // per_source, 0, h % per_source)
            )
        ],
        out_specs=pl.BlockSpec(memory_space=pl.ANY),
        out_shape=jax.ShapeDtypeStruct((blocks * rows, PROJW), F32),
        scratch_shapes=[
            pltpu.VMEM((2, blocks * rows, HEAD_WIDTH), F32),
            pltpu.SemaphoreType.DMA((2, len(columns_of))),
        ],
        compiler_params=pltpu.CompilerParams(vmem_limit_bytes=VMEM_LIMIT),
        name="place_w_in",
    )(value)


def place_gu_kernel(half, gate_ref, wide_ref, out_ref):
    def put(ref):
        width = ref.shape[2]
        for at in range(ref.shape[0]):
            out_ref[:, at * width : (at + 1) * width] = ref[at].astype(F32)

    @pl.when(pl.program_id(0) < half)
    def _():
        put(gate_ref)

    @pl.when(pl.program_id(0) >= half)
    def _():
        put(wide_ref)


def place_gu(gate, wide):
    sources, rows, width = gate.shape
    together = 1
    while together * width % 128:
        together *= 2
    half = sources // together
    return pl.pallas_call(
        functools.partial(place_gu_kernel, half),
        grid=(2 * half,),
        in_specs=[
            pl.BlockSpec((together, rows, width), lambda j: (jnp.minimum(j, half - 1), 0, 0)),
            pl.BlockSpec((together, rows, width), lambda j: (jnp.maximum(j - half, 0), 0, 0)),
        ],
        out_specs=pl.BlockSpec((rows, together * width), lambda j: (0, j)),
        out_shape=jax.ShapeDtypeStruct((rows, 2 * sources * width), F32),
        compiler_params=pltpu.CompilerParams(vmem_limit_bytes=VMEM_LIMIT),
        name="place_w_gu",
    )(gate, wide)


def line_first(value):
    return lax.ppermute(value, "replica", [(0, 1), (3, 2)])


def line_second(value):
    return lax.ppermute(value, "replica", [(1, 2), (2, 1)])


def line_third(value):
    return lax.ppermute(value, "replica", [(1, 0), (2, 3)])


def added(left, right):
    return (left.astype(F32) + right.astype(F32)).astype(BF16)


def pinned(*values):
    return lax.optimization_barrier(values)


def line_sum(value):
    value = added(value, line_first(value))
    value = added(value, line_second(value))
    return settled_pair((value, line_third(value)))


def settled_pair(pair):
    place = lax.axis_index("replica")
    return jnp.where((place == 1) | (place == 2), pair[0], pair[1]).astype(F32)


def swapped(value, axis, step):
    count = lax.axis_size(axis)
    return lax.ppermute(value, axis, [(source, source ^ step) for source in range(count)])


def around(value, axis):
    return [value] + [swapped(value, axis, step) for step in range(1, lax.axis_size(axis))]


def settled(parts, index):
    stacked = jnp.stack(parts)
    return [
        lax.dynamic_index_in_dim(stacked, jnp.bitwise_xor(index, at), 0, keepdims=False)
        for at in range(len(parts))
    ]


def part_of(value, index, count, axis):
    width = value.shape[axis] // count
    return lax.dynamic_slice_in_dim(value, index * width, width, axis)


def dot(left, right):
    return jnp.dot(left, right, preferred_element_type=F32)


def dot_rows(left, right):
    return lax.dot_general(left, right, (((1,), (1,)), ((), ())), preferred_element_type=F32)


def dot_cols(left, right):
    return lax.dot_general(left, right, (((0,), (0,)), ((), ())), preferred_element_type=F32)


def rms_parts(values):
    return lax.rsqrt(jnp.mean(values * values, -1, keepdims=True) + EPS)


def rms_back(values, scale, gain, grad):
    weighted = grad * gain
    unit_rows = values * scale
    inner = jnp.mean(weighted * unit_rows, -1, keepdims=True)
    return scale * (weighted - unit_rows * inner), jnp.sum(grad * unit_rows, 0)


def body(
    tokens,
    cotangent,
    lengths,
    norm_gains,
    w_in,
    w_ab,
    conv_weight,
    gate_params,
    onorm_gain,
    w_o,
    w_gu,
    w_down,
):
    shards, seqs, replicas = (lax.axis_size(name) for name in EVERY)
    shard, seq = lax.axis_index("shard"), lax.axis_index("seq")
    owners = shards * seqs
    owner = shard * seqs + seq
    micro, row = tokens.shape[0], tokens.shape[1]
    flat = micro * row
    length = row * seqs
    heads = HEADS // seqs
    depth = D // shards
    seq_place = jnp.reshape(seq, (1,)).astype(jnp.int32)
    shard_place = jnp.reshape(shard, (1,)).astype(jnp.int32)
    places = jnp.stack([seq, shard]).astype(jnp.int32)

    def blocks(value, count, axis=1):
        return [part_of(value, jnp.bitwise_xor(shard, step), count, axis) for step in range(count)]

    flat_tokens = tokens.reshape(flat, D)
    in_own = pick_heads(seq_place, w_in, heads)
    sent_tokens, in_own = pinned(flat_tokens, in_own)
    pieces = around(sent_tokens, "seq")
    gain_parts = around(norm_gains, "shard")
    in_parts = around(in_own, "shard")
    taps_parts = around(conv_weight, "shard")
    ab_parts = around(w_ab, "shard")
    gains = jnp.concatenate(settled(gain_parts, shard), 1).astype(F32)
    gain_first, gain_second = gains[:1], gains[1:]
    taps = jnp.concatenate(settled(taps_parts, shard), 1)
    upstream = cotangent.reshape(flat, D)
    up_parts = around(upstream, "shard")
    hidden_grad = dot_rows(jnp.concatenate(up_parts, 0), w_down)
    own_out, own_gu, late_up, hidden_grad, *arrived = pinned(
        w_o, w_gu, upstream, hidden_grad, *pieces, *in_parts
    )
    pieces, in_parts = arrived[:seqs], arrived[seqs:]
    all_up = lax.all_gather(late_up, EVERY, axis=0, tiled=True)
    out_parts = around(own_out, "shard")
    gu_parts = around(own_gu, "shard")

    normed, projected = project(shard_place, gain_first, pieces, in_parts)
    rate_in = sum(dot(left, right) for left, right in zip(blocks(normed, shards), ab_parts))
    rate_in = part_of(rate_in.reshape(seqs, micro, row, 2, HEADS), seq, seqs, 4)
    rate_in = jnp.stack(settled(list(rate_in), seq))
    rate_in = jnp.transpose(rate_in, (3, 1, 4, 0, 2)).reshape(2, micro, heads, length)
    position = jnp.arange(length, dtype=jnp.int32)
    valid = (position[None, :] < lengths[:, None]).astype(F32)[:, None, :]
    own_params = part_of(gate_params, seq, seqs, 1)[:, None, :, None]
    rate_shifted = rate_in[0] + own_params[1]
    decays = -jnp.exp(own_params[0]) * jax.nn.softplus(rate_shifted) * valid
    written = jax.nn.sigmoid(rate_in[1])
    rates = jnp.stack([jnp.maximum(decays, LOWEST_DECAY), written * valid], 2)
    rates = jnp.pad(rates, ((0, 0), (0, 0), (0, SMALL_ROWS - 2), (0, 0)))
    gain_row = onorm_gain.reshape(1, DV)
    projected = projected.reshape(seqs, micro, row, -1)
    *gated, inverse, update = mixer_forward(seq_place, projected, taps, rates, gain_row, 2)
    gated = [item.reshape(flat, heads * DV) for item in gated]

    mixed_parts = [gated[0]] + [swapped(gated[step], "seq", step) for step in range(1, seqs)]
    arrived = pinned(*mixed_parts, *gu_parts)
    mixed_parts, gu_parts = list(arrived[:seqs]), list(arrived[seqs:])

    def over_seq(value):
        value = jnp.broadcast_to(value[None], (seqs,) + value.shape)
        return lax.all_to_all(value, "seq", split_axis=0, concat_axis=0)

    middle, renormed, *mixed_left = merge(
        places, gain_second, flat_tokens, mixed_parts, out_parts
    )
    line_renormed = lax.all_gather(renormed, "replica", axis=0, tiled=True)

    mixed_left = [
        swapped(item, "seq", step) if step else item for step, item in enumerate(mixed_left)
    ]
    fed = feed(places, around(renormed, "shard"), hidden_grad, gu_parts)
    fed = pinned(*fed, *mixed_left)
    fed, mixed_left = fed[: shards + 1], fed[shards + 1 :]
    grads_back = [fed[0]] + [swapped(fed[step], "shard", step) for step in range(1, shards)]
    middle_grad, mixed_grad, gain2_grad, *gated_grad = unmerge(
        places, gain_second, middle, upstream, grads_back, out_parts, seqs
    )
    hidden = fed[shards]

    ff_own = FF // owners
    own_down = part_of(w_down, seq, seqs, 0)
    own_gate = [part_of(part, owner, 2 * owners, 1) for part in gu_parts]
    own_wide = [part_of(part, owners + owner, 2 * owners, 1) for part in gu_parts]

    gated_grad = [
        swapped(item, "seq", step) if step else item for step, item in enumerate(gated_grad)
    ]
    all_up, mixed_grad, own_down, *others = pinned(
        all_up, mixed_grad, own_down, *own_gate, *own_wide, *gated_grad
    )
    own_gate, own_wide = others[:shards], others[shards : 2 * shards]
    gated_grad = others[2 * shards :]
    gated_grad = [item.reshape(micro, row, heads * DV) for item in gated_grad]
    mid_pieces = around(mixed_grad, "seq")
    proj_grad, small_grad = mixer_backward(
        seq_place, projected, taps, rates, gain_row, inverse, update, gated_grad, 1
    )
    proj_grad, *mid_pieces = pinned(proj_grad, *mid_pieces)
    rows_all = seqs * flat
    proj_grad = proj_grad.reshape(rows_all, -1)
    pair_proj = [
        swapped(part_of(proj_grad, jnp.bitwise_xor(shard, step), shards, 1), "shard", step)
        for step in range(1, shards)
    ]

    pair_normed = around(normed, "shard")
    grad_in = outer_products(places, pair_normed, proj_grad, pair_proj, owners, replicas)
    width = grad_in.shape[3]
    proj_grad, small_grad, grad_in, line_renormed, *mid_pieces = pinned(
        proj_grad, small_grad, grad_in, line_renormed, *mid_pieces
    )
    grad_in = lax.psum_scatter(grad_in, "replica", scatter_dimension=0, tiled=False)
    own_renormed = over_seq(line_renormed).reshape(-1, D)

    grad_out = own_rows(places, mixed_left, mid_pieces, shards)
    grad_out = functools.reduce(
        added, [grad_out[0]] + [swapped(grad_out[step], "shard", step) for step in range(1, shards)]
    )

    def input_gradient_parts(proj_grad, small_grad):
        decay_grad = small_grad[:, :, 5, :length]
        write_grad = small_grad[:, :, 6, :length]
        shifted_grad = decay_grad * -jnp.exp(own_params[0]) * jax.nn.sigmoid(rate_shifted) * valid
        params_grad = jnp.stack(
            [jnp.sum(decay_grad * decays, (0, 2)), jnp.sum(shifted_grad, (0, 2))]
        )
        rate_grad = jnp.stack([shifted_grad, write_grad * written * (1.0 - written) * valid])
        rate_grad = jnp.transpose(rate_grad.reshape(2, micro, heads, seqs, row), (3, 1, 4, 0, 2))
        rate_grad = jnp.stack(settled(list(rate_grad), seq))
        rate_grad = rate_grad.reshape(rows_all, 2 * heads)
        grad_ab = lax.dot_general(
            rate_grad, normed.astype(F32), (((0,), (0,)), ((), ())), precision=HIGHEST
        )
        own_ab = [
            part_of(part.reshape(depth, 2, HEADS), seq, seqs, 2).reshape(depth, 2 * heads)
            for part in ab_parts
        ]
        normed_grad = [
            dot_rows(proj_grad, part)
            + lax.dot_general(
                rate_grad, ab.astype(F32), (((1,), (1,)), ((), ())), precision=HIGHEST
            )
            for part, ab in zip(in_parts, own_ab)
        ]
        return (*normed_grad, grad_ab, params_grad)

    def input_gradient(*normed_grad):
        *normed_grad, grad_ab, params_grad = normed_grad
        normed_grad = jnp.concatenate(settled(normed_grad, shard), 1).reshape(seqs, flat, D)
        normed_grad = normed_grad[0] + sum(
            swapped(normed_grad[step].astype(BF16), "seq", step).astype(F32)
            for step in range(1, seqs)
        )
        flat_in = flat_tokens.astype(F32)
        inputs_grad, gain1_grad = rms_back(flat_in, rms_parts(flat_in), gains[0], normed_grad)
        input_grads = (inputs_grad + middle_grad).astype(BF16).reshape(micro, row, D)
        return input_grads, gain1_grad, grad_ab, params_grad

    def to_group(value):
        return lax.all_to_all(value, GROUP, split_axis=0, concat_axis=0, tiled=False)

    def to_owners(value):
        return to_group(value.astype(BF16).reshape(owners, D // owners, ff_own))

    normed_parts = input_gradient_parts(proj_grad, small_grad)
    replica = lax.axis_index("replica")
    grad_out = [
        swapped(part_of(grad_out, jnp.bitwise_xor(replica, step), replicas, 0), "replica", step)
        if step
        else part_of(grad_out, replica, replicas, 0)
        for step in range(replicas)
    ]
    own_renormed, *normed_parts = pinned(own_renormed, *grad_out, *normed_parts)
    grad_out, normed_parts = normed_parts[:replicas], normed_parts[replicas:]
    grad_out = sum(item.astype(F32) for item in grad_out).astype(BF16)
    grad_out = lax.all_gather(grad_out, "replica", axis=0, tiled=True)
    all_renormed = around(own_renormed, "shard")

    def again(at, before=()):
        return feed_again(
            places, all_renormed[at], all_up, own_gate, own_wide, own_down, at, before
        )

    def over_tokens(lefts, rights):
        return sum(dot_cols(left, right) for left, right in zip(lefts, rights))

    parts = [again(0)]
    grad_in, hidden, *parts[0] = pinned(grad_in, hidden, *parts[0])
    grad_in = to_group(grad_in)
    for at in range(1, shards):
        parts.append(again(at, parts[-1][:1]))
    grad_in, own_hidden, *normed_parts = pinned(grad_in, parts[-1][0], *normed_parts)
    grad_in = lax.all_gather(grad_in, "replica", axis=0)
    gate_grad, wide_grad = ([part[which] for part in parts] for which in (1, 2))
    input_grads, gain1_grad, grad_ab, params_grad = input_gradient(*normed_parts)
    gain2_grad = gain2_grad[0]
    grad_gate = over_tokens(all_renormed, gate_grad).astype(BF16)
    grad_gate, own_hidden, input_grads, gain1_grad, grad_ab, params_grad, *wide_grad = pinned(
        grad_gate, own_hidden, input_grads, gain1_grad, grad_ab, params_grad, *wide_grad
    )
    grad_gate = to_owners(grad_gate)
    grad_wide = over_tokens(all_renormed, wide_grad).astype(BF16)
    taps_grad = jnp.sum(small_grad[:, :, :KERNEL], 0)
    conv_grad = jnp.concatenate(
        [
            jnp.swapaxes(taps_grad[..., low:high], 0, 1).reshape(KERNEL, -1)
            for low, high in ((0, DK), (DK, 2 * DK), (2 * DK, 2 * DK + DV))
        ],
        1,
    )
    onorm_grad = jnp.sum(small_grad[:, :, 4, :DV], (0, 1))
    loose = jnp.concatenate([onorm_grad, params_grad.reshape(-1)])
    loose = jnp.pad(loose, (0, D - loose.size))
    rows_ab = 2 * heads
    smalls = jnp.concatenate(
        [grad_ab, conv_grad, loose[None], gain1_grad[None], gain2_grad[None]], 0
    )
    step = 1
    while step < shards:
        smalls = smalls + swapped(smalls, "shard", step)
        step *= 2
    grad_down = dot_cols(own_hidden, all_up)
    grad_wide, grad_gate, grad_out = pinned(grad_wide, grad_gate, grad_out)
    grad_wide = to_owners(grad_wide)
    step = 1
    while step < replicas:
        smalls = smalls + swapped(smalls, "replica", step)
        step *= 2
    rows_down = dot(hidden, w_down).reshape(shards, flat, D)
    result = (
        middle
        + rows_down[0]
        + sum(swapped(rows_down[step], "shard", step) for step in range(1, shards))
    )
    results = result.astype(BF16).reshape(micro, row, D)
    grad_out = grad_out.astype(F32)
    every = jnp.stack(settled(around(smalls, "seq"), seq))
    grad_gu = place_gu(grad_gate, grad_wide)
    if width % HEAD_WIDTH == 0:
        grad_in = place_in(grad_in, seqs)
    else:
        grad_in = grad_in.reshape(replicas, shards, seqs, -1, width)
        grad_in = jnp.transpose(grad_in, (0, 3, 2, 1, 4)).reshape(D // owners, HEADS, HEAD_WIDTH)
        cuts = (0, DK, 2 * DK, 2 * DK + DV, HEAD_WIDTH)
        grad_in = jnp.concatenate(
            [
                grad_in[..., low:high].reshape(D // owners, -1)
                for low, high in zip(cuts[:-1], cuts[1:])
            ],
            1,
        ).astype(F32)

    ab_total = jnp.transpose(every[:, :rows_ab].reshape(seqs, 2, heads, D), (3, 1, 0, 2))
    ab_total = ab_total.reshape(D, 2 * HEADS)
    conv_all = every[:, rows_ab : rows_ab + KERNEL]
    conv_total = jnp.concatenate(
        [
            jnp.swapaxes(conv_all[..., low:high], 0, 1).reshape(KERNEL, -1)
            for low, high in (
                (0, heads * DK),
                (heads * DK, 2 * heads * DK),
                (2 * heads * DK, heads * (2 * DK + DV)),
            )
        ],
        1,
    )
    loose_all = every[:, rows_ab + KERNEL]
    onorm_total = jnp.sum(loose_all[:, :DV], 0)
    params_total = loose_all[:, DV : DV + 2 * heads].reshape(seqs, 2, heads)
    params_total = jnp.swapaxes(params_total, 0, 1).reshape(2, HEADS)
    gains_total = jnp.sum(every[:, rows_ab + KERNEL + 1 : rows_ab + KERNEL + 3], 0)
    gains_own = part_of(gains_total, owner, owners, 1)
    ab_own = part_of(ab_total, owner, owners, 0)
    conv_own = part_of(conv_total, owner, owners, 1)
    return (
        results,
        input_grads,
        gains_own,
        grad_in,
        ab_own,
        conv_own,
        params_total,
        onorm_total,
        grad_out,
        grad_gu,
        grad_down,
    )


def solution(mesh):
    in_specs = (
        P(("shard", "replica"), "seq", None),
        P(("shard", "replica"), "seq", None),
        P(("shard", "replica")),
        P(None, "shard"),
        P("shard", None),
        P("shard", None),
        P(None, "shard"),
        P(),
        P(),
        P("shard", None),
        P("shard", None),
        P("shard", None),
    )
    out_specs = (
        P(("shard", "replica"), "seq", None),
        P(("shard", "replica"), "seq", None),
        P(None, ("shard", "seq")),
        P(("shard", "seq"), None),
        P(("shard", "seq"), None),
        P(None, ("shard", "seq")),
        P(),
        P(),
        P(("shard", "seq"), None),
        P(("shard", "seq"), None),
        P(("shard", "seq"), None),
    )
    return jax.shard_map(body, mesh=mesh, in_specs=in_specs, out_specs=out_specs, check_vma=False)
```

```python
import functools

import jax
import jax.numpy as jnp
from jax import lax
from jax.experimental import pallas as pl
from jax.experimental.pallas import tpu as pltpu
from jax.sharding import PartitionSpec as P

D = 2048
HEADS = 16
DK = 128
DV = 256
FF = 5632
KERNEL = 4
KD = 2048
VD = 4096
CONVW = 8192
PROJW = 12288
EPS = 1e-06
HIGHEST = lax.Precision.HIGHEST
LOWEST_DECAY = -104.0
F32 = jnp.float32
BF16 = jnp.bfloat16
EVERY = ("shard", "seq", "replica")
GROUP = ("shard", "seq")


def mm(left, right, dims=((1,), (0,))):
    return lax.dot_general(
        left.astype(BF16), right.astype(BF16), (dims, ((), ())), preferred_element_type=F32
    )


def split(value):
    high = value.astype(BF16)
    return high, (value - high.astype(F32)).astype(BF16)


def mm3s(left, right, dims=((1,), (0,))):
    return (
        mm(left[0], right[0], dims) + mm(left[0], right[1], dims) + mm(left[1], right[0], dims)
    )


def mm3(left, right, dims=((1,), (0,))):
    return mm3s(split(left), split(right), dims)


ROWS_ROWS = ((1,), (1,))
COLS_COLS = ((0,), (0,))


def delayed(value, steps, rows):
    if steps == 0:
        return value
    return jnp.where(rows >= steps, pltpu.roll(value, steps, 0), 0.0)


def advanced(value, steps, rows):
    if steps == 0:
        return value
    length = value.shape[0]
    return jnp.where(rows < length - steps, pltpu.roll(value, length - steps, 0), 0.0)


def convolved(source, taps, rows):
    mixed = taps[KERNEL - 1 : KERNEL] * source
    for offset in range(KERNEL - 1):
        mixed = mixed + taps[offset : offset + 1] * delayed(source, KERNEL - 1 - offset, rows)
    return mixed


def unit(value):
    scale = lax.rsqrt(jnp.sum(value * value, -1, keepdims=True) + EPS)
    return value * scale, scale


def decay_matrices(rates):
    length = rates.shape[1]
    row_ids = lax.broadcasted_iota(jnp.int32, (length, length), 0)
    col_ids = lax.broadcasted_iota(jnp.int32, (length, length), 1)
    decay_row = rates[0:1]
    rate_row = rates[1:2]
    diagonal = row_ids == col_ids
    running = jnp.sum(jnp.where(row_ids >= col_ids, decay_row, 0.0), 1, keepdims=True)
    running_row = jnp.sum(jnp.where(diagonal, running, 0.0), 0, keepdims=True)
    rate = jnp.sum(jnp.where(diagonal, rate_row, 0.0), 1, keepdims=True)
    spread = jnp.minimum(running - running_row, 0.0)
    weight = jnp.where(row_ids >= col_ids, jnp.exp(spread), 0.0)
    return row_ids, col_ids, rate, weight


def lower_inverses(systems, row_ids, col_ids):
    length = row_ids.shape[0]
    eye = (row_ids == col_ids).astype(F32)
    same = jnp.bitwise_xor(row_ids, col_ids)
    inverses = [eye - jnp.where(same < 2, system, 0.0) for system in systems]
    size = 2
    while size < length:
        level = (same >= size) & (same < 2 * size)
        halves = [split(inverse) for inverse in inverses]
        inner = [
            mm3s(split(jnp.where(level, system, 0.0)), half)
            for system, half in zip(systems, halves)
        ]
        inverses = [
            inverse - mm3s(half, split(item))
            for inverse, half, item in zip(inverses, halves, inner)
        ]
        size *= 2
    return inverses


def head_inputs(source, taps):
    rows = lax.broadcasted_iota(jnp.int32, (source.shape[0], 1), 0)
    cuts = (0, DK, 2 * DK, 2 * DK + DV)
    raw = [source[:, low:high].astype(BF16).astype(F32) for low, high in zip(cuts, cuts[1:])]
    mixed = [convolved(item, kernel, rows) for item, kernel in zip(raw, taps)]
    slopes = [jax.nn.sigmoid(item) for item in mixed]
    query_unit, query_scale = unit(mixed[0] * slopes[0])
    key_rows, key_scale = unit(mixed[1] * slopes[1])
    values = mixed[2] * slopes[2]
    queries = query_unit * DK ** (-0.5)
    return raw, rows, mixed, slopes, queries, key_rows, values, query_unit, query_scale, key_scale


def slot_rows(ref, place, slot, low, high):
    pieces = ref.shape[0]
    return jnp.concatenate(
        [ref[jnp.bitwise_xor(place, j), slot, :, low:high] for j in range(pieces)], 0
    )


def taps_of(refs, head):
    return [
        ref[:, head * width : (head + 1) * width].astype(F32)
        for ref, width in zip(refs, (DK, DK, DV))
    ]


def forward_kernel(
    place_ref, proj_ref, taps_q, taps_k, taps_v, rates_ref, gain_ref, *outs
):
    *gated_refs, inverse_ref, update_ref, kept = outs
    place = place_ref[0]
    micro, together = rates_ref.shape[0], rates_ref.shape[1]
    pairs = [(slot, head) for slot in range(micro) for head in range(together)]
    work = []
    for slot, head in pairs:
        source = slot_rows(proj_ref, place, slot, head * HEAD_WIDTH, (head + 1) * HEAD_WIDTH)
        items = head_inputs(source, taps_of((taps_q, taps_k, taps_v), head))
        queries, key_rows, values = items[4:7]
        row_ids, col_ids, rate, weight = decay_matrices(rates_ref[slot, head])
        system = jnp.where(
            row_ids > col_ids, rate * mm3(key_rows, key_rows, ROWS_ROWS) * weight, 0.0
        )
        scores = (mm(queries, key_rows, ROWS_ROWS) * weight).astype(BF16)
        gate = source[:, 2 * DK + DV :]
        work.append((system, scores, rate * values, gate * jax.nn.sigmoid(gate)))
    inverses = lower_inverses([item[0] for item in work], row_ids, col_ids)
    row = proj_ref.shape[2]
    for (slot, head), item, inverse in zip(pairs, work, inverses):
        update = mm3(inverse, item[2])
        outputs = mm(item[1], update)
        scaled = (
            outputs
            * lax.rsqrt(jnp.mean(outputs * outputs, -1, keepdims=True) + EPS)
            * gain_ref[...]
        )
        inverse_ref[slot, head] = inverse
        update_ref[slot, head] = update
        kept[...] = (scaled * item[3]).reshape(kept.shape)
        for step, ref in enumerate(gated_refs):
            ref[slot, :, head * DV : (head + 1) * DV] = kept[jnp.bitwise_xor(place, step)].astype(
                ref.dtype
            )


def unit_back(grad, direction, scale):
    return scale * (grad - direction * jnp.sum(grad * direction, -1, keepdims=True))


def backward_kernel(
    place_ref, proj_ref, taps_q, taps_k, taps_v, rates_ref, gain_ref, inverse_ref, update_ref,
    *refs,
):
    *grad_refs, dproj_ref, small_ref, taken, kept = refs
    place = place_ref[0]
    micro, together = rates_ref.shape[0], rates_ref.shape[1]
    small_ref[...] = jnp.zeros_like(small_ref)
    for slot in range(micro):
        for head in range(together):
            backward_head(
                place, slot, head, proj_ref, (taps_q, taps_k, taps_v), rates_ref, gain_ref,
                inverse_ref, update_ref, grad_refs, dproj_ref, small_ref,
                taken.at[slot, head], kept.at[slot, head],
            )


def backward_head(
    place, slot, head, proj_ref, taps_refs, rates_ref, gain_ref, inverse_ref, update_ref,
    grad_refs, dproj_ref, small_ref, taken, kept,
):
    source = slot_rows(proj_ref, place, slot, head * HEAD_WIDTH, (head + 1) * HEAD_WIDTH)
    taps = taps_of(taps_refs, head)
    raw, rows, mixed, slopes, queries, key_rows, values, query_unit, query_scale, key_scale = (
        head_inputs(source, taps)
    )
    for step, ref in enumerate(grad_refs):
        taken[jnp.bitwise_xor(place, step)] = ref[slot, :, head * DV : (head + 1) * DV]
    upstream = jnp.concatenate([taken[j] for j in range(len(grad_refs))], 0).astype(F32)
    row_ids, col_ids, rate, weight = decay_matrices(rates_ref[slot, head])
    inner = mm3(key_rows, key_rows, ROWS_ROWS)
    strict = row_ids > col_ids
    keyed = jnp.where(strict, inner * weight, 0.0)
    scores = mm(queries, key_rows, ROWS_ROWS) * weight
    inverse = inverse_ref[slot, head]
    update = update_ref[slot, head]
    outputs = mm(scores, update)
    gate = source[:, 2 * DK + DV :]
    gate_slope = jax.nn.sigmoid(gate)
    out_scale = lax.rsqrt(jnp.mean(outputs * outputs, -1, keepdims=True) + EPS)
    out_unit = outputs * out_scale
    gain = gain_ref[...]
    scaled_grad = upstream * (gate * gate_slope)
    gate_grad = upstream * out_unit * gain * (gate_slope * (1.0 + gate * (1.0 - gate_slope)))
    gain_grad = jnp.sum(scaled_grad * out_unit, 0, keepdims=True)
    unit_grad = scaled_grad * gain
    out_grad = out_scale * (
        unit_grad - out_unit * jnp.mean(unit_grad * out_unit, -1, keepdims=True)
    )
    scores_grad = jnp.where(row_ids >= col_ids, mm(out_grad, update, ROWS_ROWS), 0.0)
    update_grad = mm(scores, out_grad, COLS_COLS)
    target_grad = mm3(inverse, update_grad, COLS_COLS)
    system_grad = jnp.where(strict, -mm(target_grad, update, ROWS_ROWS), 0.0)
    value_grad = rate * target_grad
    keyed_grad = system_grad * keyed
    rate_grad = jnp.sum(target_grad * values, 1, keepdims=True) + jnp.sum(
        keyed_grad, 1, keepdims=True
    )
    spread_grad = keyed_grad * rate + scores_grad * scores
    inner_grad = system_grad * weight * rate
    raw_scores_grad = scores_grad * weight
    query_grad = mm(raw_scores_grad, key_rows) * DK ** (-0.5)
    key_grad = (
        mm(raw_scores_grad, queries, COLS_COLS)
        + mm(inner_grad, key_rows)
        + mm(inner_grad, key_rows, COLS_COLS)
    )
    diagonal = row_ids == col_ids
    column_sum = jnp.sum(spread_grad, 0, keepdims=True)
    running_grad = jnp.sum(spread_grad, 1, keepdims=True) - jnp.sum(
        jnp.where(diagonal, column_sum, 0.0), 1, keepdims=True
    )
    decay_grad = jnp.sum(jnp.where(row_ids >= col_ids, running_grad, 0.0), 0, keepdims=True)
    rate_grad_row = jnp.sum(jnp.where(diagonal, rate_grad, 0.0), 0, keepdims=True)
    active_grads = (
        unit_back(query_grad, query_unit, query_scale),
        unit_back(key_grad, key_rows, key_scale),
        value_grad,
    )
    cuts = (0, DK, 2 * DK, 2 * DK + DV, HEAD_WIDTH)
    for low, high, grad_out, plain, before, slope, kernel in zip(
        cuts, cuts[1:], active_grads, raw, mixed, slopes, taps
    ):
        mixed_grad = grad_out * (slope * (1.0 + before * (1.0 - slope)))
        total = kernel[KERNEL - 1 : KERNEL] * mixed_grad
        for offset in range(KERNEL):
            steps = KERNEL - 1 - offset
            if steps:
                total = total + kernel[offset : offset + 1] * advanced(mixed_grad, steps, rows)
            small_ref[slot, head, offset : offset + 1, low:high] = jnp.sum(
                mixed_grad * delayed(plain, steps, rows), 0, keepdims=True
            )
        kept[:, :, low:high] = total.reshape(kept.shape[:2] + (high - low,))
    kept[:, :, cuts[3] : cuts[4]] = gate_grad.reshape(kept.shape[:2] + (DV,))
    for step in range(kept.shape[0]):
        dproj_ref[step, slot, :, head * HEAD_WIDTH : (head + 1) * HEAD_WIDTH] = kept[
            jnp.bitwise_xor(place, step)
        ].astype(dproj_ref.dtype)
    small_ref[slot, head, 4:5, 0:DV] = gain_grad
    length = decay_grad.shape[1]
    small_ref[slot, head, 5:6, 0:length] = decay_grad
    small_ref[slot, head, 6:7, 0:length] = rate_grad_row


VMEM_LIMIT = 56 * 1024 * 1024
HEAD_WIDTH = 2 * DK + 2 * DV
SMALL_ROWS = 8


def mixer_specs(pieces, micro, row, heads, length, together):
    def slots(width):
        return pl.BlockSpec((micro, row, together * width), lambda h, place: (0, 0, h))

    def taps(width, first):
        at = first // (together * width)
        return pl.BlockSpec(
            (KERNEL, together * width),
            lambda h, place: (0, at + place[0] * (heads // together) + h),
        )

    proj = pl.BlockSpec(
        (pieces, micro, row, together * HEAD_WIDTH), lambda h, place: (0, 0, 0, h)
    )
    kernel = [taps(DK, 0), taps(DK, KD), taps(DV, 2 * KD)]
    rates = pl.BlockSpec((micro, together, SMALL_ROWS, length), lambda h, place: (0, h, 0, 0))
    gain = pl.BlockSpec((1, DV), lambda h, place: (0, 0))

    def square(width):
        return pl.BlockSpec((micro, together, length, width), lambda h, place: (0, h, 0, 0))

    return slots, proj, kernel, rates, gain, square


def mixer_forward(place, projected, taps, rates, gain, together):
    pieces, micro, row, _ = projected.shape
    heads, length = rates.shape[1], rates.shape[3]
    slots, proj, kernel, rate_spec, gain_spec, square = mixer_specs(
        pieces, micro, row, heads, length, together
    )
    return pl.pallas_call(
        forward_kernel,
        grid_spec=pltpu.PrefetchScalarGridSpec(
            num_scalar_prefetch=1,
            grid=(heads // together,),
            in_specs=[proj] + kernel + [rate_spec, gain_spec],
            out_specs=[slots(DV)] * pieces + [square(length), square(DV)],
            scratch_shapes=[pltpu.VMEM((pieces, row, DV), F32)],
        ),
        out_shape=[jax.ShapeDtypeStruct((micro, row, heads * DV), BF16)] * pieces
        + [
            jax.ShapeDtypeStruct((micro, heads, length, length), F32),
            jax.ShapeDtypeStruct((micro, heads, length, DV), F32),
        ],
        compiler_params=pltpu.CompilerParams(vmem_limit_bytes=VMEM_LIMIT),
        name="mixer_forward",
    )(place, projected, taps, taps, taps, rates, gain)


def mixer_backward(place, projected, taps, rates, gain, inverse, update, grads, together):
    pieces, micro, row, _ = projected.shape
    heads, length = rates.shape[1], rates.shape[3]
    slots, proj, kernel, rate_spec, gain_spec, square = mixer_specs(
        pieces, micro, row, heads, length, together
    )
    small_width = 2 * DK + DV
    return pl.pallas_call(
        backward_kernel,
        grid_spec=pltpu.PrefetchScalarGridSpec(
            num_scalar_prefetch=1,
            grid=(heads // together,),
            in_specs=[proj]
            + kernel
            + [rate_spec, gain_spec, square(length), square(DV)]
            + [slots(DV)] * pieces,
            out_specs=[
                proj,
                pl.BlockSpec(
                    (micro, together, SMALL_ROWS, small_width), lambda h, place: (0, h, 0, 0)
                ),
            ],
            scratch_shapes=[
                pltpu.VMEM((micro, together, pieces, row, DV), BF16),
                pltpu.VMEM((micro, together, pieces, row, HEAD_WIDTH), F32),
            ],
        ),
        out_shape=[
            jax.ShapeDtypeStruct((pieces, micro, row, heads * HEAD_WIDTH), BF16),
            jax.ShapeDtypeStruct((micro, heads, SMALL_ROWS, small_width), F32),
        ],
        compiler_params=pltpu.CompilerParams(vmem_limit_bytes=VMEM_LIMIT),
        name="mixer_backward",
    )(place, projected, taps, taps, taps, rates, gain, inverse, update, *grads)


def pick_kernel(place_ref, q_ref, k_ref, v_ref, g_ref, out_ref):
    at = 0
    for ref in (q_ref, k_ref, v_ref, g_ref):
        out_ref[:, at : at + ref.shape[1]] = ref[...]
        at += ref.shape[1]


def pick_heads(place, w_in, heads):
    depth = w_in.shape[0]

    def one(width, first):
        at = first // width
        return pl.BlockSpec((depth, width), lambda h, place: (0, at + place[0] * heads + h))

    return pl.pallas_call(
        pick_kernel,
        grid_spec=pltpu.PrefetchScalarGridSpec(
            num_scalar_prefetch=1,
            grid=(heads,),
            in_specs=[one(DK, 0), one(DK, KD), one(DV, 2 * KD), one(DV, CONVW)],
            out_specs=pl.BlockSpec((depth, HEAD_WIDTH), lambda h, place: (0, h)),
        ),
        out_shape=jax.ShapeDtypeStruct((depth, heads * HEAD_WIDTH), w_in.dtype),
        compiler_params=pltpu.CompilerParams(vmem_limit_bytes=VMEM_LIMIT),
        name="pick_heads",
    )(place, w_in, w_in, w_in, w_in)


def project_kernel(parts, pieces, place_ref, gain_ref, *refs):
    piece_refs, weight_refs = refs[:pieces], refs[pieces : pieces + parts]
    normed_ref, out_ref = refs[pieces + parts :]
    rows = piece_refs[0].shape[0]

    @pl.when(pl.program_id(0) == 0)
    def _():
        for at, ref in enumerate(piece_refs):
            values = ref[...].astype(F32)
            scale = lax.rsqrt(jnp.mean(values * values, -1, keepdims=True) + EPS)
            normed_ref[at * rows : (at + 1) * rows] = (values * scale * gain_ref[...]).astype(BF16)

    total = None
    for step, ref in enumerate(weight_refs):
        depth = ref.shape[0]
        at = pl.multiple_of(jnp.bitwise_xor(place_ref[0], step) * depth, 128)
        term = jnp.dot(normed_ref[:, pl.ds(at, depth)], ref[...], preferred_element_type=F32)
        total = term if total is None else total + term
    out_ref[...] = total


def project(shard_place, gain, piece_list, weights):
    rows, width = piece_list[0].shape
    columns = weights[0].shape[1]
    tile = HEAD_WIDTH
    pieces, parts = len(piece_list), len(weights)
    whole = pl.BlockSpec((rows, width), lambda j, place: (0, 0))
    return pl.pallas_call(
        functools.partial(project_kernel, parts, pieces),
        grid_spec=pltpu.PrefetchScalarGridSpec(
            num_scalar_prefetch=1,
            grid=(columns // tile,),
            in_specs=[pl.BlockSpec((1, width), lambda j, place: (0, 0))]
            + [whole] * pieces
            + [pl.BlockSpec((weights[0].shape[0], tile), lambda j, place: (0, j))] * parts,
            out_specs=[
                pl.BlockSpec((pieces * rows, width), lambda j, place: (0, 0)),
                pl.BlockSpec((pieces * rows, tile), lambda j, place: (0, j)),
            ],
        ),
        out_shape=[
            jax.ShapeDtypeStruct((pieces * rows, width), BF16),
            jax.ShapeDtypeStruct((pieces * rows, columns), F32),
        ],
        compiler_params=pltpu.CompilerParams(vmem_limit_bytes=VMEM_LIMIT),
        name="project",
    )(shard_place, gain, *piece_list, *weights)


def head_rows(places_ref, step, rows, group):
    width = min(rows, group)
    found = []
    for at in range(rows // width):
        first = jnp.bitwise_xor(places_ref[1], step) * rows + at * width
        whose = jnp.bitwise_xor(first // group, places_ref[0])
        found.append((whose, pl.multiple_of(first % group, 128) if width < group else 0, width))
    return found


def merge_kernel(parts, pieces, places_ref, gain_ref, tokens_ref, *refs):
    mixed_refs, weight_refs = refs[:pieces], refs[pieces : pieces + parts]
    middle_ref, normed_ref, *left_refs, gathered = refs[pieces + parts :]
    step_id = pl.program_id(0)
    group = mixed_refs[0].shape[1]

    @pl.when(step_id == 0)
    def _():
        for at, ref in enumerate(mixed_refs):
            gathered[at] = ref[...]
        height = left_refs[0].shape[1] // parts
        for at, ref in enumerate(left_refs):
            for part in range(parts):
                first = (part * pieces + jnp.bitwise_xor(places_ref[0], at)) * height
                whose = jnp.bitwise_xor(first // group, places_ref[0])
                ref[:, part * height : (part + 1) * height] = gathered[
                    whose, :, pl.ds(pl.multiple_of(first % group, 128), height)
                ]

    tile = weight_refs[0].shape[1]
    total = tokens_ref[...].astype(F32)
    for step, ref in enumerate(weight_refs):
        rows = ref.shape[0]
        for at, (whose, first, width) in enumerate(head_rows(places_ref, step, rows, group)):
            total = total + jnp.dot(
                gathered[whose, :, pl.ds(first, width)],
                ref[at * width : (at + 1) * width],
                preferred_element_type=F32,
            )
    middle_ref[:, pl.ds(pl.multiple_of(step_id * tile, 128), tile)] = total

    @pl.when(step_id == pl.num_programs(0) - 1)
    def _():
        values = middle_ref[...]
        scale = lax.rsqrt(jnp.mean(values * values, -1, keepdims=True) + EPS)
        normed_ref[...] = (values * scale * gain_ref[...]).astype(BF16)


def merge(places, gain, tokens, mixed, weights):
    rows, width = tokens.shape
    tile = 512
    pieces, parts = len(mixed), len(weights)
    group = mixed[0].shape[1]
    whole = pl.BlockSpec((rows, width), lambda j, place: (0, 0))
    return pl.pallas_call(
        functools.partial(merge_kernel, parts, pieces),
        grid_spec=pltpu.PrefetchScalarGridSpec(
            num_scalar_prefetch=1,
            grid=(width // tile,),
            in_specs=[
                pl.BlockSpec((1, width), lambda j, place: (0, 0)),
                pl.BlockSpec((rows, tile), lambda j, place: (0, j)),
            ]
            + [pl.BlockSpec((rows, group), lambda j, place: (0, 0))] * pieces
            + [pl.BlockSpec((weights[0].shape[0], tile), lambda j, place: (0, j))] * parts,
            out_specs=[whole, whole]
            + [pl.BlockSpec((rows, group), lambda j, place: (0, 0))] * pieces,
            scratch_shapes=[pltpu.VMEM((pieces, rows, group), BF16)],
        ),
        out_shape=[
            jax.ShapeDtypeStruct((rows, width), F32),
            jax.ShapeDtypeStruct((rows, width), BF16),
        ]
        + [jax.ShapeDtypeStruct((rows, group), BF16)] * pieces,
        compiler_params=pltpu.CompilerParams(vmem_limit_bytes=VMEM_LIMIT),
        name="merge_heads",
    )(places, gain, tokens, *mixed, *weights)


def feed_kernel(parts, places_ref, *refs):
    normed_refs, grad_ref = refs[:parts], refs[parts]
    gate_refs, wide_refs = refs[parts + 1 : 2 * parts + 1], refs[2 * parts + 1 : 3 * parts + 1]
    outs, hidden_ref = refs[3 * parts + 1 : 4 * parts + 1], refs[4 * parts + 1]
    normed_all, grad_all = refs[4 * parts + 2 :]
    step_id = pl.program_id(0)
    rows, depth = normed_refs[0].shape[0], gate_refs[0].shape[0]

    @pl.when(step_id == 0)
    def _():
        for at in range(parts):
            where = slice(at * rows, (at + 1) * rows)
            for step in range(parts):
                first = pl.multiple_of(jnp.bitwise_xor(places_ref[1], step) * depth, 128)
                normed_all[step, where] = normed_refs[at][:, pl.ds(first, depth)]
        grad_all[...] = jnp.zeros_like(grad_all)

    gate, wide = None, None
    for step in range(parts):
        left = normed_all[step]
        one = jnp.dot(left, gate_refs[step][...], preferred_element_type=F32)
        two = jnp.dot(left, wide_refs[step][...], preferred_element_type=F32)
        gate, wide = (one, two) if gate is None else (gate + one, wide + two)
    hidden_grad = grad_ref[...]
    slope = jax.nn.sigmoid(gate)
    hidden_ref[...] = (gate * slope * wide).astype(BF16)
    gate_grad = (hidden_grad * wide * (slope * (1.0 + gate * (1.0 - slope)))).astype(BF16)
    wide_grad = (hidden_grad * gate * slope).astype(BF16)
    for step in range(parts):
        grad_all[step] += mm(gate_grad, gate_refs[step][...], ROWS_ROWS) + mm(
            wide_grad, wide_refs[step][...], ROWS_ROWS
        )

    @pl.when(step_id == pl.num_programs(0) - 1)
    def _():
        for at in range(parts):
            where = slice(at * rows, (at + 1) * rows)
            for step in range(parts):
                outs[at][step ^ at] = grad_all[step, where]


def feed(places, normed, hidden_grad, weights):
    rows, width = normed[0].shape
    parts = len(weights)
    depth = weights[0].shape[0]
    shard_columns = hidden_grad.shape[1]
    tile = 256 if shard_columns % 256 == 0 else shard_columns
    if tile == 256:
        sources = [(part, part) for part in weights]
        columns = weights[0].shape[1] // 2
        gate_at = lambda j, place: (0, place[1] * (shard_columns // tile) + j)
        wide_at = lambda j, place: (
            0,
            columns // tile + place[1] * (shard_columns // tile) + j,
        )
    else:
        shard = lax.axis_index("shard")
        sources = [
            (
                part_of(part[:, : part.shape[1] // 2], shard, parts, 1),
                part_of(part[:, part.shape[1] // 2 :], shard, parts, 1),
            )
            for part in weights
        ]
        gate_at = wide_at = lambda j, place: (0, j)
    whole = pl.BlockSpec((rows, width), lambda j, place: (0, 0))
    narrow = pl.BlockSpec((parts * rows, tile), lambda j, place: (0, j))
    return pl.pallas_call(
        functools.partial(feed_kernel, parts),
        grid_spec=pltpu.PrefetchScalarGridSpec(
            num_scalar_prefetch=1,
            grid=(shard_columns // tile,),
            in_specs=[whole] * parts
            + [narrow]
            + [pl.BlockSpec((depth, tile), gate_at)] * parts
            + [pl.BlockSpec((depth, tile), wide_at)] * parts,
            out_specs=[pl.BlockSpec((parts, rows, depth), lambda j, place: (0, 0, 0))] * parts
            + [narrow],
            scratch_shapes=[
                pltpu.VMEM((parts, parts * rows, depth), BF16),
                pltpu.VMEM((parts, parts * rows, depth), F32),
            ],
        ),
        out_shape=[jax.ShapeDtypeStruct((parts, rows, depth), F32)] * parts
        + [jax.ShapeDtypeStruct((parts * rows, shard_columns), BF16)],
        compiler_params=pltpu.CompilerParams(vmem_limit_bytes=VMEM_LIMIT),
        name="feed_forward",
    )(
        places,
        *normed,
        hidden_grad,
        *[source[0] for source in sources],
        *[source[1] for source in sources],
    )


def unmerge_kernel(parts, pieces, places_ref, gain_ref, middle_ref, up_ref, *refs):
    grad_refs, weight_refs = refs[:parts], refs[parts : 2 * parts]
    grad_out, sent_out, gain_out = refs[2 * parts : 2 * parts + 3]
    piece_outs = refs[2 * parts + 3 : 2 * parts + 3 + pieces]
    gathered = refs[-1]
    step_id = pl.program_id(0)
    depth = grad_refs[0].shape[2]

    @pl.when(step_id == 0)
    def _():
        for step in range(parts):
            first = pl.multiple_of(jnp.bitwise_xor(places_ref[1], step) * depth, 128)
            total = grad_refs[0][step]
            for ref in grad_refs[1:]:
                total = total + ref[step]
            grad_out[:, pl.ds(first, depth)] = total
        values, grad, gain = middle_ref[...], grad_out[...], gain_ref[...]
        scale = lax.rsqrt(jnp.mean(values * values, -1, keepdims=True) + EPS)
        unit_rows = values * scale
        weighted = grad * gain
        inner = jnp.mean(weighted * unit_rows, -1, keepdims=True)
        gain_out[...] = jnp.sum(grad * unit_rows, 0, keepdims=True)
        total = scale * (weighted - unit_rows * inner) + up_ref[...].astype(F32)
        grad_out[...] = total
        sent_out[...] = total.astype(BF16)

    count = pl.num_programs(0)
    group = gathered.shape[2]
    for step, ref in enumerate(weight_refs):
        width = ref.shape[0]
        first = jnp.bitwise_xor(places_ref[1], step) * (width * count) + step_id * width
        whose = jnp.bitwise_xor(first // group, places_ref[0])
        at = pl.multiple_of(first % group, 128) if width < group else 0
        gathered[whose, :, pl.ds(at, width)] = mm(sent_out[...], ref[...], ROWS_ROWS).astype(BF16)

    @pl.when(step_id == count - 1)
    def _():
        for at, ref in enumerate(piece_outs):
            ref[...] = gathered[at]


def unmerge(places, gain, middle, upstream, grads, weights, pieces):
    rows, width = middle.shape
    parts = len(weights)
    depth = grads[0].shape[2]
    group = VD // pieces
    tile = min(weights[0].shape[0], group)
    whole = pl.BlockSpec((rows, width), lambda j, place: (0, 0))
    one_row = pl.BlockSpec((1, width), lambda j, place: (0, 0))
    return pl.pallas_call(
        functools.partial(unmerge_kernel, parts, pieces),
        grid_spec=pltpu.PrefetchScalarGridSpec(
            num_scalar_prefetch=1,
            grid=(weights[0].shape[0] // tile,),
            in_specs=[one_row, whole, whole]
            + [pl.BlockSpec((parts, rows, depth), lambda j, place: (0, 0, 0))] * parts
            + [pl.BlockSpec((tile, width), lambda j, place: (j, 0))] * parts,
            out_specs=[whole, whole, one_row]
            + [pl.BlockSpec((rows, group), lambda j, place: (0, 0))] * pieces,
            scratch_shapes=[pltpu.VMEM((pieces, rows, group), BF16)],
        ),
        out_shape=[
            jax.ShapeDtypeStruct((rows, width), F32),
            jax.ShapeDtypeStruct((rows, width), BF16),
            jax.ShapeDtypeStruct((1, width), F32),
        ]
        + [jax.ShapeDtypeStruct((rows, group), BF16)] * pieces,
        compiler_params=pltpu.CompilerParams(vmem_limit_bytes=VMEM_LIMIT),
        name="split_heads",
    )(places, gain, middle, upstream, *grads, *weights)


def outer_kernel(parts, places_ref, *refs):
    left_refs, right_refs, out_refs = refs[:parts], refs[parts : 2 * parts], refs[2 * parts :]
    total = None
    for left, right in zip(left_refs, right_refs):
        term = mm(left[...], right[...], COLS_COLS)
        total = term if total is None else total + term
    (out_ref,) = out_refs
    chunks, several, height, _ = out_ref.shape
    for one in range(several):
        for at in range(chunks):
            first = (one * chunks + at) * height
            out_ref[at, one] = total[first : first + height].astype(out_ref.dtype)


def outer_products(places, lefts, own_right, rights, owners, chunks):
    rows, width = lefts[0].shape
    parts = len(lefts)
    columns = own_right.shape[1] // parts
    own = width // owners
    tile = max(own, 256)
    fixed = pl.BlockSpec((rows, columns), lambda j, place: (0, 0))
    return pl.pallas_call(
        functools.partial(outer_kernel, parts),
        grid_spec=pltpu.PrefetchScalarGridSpec(
            num_scalar_prefetch=1,
            grid=(width // tile,),
            in_specs=[pl.BlockSpec((rows, tile), lambda j, place: (0, j))] * parts
            + [pl.BlockSpec((rows, columns), lambda j, place: (0, place[1]))]
            + [fixed] * (parts - 1),
            out_specs=pl.BlockSpec(
                (chunks, tile // own, own // chunks, columns), lambda j, place: (0, j, 0, 0)
            ),
        ),
        out_shape=jax.ShapeDtypeStruct((chunks, owners, own // chunks, columns), BF16),
        compiler_params=pltpu.CompilerParams(vmem_limit_bytes=VMEM_LIMIT),
        name="outer_products",
    )(places, *lefts, own_right, *rights)


def rows_kernel(pieces, places_ref, *refs):
    left_refs, right_refs, out_ref, left, right = (
        refs[:pieces], refs[pieces : 2 * pieces], refs[2 * pieces], refs[-2], refs[-1],
    )
    rows = left_refs[0].shape[0]

    @pl.when(pl.program_id(0) == 0)
    def _():
        for at, ref in enumerate(left_refs):
            left[at * rows : (at + 1) * rows] = ref[...]

    for at, ref in enumerate(right_refs):
        right[at * rows : (at + 1) * rows] = ref[...]
    parts, height, _ = out_ref.shape
    for step in range(parts):
        first = pl.multiple_of(jnp.bitwise_xor(places_ref[1], step) * height, 128)
        out_ref[step] = mm(left[:, pl.ds(first, height)], right[...], COLS_COLS).astype(
            out_ref.dtype
        )


def own_rows(places, lefts, rights, parts):
    pieces = len(lefts)
    rows, columns = lefts[0].shape
    height = columns // parts
    width = rights[0].shape[1]
    tile = 512
    return pl.pallas_call(
        functools.partial(rows_kernel, pieces),
        grid_spec=pltpu.PrefetchScalarGridSpec(
            num_scalar_prefetch=1,
            grid=(width // tile,),
            in_specs=[pl.BlockSpec((rows, columns), lambda j, place: (0, 0))] * pieces
            + [pl.BlockSpec((rows, tile), lambda j, place: (0, j))] * pieces,
            out_specs=pl.BlockSpec((parts, height, tile), lambda j, place: (0, 0, j)),
            scratch_shapes=[
                pltpu.VMEM((pieces * rows, columns), BF16),
                pltpu.VMEM((pieces * rows, tile), BF16),
            ],
        ),
        out_shape=jax.ShapeDtypeStruct((parts, height, width), BF16),
        compiler_params=pltpu.CompilerParams(vmem_limit_bytes=VMEM_LIMIT),
        name="own_rows",
    )(places, *lefts, *rights)


def again_kernel(parts, places_ref, normed_ref, up_ref, *refs):
    gate_refs, wide_refs, down_ref = refs[:parts], refs[parts : 2 * parts], refs[2 * parts]
    hidden_ref, gate_out, wide_out = refs[-3:]
    depth = gate_refs[0].shape[0]
    gate, wide = None, None
    for step in range(parts):
        first = pl.multiple_of(jnp.bitwise_xor(places_ref[1], step) * depth, 128)
        left = normed_ref[:, pl.ds(first, depth)]
        one, two = mm(left, gate_refs[step][...]), mm(left, wide_refs[step][...])
        gate, wide = (one, two) if gate is None else (gate + one, wide + two)
    hidden_grad = mm(up_ref[...], down_ref[...], ROWS_ROWS)
    slope = jax.nn.sigmoid(gate)
    hidden_ref[...] = (gate * slope * wide).astype(BF16)
    gate_out[...] = (hidden_grad * wide * (slope * (1.0 + gate * (1.0 - slope)))).astype(BF16)
    wide_out[...] = (hidden_grad * gate * slope).astype(BF16)


def feed_again(places, normed, upstream, gates, wides, down, step, before=()):
    count, width = normed.shape
    parts = len(gates)
    depth, columns = gates[0].shape
    tile = 256
    tiles = count // tile
    there = lambda j, place: (jnp.bitwise_xor(place[1], step) * tiles + j, 0)
    here = lambda j, place: (j, 0)
    fixed = pl.BlockSpec((depth, columns), lambda j, place: (0, 0))
    carried = 1 + 2 + 2 * parts + 1
    return pl.pallas_call(
        functools.partial(again_kernel, parts),
        grid_spec=pltpu.PrefetchScalarGridSpec(
            num_scalar_prefetch=1,
            grid=(tiles,),
            in_specs=[pl.BlockSpec((tile, width), here), pl.BlockSpec((tile, width), there)]
            + [fixed] * (2 * parts)
            + [pl.BlockSpec((columns, width), lambda j, place: (0, 0))]
            + [pl.BlockSpec(memory_space=pl.ANY)] * len(before),
            out_specs=[pl.BlockSpec((tile, columns), there)]
            + [pl.BlockSpec((tile, columns), here)] * 2,
        ),
        out_shape=[
            jax.ShapeDtypeStruct((upstream.shape[0], columns), BF16),
            jax.ShapeDtypeStruct((count, columns), BF16),
            jax.ShapeDtypeStruct((count, columns), BF16),
        ],
        input_output_aliases={carried + at: at for at in range(len(before))},
        compiler_params=pltpu.CompilerParams(vmem_limit_bytes=VMEM_LIMIT),
        name="feed_again",
    )(places, normed, upstream, *gates, *wides, down, *before)


def place_in_kernel(columns_of, head_of, in_ref, out_ref, held, sems):
    step_id = pl.program_id(0)
    slot = lax.rem(step_id, 2)

    def copies(which, where):
        found = []
        for number, (low, width, first) in enumerate(columns_of):
            at = pl.multiple_of(first + head_of(which) * width, 128)
            found.append(
                pltpu.make_async_copy(
                    held.at[where, :, pl.ds(low, width)],
                    out_ref.at[:, pl.ds(at, width)],
                    sems.at[where, number],
                )
            )
        return found

    @pl.when(step_id >= 2)
    def _():
        for copy in copies(step_id - 2, slot):
            copy.wait()

    held[slot] = in_ref[:, 0].astype(F32).reshape(held.shape[1:])
    for copy in copies(step_id, slot):
        copy.start()

    @pl.when(step_id == pl.num_programs(0) - 1)
    def _():
        for copy in copies(step_id - 1, 1 - slot) + copies(step_id, slot):
            copy.wait()


def place_in(value, seqs):
    blocks, sources, rows, columns = value.shape
    heads = HEADS // seqs
    per_source = columns // HEAD_WIDTH
    columns_of = [(0, DK, 0), (DK, DK, KD), (2 * DK, DV, 2 * KD), (2 * DK + DV, DV, CONVW)]

    def head_of(step):
        source = step // per_source
        return source % seqs * heads + source // seqs * per_source + step % per_source

    return pl.pallas_call(
        functools.partial(place_in_kernel, columns_of, head_of),
        grid=(sources * per_source,),
        in_specs=[
            pl.BlockSpec(
                (blocks, 1, rows, HEAD_WIDTH), lambda h: (0, h // per_source, 0, h % per_source)
            )
        ],
        out_specs=pl.BlockSpec(memory_space=pl.ANY),
        out_shape=jax.ShapeDtypeStruct((blocks * rows, PROJW), F32),
        scratch_shapes=[
            pltpu.VMEM((2, blocks * rows, HEAD_WIDTH), F32),
            pltpu.SemaphoreType.DMA((2, len(columns_of))),
        ],
        compiler_params=pltpu.CompilerParams(vmem_limit_bytes=VMEM_LIMIT),
        name="place_w_in",
    )(value)


def place_gu_kernel(half, gate_ref, wide_ref, out_ref):
    def put(ref):
        width = ref.shape[2]
        for at in range(ref.shape[0]):
            out_ref[:, at * width : (at + 1) * width] = ref[at].astype(F32)

    @pl.when(pl.program_id(0) < half)
    def _():
        put(gate_ref)

    @pl.when(pl.program_id(0) >= half)
    def _():
        put(wide_ref)


def place_gu(gate, wide):
    sources, rows, width = gate.shape
    together = 1
    while together * width % 128:
        together *= 2
    half = sources // together
    return pl.pallas_call(
        functools.partial(place_gu_kernel, half),
        grid=(2 * half,),
        in_specs=[
            pl.BlockSpec((together, rows, width), lambda j: (jnp.minimum(j, half - 1), 0, 0)),
            pl.BlockSpec((together, rows, width), lambda j: (jnp.maximum(j - half, 0), 0, 0)),
        ],
        out_specs=pl.BlockSpec((rows, together * width), lambda j: (0, j)),
        out_shape=jax.ShapeDtypeStruct((rows, 2 * sources * width), F32),
        compiler_params=pltpu.CompilerParams(vmem_limit_bytes=VMEM_LIMIT),
        name="place_w_gu",
    )(gate, wide)


def line_first(value):
    return lax.ppermute(value, "replica", [(0, 1), (3, 2)])


def line_second(value):
    return lax.ppermute(value, "replica", [(1, 2), (2, 1)])


def line_third(value):
    return lax.ppermute(value, "replica", [(1, 0), (2, 3)])


def added(left, right):
    return (left.astype(F32) + right.astype(F32)).astype(BF16)


def pinned(*values):
    return lax.optimization_barrier(values)


def line_sum(value):
    value = added(value, line_first(value))
    value = added(value, line_second(value))
    return settled_pair((value, line_third(value)))


def settled_pair(pair):
    place = lax.axis_index("replica")
    return jnp.where((place == 1) | (place == 2), pair[0], pair[1]).astype(F32)


def swapped(value, axis, step):
    count = lax.axis_size(axis)
    return lax.ppermute(value, axis, [(source, source ^ step) for source in range(count)])


def around(value, axis):
    return [value] + [swapped(value, axis, step) for step in range(1, lax.axis_size(axis))]


def settled(parts, index):
    stacked = jnp.stack(parts)
    return [
        lax.dynamic_index_in_dim(stacked, jnp.bitwise_xor(index, at), 0, keepdims=False)
        for at in range(len(parts))
    ]


def part_of(value, index, count, axis):
    width = value.shape[axis] // count
    return lax.dynamic_slice_in_dim(value, index * width, width, axis)


def dot(left, right):
    return jnp.dot(left, right, preferred_element_type=F32)


def dot_rows(left, right):
    return lax.dot_general(left, right, (((1,), (1,)), ((), ())), preferred_element_type=F32)


def dot_cols(left, right):
    return lax.dot_general(left, right, (((0,), (0,)), ((), ())), preferred_element_type=F32)


def rms_parts(values):
    return lax.rsqrt(jnp.mean(values * values, -1, keepdims=True) + EPS)


def rms_back(values, scale, gain, grad):
    weighted = grad * gain
    unit_rows = values * scale
    inner = jnp.mean(weighted * unit_rows, -1, keepdims=True)
    return scale * (weighted - unit_rows * inner), jnp.sum(grad * unit_rows, 0)


def body(
    tokens,
    cotangent,
    lengths,
    norm_gains,
    w_in,
    w_ab,
    conv_weight,
    gate_params,
    onorm_gain,
    w_o,
    w_gu,
    w_down,
):
    shards, seqs, replicas = (lax.axis_size(name) for name in EVERY)
    shard, seq = lax.axis_index("shard"), lax.axis_index("seq")
    owners = shards * seqs
    owner = shard * seqs + seq
    micro, row = tokens.shape[0], tokens.shape[1]
    flat = micro * row
    length = row * seqs
    heads = HEADS // seqs
    depth = D // shards
    seq_place = jnp.reshape(seq, (1,)).astype(jnp.int32)
    shard_place = jnp.reshape(shard, (1,)).astype(jnp.int32)
    places = jnp.stack([seq, shard]).astype(jnp.int32)

    def blocks(value, count, axis=1):
        return [part_of(value, jnp.bitwise_xor(shard, step), count, axis) for step in range(count)]

    flat_tokens = tokens.reshape(flat, D)
    in_own = pick_heads(seq_place, w_in, heads)
    sent_tokens, in_own = pinned(flat_tokens, in_own)
    pieces = around(sent_tokens, "seq")
    gain_parts = around(norm_gains, "shard")
    in_parts = around(in_own, "shard")
    taps_parts = around(conv_weight, "shard")
    ab_parts = around(w_ab, "shard")
    gains = jnp.concatenate(settled(gain_parts, shard), 1).astype(F32)
    gain_first, gain_second = gains[:1], gains[1:]
    taps = jnp.concatenate(settled(taps_parts, shard), 1)
    upstream = cotangent.reshape(flat, D)
    up_parts = around(upstream, "shard")
    hidden_grad = dot_rows(jnp.concatenate(up_parts, 0), w_down)
    own_out, own_gu, late_up, hidden_grad, *arrived = pinned(
        w_o, w_gu, upstream, hidden_grad, *pieces, *in_parts
    )
    pieces, in_parts = arrived[:seqs], arrived[seqs:]
    all_up = lax.all_gather(late_up, EVERY, axis=0, tiled=True)
    out_parts = around(own_out, "shard")
    gu_parts = around(own_gu, "shard")

    normed, projected = project(shard_place, gain_first, pieces, in_parts)
    rate_in = sum(dot(left, right) for left, right in zip(blocks(normed, shards), ab_parts))
    rate_in = part_of(rate_in.reshape(seqs, micro, row, 2, HEADS), seq, seqs, 4)
    rate_in = jnp.stack(settled(list(rate_in), seq))
    rate_in = jnp.transpose(rate_in, (3, 1, 4, 0, 2)).reshape(2, micro, heads, length)
    position = jnp.arange(length, dtype=jnp.int32)
    valid = (position[None, :] < lengths[:, None]).astype(F32)[:, None, :]
    own_params = part_of(gate_params, seq, seqs, 1)[:, None, :, None]
    rate_shifted = rate_in[0] + own_params[1]
    decays = -jnp.exp(own_params[0]) * jax.nn.softplus(rate_shifted) * valid
    written = jax.nn.sigmoid(rate_in[1])
    rates = jnp.stack([jnp.maximum(decays, LOWEST_DECAY), written * valid], 2)
    rates = jnp.pad(rates, ((0, 0), (0, 0), (0, SMALL_ROWS - 2), (0, 0)))
    gain_row = onorm_gain.reshape(1, DV)
    projected = projected.reshape(seqs, micro, row, -1)
    *gated, inverse, update = mixer_forward(seq_place, projected, taps, rates, gain_row, 2)
    gated = [item.reshape(flat, heads * DV) for item in gated]

    mixed_parts = [gated[0]] + [swapped(gated[step], "seq", step) for step in range(1, seqs)]
    arrived = pinned(*mixed_parts, *gu_parts)
    mixed_parts, gu_parts = list(arrived[:seqs]), list(arrived[seqs:])

    middle, renormed, *mixed_left = merge(
        places, gain_second, flat_tokens, mixed_parts, out_parts
    )
    line_renormed = lax.all_gather(renormed, "replica", axis=0, tiled=True)

    mixed_left = [
        swapped(item, "seq", step) if step else item for step, item in enumerate(mixed_left)
    ]
    fed = feed(places, around(renormed, "shard"), hidden_grad, gu_parts)
    fed = pinned(*fed, *mixed_left)
    fed, mixed_left = fed[: shards + 1], fed[shards + 1 :]
    grads_back = [fed[0]] + [swapped(fed[step], "shard", step) for step in range(1, shards)]
    middle_grad, mixed_grad, gain2_grad, *gated_grad = unmerge(
        places, gain_second, middle, upstream, grads_back, out_parts, seqs
    )
    hidden = fed[shards]

    ff_own = FF // owners
    own_down = part_of(w_down, seq, seqs, 0)
    own_gate = [part_of(part, owner, 2 * owners, 1) for part in gu_parts]
    own_wide = [part_of(part, owners + owner, 2 * owners, 1) for part in gu_parts]

    gated_grad = [
        swapped(item, "seq", step) if step else item for step, item in enumerate(gated_grad)
    ]
    all_up, mixed_grad, own_down, *others = pinned(
        all_up, mixed_grad, own_down, *own_gate, *own_wide, *gated_grad
    )
    own_gate, own_wide = others[:shards], others[shards : 2 * shards]
    gated_grad = others[2 * shards :]
    gated_grad = [item.reshape(micro, row, heads * DV) for item in gated_grad]
    mid_pieces = around(mixed_grad, "seq")
    proj_grad, small_grad = mixer_backward(
        seq_place, projected, taps, rates, gain_row, inverse, update, gated_grad, 1
    )
    proj_grad, *mid_pieces = pinned(proj_grad, *mid_pieces)
    rows_all = seqs * flat
    proj_grad = proj_grad.reshape(rows_all, -1)
    pair_proj = [
        swapped(part_of(proj_grad, jnp.bitwise_xor(shard, step), shards, 1), "shard", step)
        for step in range(1, shards)
    ]

    pair_normed = around(normed, "shard")
    spread = jnp.broadcast_to(line_renormed[None], (seqs,) + line_renormed.shape)
    spread, *pair_proj = pinned(spread, *pair_proj)
    grad_in = outer_products(places, pair_normed, proj_grad, pair_proj, owners, replicas)
    width = grad_in.shape[3]
    proj_grad, small_grad, grad_in, spread, *mid_pieces = pinned(
        proj_grad, small_grad, grad_in, spread, *mid_pieces
    )
    grad_in = lax.psum_scatter(grad_in, "replica", scatter_dimension=0, tiled=False)
    own_renormed = lax.all_to_all(spread, "seq", split_axis=0, concat_axis=0).reshape(-1, D)

    grad_out = own_rows(places, mixed_left, mid_pieces, shards)
    grad_out = functools.reduce(
        added, [grad_out[0]] + [swapped(grad_out[step], "shard", step) for step in range(1, shards)]
    )

    def input_gradient_parts(proj_grad, small_grad):
        decay_grad = small_grad[:, :, 5, :length]
        write_grad = small_grad[:, :, 6, :length]
        shifted_grad = decay_grad * -jnp.exp(own_params[0]) * jax.nn.sigmoid(rate_shifted) * valid
        params_grad = jnp.stack(
            [jnp.sum(decay_grad * decays, (0, 2)), jnp.sum(shifted_grad, (0, 2))]
        )
        rate_grad = jnp.stack([shifted_grad, write_grad * written * (1.0 - written) * valid])
        rate_grad = jnp.transpose(rate_grad.reshape(2, micro, heads, seqs, row), (3, 1, 4, 0, 2))
        rate_grad = jnp.stack(settled(list(rate_grad), seq))
        rate_grad = rate_grad.reshape(rows_all, 2 * heads)
        grad_ab = lax.dot_general(
            rate_grad, normed.astype(F32), (((0,), (0,)), ((), ())), precision=HIGHEST
        )
        own_ab = [
            part_of(part.reshape(depth, 2, HEADS), seq, seqs, 2).reshape(depth, 2 * heads)
            for part in ab_parts
        ]
        normed_grad = [
            dot_rows(proj_grad, part)
            + lax.dot_general(
                rate_grad, ab.astype(F32), (((1,), (1,)), ((), ())), precision=HIGHEST
            )
            for part, ab in zip(in_parts, own_ab)
        ]
        return (*normed_grad, grad_ab, params_grad)

    def input_gradient(*normed_grad):
        *normed_grad, grad_ab, params_grad = normed_grad
        normed_grad = jnp.concatenate(settled(normed_grad, shard), 1).reshape(seqs, flat, D)
        normed_grad = normed_grad[0] + sum(
            swapped(normed_grad[step].astype(BF16), "seq", step).astype(F32)
            for step in range(1, seqs)
        )
        flat_in = flat_tokens.astype(F32)
        inputs_grad, gain1_grad = rms_back(flat_in, rms_parts(flat_in), gains[0], normed_grad)
        input_grads = (inputs_grad + middle_grad).astype(BF16).reshape(micro, row, D)
        return input_grads, gain1_grad, grad_ab, params_grad

    def to_group(value):
        return lax.all_to_all(value, GROUP, split_axis=0, concat_axis=0, tiled=False)

    def to_owners(value):
        return to_group(value.astype(BF16).reshape(owners, D // owners, ff_own))

    normed_parts = input_gradient_parts(proj_grad, small_grad)
    replica = lax.axis_index("replica")
    grad_out = [
        swapped(part_of(grad_out, jnp.bitwise_xor(replica, step), replicas, 0), "replica", step)
        if step
        else part_of(grad_out, replica, replicas, 0)
        for step in range(replicas)
    ]
    own_renormed, *normed_parts = pinned(own_renormed, *normed_parts)
    input_grads, gain1_grad, grad_ab, params_grad = input_gradient(*normed_parts)
    gain2_grad = gain2_grad[0]
    all_renormed = around(own_renormed, "shard")

    def again(at, before=()):
        return feed_again(
            places, all_renormed[at], all_up, own_gate, own_wide, own_down, at, before
        )

    def over_tokens(lefts, rights):
        return sum(dot_cols(left, right) for left, right in zip(lefts, rights))

    parts = [again(0)]
    input_grads, gain1_grad, grad_ab, params_grad, *others = pinned(
        input_grads, gain1_grad, grad_ab, params_grad, *grad_out, *parts[0]
    )
    grad_out, parts[0] = others[:replicas], others[replicas:]
    grad_out = sum(item.astype(F32) for item in grad_out).astype(BF16)
    taps_grad = jnp.sum(small_grad[:, :, :KERNEL], 0)
    conv_grad = jnp.concatenate(
        [
            jnp.swapaxes(taps_grad[..., low:high], 0, 1).reshape(KERNEL, -1)
            for low, high in ((0, DK), (DK, 2 * DK), (2 * DK, 2 * DK + DV))
        ],
        1,
    )
    onorm_grad = jnp.sum(small_grad[:, :, 4, :DV], (0, 1))
    loose = jnp.concatenate([onorm_grad, params_grad.reshape(-1)])
    loose = jnp.pad(loose, (0, D - loose.size))
    rows_ab = 2 * heads
    smalls = jnp.concatenate(
        [grad_ab, conv_grad, loose[None], gain1_grad[None], gain2_grad[None]], 0
    )
    step = 1
    while step < shards:
        smalls = smalls + swapped(smalls, "shard", step)
        step *= 2
    rows_small = smalls.shape[0]
    high = lax.optimization_barrier(smalls.astype(BF16))
    low = (smalls - high.astype(F32)).astype(BF16)
    fill = jnp.zeros((-(2 * rows_small) % 16, D), BF16)
    rows_own = grad_out.shape[0]
    grad_out = jnp.concatenate([grad_out, high, low, fill], 0)
    grad_out, *all_renormed = pinned(grad_out, *all_renormed)
    grad_out = lax.all_gather(grad_out, "replica", axis=0)
    for at in range(1, shards):
        parts.append(again(at, parts[-1][:1]))
    grad_in, hidden, own_hidden = pinned(grad_in, hidden, parts[-1][0])
    grad_in = to_group(grad_in)
    gate_grad, wide_grad = ([part[which] for part in parts] for which in (1, 2))
    grad_gate = over_tokens(all_renormed, gate_grad).astype(BF16)
    grad_in, grad_gate, own_hidden, *wide_grad = pinned(
        grad_in, grad_gate, own_hidden, *wide_grad
    )
    grad_in = lax.all_gather(grad_in, "replica", axis=0)
    grad_gate = to_owners(grad_gate)
    grad_wide = over_tokens(all_renormed, wide_grad).astype(BF16)
    grad_down = dot_cols(own_hidden, all_up)
    grad_wide, grad_gate, grad_out = pinned(grad_wide, grad_gate, grad_out)
    grad_wide = to_owners(grad_wide)
    rows_down = dot(hidden, w_down).reshape(shards, flat, D)
    result = (
        middle
        + rows_down[0]
        + sum(swapped(rows_down[step], "shard", step) for step in range(1, shards))
    )
    results = result.astype(BF16).reshape(micro, row, D)
    smalls = grad_out[:, rows_own : rows_own + 2 * rows_small].astype(F32)
    smalls = jnp.sum(smalls[:, :rows_small] + smalls[:, rows_small:], 0)
    grad_out = grad_out[:, :rows_own].reshape(replicas * rows_own, D).astype(F32)
    every = jnp.stack(settled(around(smalls, "seq"), seq))
    grad_gu = place_gu(grad_gate, grad_wide)
    if width % HEAD_WIDTH == 0:
        grad_in = place_in(grad_in, seqs)
    else:
        grad_in = grad_in.reshape(replicas, shards, seqs, -1, width)
        grad_in = jnp.transpose(grad_in, (0, 3, 2, 1, 4)).reshape(D // owners, HEADS, HEAD_WIDTH)
        cuts = (0, DK, 2 * DK, 2 * DK + DV, HEAD_WIDTH)
        grad_in = jnp.concatenate(
            [
                grad_in[..., low:high].reshape(D // owners, -1)
                for low, high in zip(cuts[:-1], cuts[1:])
            ],
            1,
        ).astype(F32)

    ab_total = jnp.transpose(every[:, :rows_ab].reshape(seqs, 2, heads, D), (3, 1, 0, 2))
    ab_total = ab_total.reshape(D, 2 * HEADS)
    conv_all = every[:, rows_ab : rows_ab + KERNEL]
    conv_total = jnp.concatenate(
        [
            jnp.swapaxes(conv_all[..., low:high], 0, 1).reshape(KERNEL, -1)
            for low, high in (
                (0, heads * DK),
                (heads * DK, 2 * heads * DK),
                (2 * heads * DK, heads * (2 * DK + DV)),
            )
        ],
        1,
    )
    loose_all = every[:, rows_ab + KERNEL]
    onorm_total = jnp.sum(loose_all[:, :DV], 0)
    params_total = loose_all[:, DV : DV + 2 * heads].reshape(seqs, 2, heads)
    params_total = jnp.swapaxes(params_total, 0, 1).reshape(2, HEADS)
    gains_total = jnp.sum(every[:, rows_ab + KERNEL + 1 : rows_ab + KERNEL + 3], 0)
    gains_own = part_of(gains_total, owner, owners, 1)
    ab_own = part_of(ab_total, owner, owners, 0)
    conv_own = part_of(conv_total, owner, owners, 1)
    return (
        results,
        input_grads,
        gains_own,
        grad_in,
        ab_own,
        conv_own,
        params_total,
        onorm_total,
        grad_out,
        grad_gu,
        grad_down,
    )


def solution(mesh):
    in_specs = (
        P(("shard", "replica"), "seq", None),
        P(("shard", "replica"), "seq", None),
        P(("shard", "replica")),
        P(None, "shard"),
        P("shard", None),
        P("shard", None),
        P(None, "shard"),
        P(),
        P(),
        P("shard", None),
        P("shard", None),
        P("shard", None),
    )
    out_specs = (
        P(("shard", "replica"), "seq", None),
        P(("shard", "replica"), "seq", None),
        P(None, ("shard", "seq")),
        P(("shard", "seq"), None),
        P(("shard", "seq"), None),
        P(None, ("shard", "seq")),
        P(),
        P(),
        P(("shard", "seq"), None),
        P(("shard", "seq"), None),
        P(("shard", "seq"), None),
    )
    return jax.shard_map(body, mesh=mesh, in_specs=in_specs, out_specs=out_specs, check_vma=False)
```

```python
import functools

import jax
import jax.numpy as jnp
from jax import lax
from jax.experimental import pallas as pl
from jax.experimental.pallas import tpu as pltpu
from jax.sharding import PartitionSpec as P

D = 2048
HEADS = 16
DK = 128
DV = 256
FF = 5632
KERNEL = 4
KD = 2048
VD = 4096
CONVW = 8192
PROJW = 12288
EPS = 1e-06
HIGHEST = lax.Precision.HIGHEST
LOWEST_DECAY = -104.0
F32 = jnp.float32
BF16 = jnp.bfloat16
EVERY = ("shard", "seq", "replica")
GROUP = ("shard", "seq")


def mm(left, right, dims=((1,), (0,))):
    return lax.dot_general(
        left.astype(BF16), right.astype(BF16), (dims, ((), ())), preferred_element_type=F32
    )


def split(value):
    high = value.astype(BF16)
    return high, (value - high.astype(F32)).astype(BF16)


def mm3s(left, right, dims=((1,), (0,))):
    return (
        mm(left[0], right[0], dims) + mm(left[0], right[1], dims) + mm(left[1], right[0], dims)
    )


def mm3(left, right, dims=((1,), (0,))):
    return mm3s(split(left), split(right), dims)


ROWS_ROWS = ((1,), (1,))
COLS_COLS = ((0,), (0,))


def delayed(value, steps, rows):
    if steps == 0:
        return value
    return jnp.where(rows >= steps, pltpu.roll(value, steps, 0), 0.0)


def advanced(value, steps, rows):
    if steps == 0:
        return value
    length = value.shape[0]
    return jnp.where(rows < length - steps, pltpu.roll(value, length - steps, 0), 0.0)


def convolved(source, taps, rows):
    mixed = taps[KERNEL - 1 : KERNEL] * source
    for offset in range(KERNEL - 1):
        mixed = mixed + taps[offset : offset + 1] * delayed(source, KERNEL - 1 - offset, rows)
    return mixed


def unit(value):
    scale = lax.rsqrt(jnp.sum(value * value, -1, keepdims=True) + EPS)
    return value * scale, scale


def decay_matrices(rates):
    length = rates.shape[1]
    row_ids = lax.broadcasted_iota(jnp.int32, (length, length), 0)
    col_ids = lax.broadcasted_iota(jnp.int32, (length, length), 1)
    decay_row = rates[0:1]
    rate_row = rates[1:2]
    diagonal = row_ids == col_ids
    running = jnp.sum(jnp.where(row_ids >= col_ids, decay_row, 0.0), 1, keepdims=True)
    running_row = jnp.sum(jnp.where(diagonal, running, 0.0), 0, keepdims=True)
    rate = jnp.sum(jnp.where(diagonal, rate_row, 0.0), 1, keepdims=True)
    spread = jnp.minimum(running - running_row, 0.0)
    weight = jnp.where(row_ids >= col_ids, jnp.exp(spread), 0.0)
    return row_ids, col_ids, rate, weight


def lower_inverses(systems, row_ids, col_ids):
    length = row_ids.shape[0]
    eye = (row_ids == col_ids).astype(F32)
    same = jnp.bitwise_xor(row_ids, col_ids)
    inverses = [eye - jnp.where(same < 2, system, 0.0) for system in systems]
    size = 2
    while size < length:
        level = (same >= size) & (same < 2 * size)
        halves = [split(inverse) for inverse in inverses]
        inner = [
            mm3s(split(jnp.where(level, system, 0.0)), half)
            for system, half in zip(systems, halves)
        ]
        inverses = [
            inverse - mm3s(half, split(item))
            for inverse, half, item in zip(inverses, halves, inner)
        ]
        size *= 2
    return inverses


def head_inputs(source, taps):
    rows = lax.broadcasted_iota(jnp.int32, (source.shape[0], 1), 0)
    cuts = (0, DK, 2 * DK, 2 * DK + DV)
    raw = [source[:, low:high].astype(BF16).astype(F32) for low, high in zip(cuts, cuts[1:])]
    mixed = [convolved(item, kernel, rows) for item, kernel in zip(raw, taps)]
    slopes = [jax.nn.sigmoid(item) for item in mixed]
    query_unit, query_scale = unit(mixed[0] * slopes[0])
    key_rows, key_scale = unit(mixed[1] * slopes[1])
    values = mixed[2] * slopes[2]
    queries = query_unit * DK ** (-0.5)
    return raw, rows, mixed, slopes, queries, key_rows, values, query_unit, query_scale, key_scale


def slot_rows(ref, place, slot, low, high):
    pieces = ref.shape[0]
    return jnp.concatenate(
        [ref[jnp.bitwise_xor(place, j), slot, :, low:high] for j in range(pieces)], 0
    )


def taps_of(refs, head):
    return [
        ref[:, head * width : (head + 1) * width].astype(F32)
        for ref, width in zip(refs, (DK, DK, DV))
    ]


def forward_kernel(
    place_ref, proj_ref, taps_q, taps_k, taps_v, rates_ref, gain_ref, *outs
):
    *gated_refs, inverse_ref, update_ref, kept = outs
    place = place_ref[0]
    micro, together = rates_ref.shape[0], rates_ref.shape[1]
    pairs = [(slot, head) for slot in range(micro) for head in range(together)]
    work = []
    for slot, head in pairs:
        source = slot_rows(proj_ref, place, slot, head * HEAD_WIDTH, (head + 1) * HEAD_WIDTH)
        items = head_inputs(source, taps_of((taps_q, taps_k, taps_v), head))
        queries, key_rows, values = items[4:7]
        row_ids, col_ids, rate, weight = decay_matrices(rates_ref[slot, head])
        system = jnp.where(
            row_ids > col_ids, rate * mm3(key_rows, key_rows, ROWS_ROWS) * weight, 0.0
        )
        scores = (mm(queries, key_rows, ROWS_ROWS) * weight).astype(BF16)
        gate = source[:, 2 * DK + DV :]
        work.append((system, scores, rate * values, gate * jax.nn.sigmoid(gate)))
    inverses = lower_inverses([item[0] for item in work], row_ids, col_ids)
    row = proj_ref.shape[2]
    for (slot, head), item, inverse in zip(pairs, work, inverses):
        update = mm3(inverse, item[2])
        outputs = mm(item[1], update)
        scaled = (
            outputs
            * lax.rsqrt(jnp.mean(outputs * outputs, -1, keepdims=True) + EPS)
            * gain_ref[...]
        )
        inverse_ref[slot, head] = inverse
        update_ref[slot, head] = update
        kept[...] = (scaled * item[3]).reshape(kept.shape)
        for step, ref in enumerate(gated_refs):
            ref[slot, :, head * DV : (head + 1) * DV] = kept[jnp.bitwise_xor(place, step)].astype(
                ref.dtype
            )


def unit_back(grad, direction, scale):
    return scale * (grad - direction * jnp.sum(grad * direction, -1, keepdims=True))


def backward_kernel(
    place_ref, proj_ref, taps_q, taps_k, taps_v, rates_ref, gain_ref, inverse_ref, update_ref,
    *refs,
):
    *grad_refs, dproj_ref, small_ref, taken, kept = refs
    place = place_ref[0]
    micro, together = rates_ref.shape[0], rates_ref.shape[1]
    small_ref[...] = jnp.zeros_like(small_ref)
    for slot in range(micro):
        for head in range(together):
            backward_head(
                place, slot, head, proj_ref, (taps_q, taps_k, taps_v), rates_ref, gain_ref,
                inverse_ref, update_ref, grad_refs, dproj_ref, small_ref,
                taken.at[slot, head], kept.at[slot, head],
            )


def backward_head(
    place, slot, head, proj_ref, taps_refs, rates_ref, gain_ref, inverse_ref, update_ref,
    grad_refs, dproj_ref, small_ref, taken, kept,
):
    source = slot_rows(proj_ref, place, slot, head * HEAD_WIDTH, (head + 1) * HEAD_WIDTH)
    taps = taps_of(taps_refs, head)
    raw, rows, mixed, slopes, queries, key_rows, values, query_unit, query_scale, key_scale = (
        head_inputs(source, taps)
    )
    for step, ref in enumerate(grad_refs):
        taken[jnp.bitwise_xor(place, step)] = ref[slot, :, head * DV : (head + 1) * DV]
    upstream = jnp.concatenate([taken[j] for j in range(len(grad_refs))], 0).astype(F32)
    row_ids, col_ids, rate, weight = decay_matrices(rates_ref[slot, head])
    inner = mm3(key_rows, key_rows, ROWS_ROWS)
    strict = row_ids > col_ids
    keyed = jnp.where(strict, inner * weight, 0.0)
    scores = mm(queries, key_rows, ROWS_ROWS) * weight
    inverse = inverse_ref[slot, head]
    update = update_ref[slot, head]
    outputs = mm(scores, update)
    gate = source[:, 2 * DK + DV :]
    gate_slope = jax.nn.sigmoid(gate)
    out_scale = lax.rsqrt(jnp.mean(outputs * outputs, -1, keepdims=True) + EPS)
    out_unit = outputs * out_scale
    gain = gain_ref[...]
    scaled_grad = upstream * (gate * gate_slope)
    gate_grad = upstream * out_unit * gain * (gate_slope * (1.0 + gate * (1.0 - gate_slope)))
    gain_grad = jnp.sum(scaled_grad * out_unit, 0, keepdims=True)
    unit_grad = scaled_grad * gain
    out_grad = out_scale * (
        unit_grad - out_unit * jnp.mean(unit_grad * out_unit, -1, keepdims=True)
    )
    scores_grad = jnp.where(row_ids >= col_ids, mm(out_grad, update, ROWS_ROWS), 0.0)
    update_grad = mm(scores, out_grad, COLS_COLS)
    target_grad = mm3(inverse, update_grad, COLS_COLS)
    system_grad = jnp.where(strict, -mm(target_grad, update, ROWS_ROWS), 0.0)
    value_grad = rate * target_grad
    keyed_grad = system_grad * keyed
    rate_grad = jnp.sum(target_grad * values, 1, keepdims=True) + jnp.sum(
        keyed_grad, 1, keepdims=True
    )
    spread_grad = keyed_grad * rate + scores_grad * scores
    inner_grad = system_grad * weight * rate
    raw_scores_grad = scores_grad * weight
    query_grad = mm(raw_scores_grad, key_rows) * DK ** (-0.5)
    key_grad = (
        mm(raw_scores_grad, queries, COLS_COLS)
        + mm(inner_grad, key_rows)
        + mm(inner_grad, key_rows, COLS_COLS)
    )
    diagonal = row_ids == col_ids
    column_sum = jnp.sum(spread_grad, 0, keepdims=True)
    running_grad = jnp.sum(spread_grad, 1, keepdims=True) - jnp.sum(
        jnp.where(diagonal, column_sum, 0.0), 1, keepdims=True
    )
    decay_grad = jnp.sum(jnp.where(row_ids >= col_ids, running_grad, 0.0), 0, keepdims=True)
    rate_grad_row = jnp.sum(jnp.where(diagonal, rate_grad, 0.0), 0, keepdims=True)
    active_grads = (
        unit_back(query_grad, query_unit, query_scale),
        unit_back(key_grad, key_rows, key_scale),
        value_grad,
    )
    cuts = (0, DK, 2 * DK, 2 * DK + DV, HEAD_WIDTH)
    for low, high, grad_out, plain, before, slope, kernel in zip(
        cuts, cuts[1:], active_grads, raw, mixed, slopes, taps
    ):
        mixed_grad = grad_out * (slope * (1.0 + before * (1.0 - slope)))
        total = kernel[KERNEL - 1 : KERNEL] * mixed_grad
        for offset in range(KERNEL):
            steps = KERNEL - 1 - offset
            if steps:
                total = total + kernel[offset : offset + 1] * advanced(mixed_grad, steps, rows)
            small_ref[slot, head, offset : offset + 1, low:high] = jnp.sum(
                mixed_grad * delayed(plain, steps, rows), 0, keepdims=True
            )
        kept[:, :, low:high] = total.reshape(kept.shape[:2] + (high - low,))
    kept[:, :, cuts[3] : cuts[4]] = gate_grad.reshape(kept.shape[:2] + (DV,))
    for step in range(kept.shape[0]):
        dproj_ref[step, slot, :, head * HEAD_WIDTH : (head + 1) * HEAD_WIDTH] = kept[
            jnp.bitwise_xor(place, step)
        ].astype(dproj_ref.dtype)
    small_ref[slot, head, 4:5, 0:DV] = gain_grad
    length = decay_grad.shape[1]
    small_ref[slot, head, 5:6, 0:length] = decay_grad
    small_ref[slot, head, 6:7, 0:length] = rate_grad_row


VMEM_LIMIT = 56 * 1024 * 1024
HEAD_WIDTH = 2 * DK + 2 * DV
SMALL_ROWS = 8


def mixer_specs(pieces, micro, row, heads, length, together):
    def slots(width):
        return pl.BlockSpec((micro, row, together * width), lambda h, place: (0, 0, h))

    def taps(width, first):
        at = first // (together * width)
        return pl.BlockSpec(
            (KERNEL, together * width),
            lambda h, place: (0, at + place[0] * (heads // together) + h),
        )

    proj = pl.BlockSpec(
        (pieces, micro, row, together * HEAD_WIDTH), lambda h, place: (0, 0, 0, h)
    )
    kernel = [taps(DK, 0), taps(DK, KD), taps(DV, 2 * KD)]
    rates = pl.BlockSpec((micro, together, SMALL_ROWS, length), lambda h, place: (0, h, 0, 0))
    gain = pl.BlockSpec((1, DV), lambda h, place: (0, 0))

    def square(width):
        return pl.BlockSpec((micro, together, length, width), lambda h, place: (0, h, 0, 0))

    return slots, proj, kernel, rates, gain, square


def mixer_forward(place, projected, taps, rates, gain, together):
    pieces, micro, row, _ = projected.shape
    heads, length = rates.shape[1], rates.shape[3]
    slots, proj, kernel, rate_spec, gain_spec, square = mixer_specs(
        pieces, micro, row, heads, length, together
    )
    return pl.pallas_call(
        forward_kernel,
        grid_spec=pltpu.PrefetchScalarGridSpec(
            num_scalar_prefetch=1,
            grid=(heads // together,),
            in_specs=[proj] + kernel + [rate_spec, gain_spec],
            out_specs=[slots(DV)] * pieces + [square(length), square(DV)],
            scratch_shapes=[pltpu.VMEM((pieces, row, DV), F32)],
        ),
        out_shape=[jax.ShapeDtypeStruct((micro, row, heads * DV), BF16)] * pieces
        + [
            jax.ShapeDtypeStruct((micro, heads, length, length), F32),
            jax.ShapeDtypeStruct((micro, heads, length, DV), F32),
        ],
        compiler_params=pltpu.CompilerParams(vmem_limit_bytes=VMEM_LIMIT),
        name="mixer_forward",
    )(place, projected, taps, taps, taps, rates, gain)


def mixer_backward(place, projected, taps, rates, gain, inverse, update, grads, together):
    pieces, micro, row, _ = projected.shape
    heads, length = rates.shape[1], rates.shape[3]
    slots, proj, kernel, rate_spec, gain_spec, square = mixer_specs(
        pieces, micro, row, heads, length, together
    )
    small_width = 2 * DK + DV
    return pl.pallas_call(
        backward_kernel,
        grid_spec=pltpu.PrefetchScalarGridSpec(
            num_scalar_prefetch=1,
            grid=(heads // together,),
            in_specs=[proj]
            + kernel
            + [rate_spec, gain_spec, square(length), square(DV)]
            + [slots(DV)] * pieces,
            out_specs=[
                proj,
                pl.BlockSpec(
                    (micro, together, SMALL_ROWS, small_width), lambda h, place: (0, h, 0, 0)
                ),
            ],
            scratch_shapes=[
                pltpu.VMEM((micro, together, pieces, row, DV), BF16),
                pltpu.VMEM((micro, together, pieces, row, HEAD_WIDTH), F32),
            ],
        ),
        out_shape=[
            jax.ShapeDtypeStruct((pieces, micro, row, heads * HEAD_WIDTH), BF16),
            jax.ShapeDtypeStruct((micro, heads, SMALL_ROWS, small_width), F32),
        ],
        compiler_params=pltpu.CompilerParams(vmem_limit_bytes=VMEM_LIMIT),
        name="mixer_backward",
    )(place, projected, taps, taps, taps, rates, gain, inverse, update, *grads)


def pick_kernel(place_ref, q_ref, k_ref, v_ref, g_ref, out_ref):
    at = 0
    for ref in (q_ref, k_ref, v_ref, g_ref):
        out_ref[:, at : at + ref.shape[1]] = ref[...]
        at += ref.shape[1]


def pick_heads(place, w_in, heads):
    depth = w_in.shape[0]

    def one(width, first):
        at = first // width
        return pl.BlockSpec((depth, width), lambda h, place: (0, at + place[0] * heads + h))

    return pl.pallas_call(
        pick_kernel,
        grid_spec=pltpu.PrefetchScalarGridSpec(
            num_scalar_prefetch=1,
            grid=(heads,),
            in_specs=[one(DK, 0), one(DK, KD), one(DV, 2 * KD), one(DV, CONVW)],
            out_specs=pl.BlockSpec((depth, HEAD_WIDTH), lambda h, place: (0, h)),
        ),
        out_shape=jax.ShapeDtypeStruct((depth, heads * HEAD_WIDTH), w_in.dtype),
        compiler_params=pltpu.CompilerParams(vmem_limit_bytes=VMEM_LIMIT),
        name="pick_heads",
    )(place, w_in, w_in, w_in, w_in)


def project_kernel(parts, pieces, place_ref, gain_ref, *refs):
    piece_refs, weight_refs = refs[:pieces], refs[pieces : pieces + parts]
    normed_ref, out_ref = refs[pieces + parts :]
    rows = piece_refs[0].shape[0]

    @pl.when(pl.program_id(0) == 0)
    def _():
        for at, ref in enumerate(piece_refs):
            values = ref[...].astype(F32)
            scale = lax.rsqrt(jnp.mean(values * values, -1, keepdims=True) + EPS)
            normed_ref[at * rows : (at + 1) * rows] = (values * scale * gain_ref[...]).astype(BF16)

    total = None
    for step, ref in enumerate(weight_refs):
        depth = ref.shape[0]
        at = pl.multiple_of(jnp.bitwise_xor(place_ref[0], step) * depth, 128)
        term = jnp.dot(normed_ref[:, pl.ds(at, depth)], ref[...], preferred_element_type=F32)
        total = term if total is None else total + term
    out_ref[...] = total


def project(shard_place, gain, piece_list, weights):
    rows, width = piece_list[0].shape
    columns = weights[0].shape[1]
    tile = HEAD_WIDTH
    pieces, parts = len(piece_list), len(weights)
    whole = pl.BlockSpec((rows, width), lambda j, place: (0, 0))
    return pl.pallas_call(
        functools.partial(project_kernel, parts, pieces),
        grid_spec=pltpu.PrefetchScalarGridSpec(
            num_scalar_prefetch=1,
            grid=(columns // tile,),
            in_specs=[pl.BlockSpec((1, width), lambda j, place: (0, 0))]
            + [whole] * pieces
            + [pl.BlockSpec((weights[0].shape[0], tile), lambda j, place: (0, j))] * parts,
            out_specs=[
                pl.BlockSpec((pieces * rows, width), lambda j, place: (0, 0)),
                pl.BlockSpec((pieces * rows, tile), lambda j, place: (0, j)),
            ],
        ),
        out_shape=[
            jax.ShapeDtypeStruct((pieces * rows, width), BF16),
            jax.ShapeDtypeStruct((pieces * rows, columns), F32),
        ],
        compiler_params=pltpu.CompilerParams(vmem_limit_bytes=VMEM_LIMIT),
        name="project",
    )(shard_place, gain, *piece_list, *weights)


def head_rows(places_ref, step, rows, group):
    width = min(rows, group)
    found = []
    for at in range(rows // width):
        first = jnp.bitwise_xor(places_ref[1], step) * rows + at * width
        whose = jnp.bitwise_xor(first // group, places_ref[0])
        found.append((whose, pl.multiple_of(first % group, 128) if width < group else 0, width))
    return found


def merge_kernel(parts, pieces, places_ref, gain_ref, tokens_ref, *refs):
    mixed_refs, weight_refs = refs[:pieces], refs[pieces : pieces + parts]
    middle_ref, normed_ref, *left_refs, gathered = refs[pieces + parts :]
    step_id = pl.program_id(0)
    group = mixed_refs[0].shape[1]

    @pl.when(step_id == 0)
    def _():
        for at, ref in enumerate(mixed_refs):
            gathered[at] = ref[...]
        height = left_refs[0].shape[1] // parts
        for at, ref in enumerate(left_refs):
            for part in range(parts):
                first = (part * pieces + jnp.bitwise_xor(places_ref[0], at)) * height
                whose = jnp.bitwise_xor(first // group, places_ref[0])
                ref[:, part * height : (part + 1) * height] = gathered[
                    whose, :, pl.ds(pl.multiple_of(first % group, 128), height)
                ]

    tile = weight_refs[0].shape[1]
    total = tokens_ref[...].astype(F32)
    for step, ref in enumerate(weight_refs):
        rows = ref.shape[0]
        for at, (whose, first, width) in enumerate(head_rows(places_ref, step, rows, group)):
            total = total + jnp.dot(
                gathered[whose, :, pl.ds(first, width)],
                ref[at * width : (at + 1) * width],
                preferred_element_type=F32,
            )
    middle_ref[:, pl.ds(pl.multiple_of(step_id * tile, 128), tile)] = total

    @pl.when(step_id == pl.num_programs(0) - 1)
    def _():
        values = middle_ref[...]
        scale = lax.rsqrt(jnp.mean(values * values, -1, keepdims=True) + EPS)
        normed_ref[...] = (values * scale * gain_ref[...]).astype(BF16)


def merge(places, gain, tokens, mixed, weights):
    rows, width = tokens.shape
    tile = 512
    pieces, parts = len(mixed), len(weights)
    group = mixed[0].shape[1]
    whole = pl.BlockSpec((rows, width), lambda j, place: (0, 0))
    return pl.pallas_call(
        functools.partial(merge_kernel, parts, pieces),
        grid_spec=pltpu.PrefetchScalarGridSpec(
            num_scalar_prefetch=1,
            grid=(width // tile,),
            in_specs=[
                pl.BlockSpec((1, width), lambda j, place: (0, 0)),
                pl.BlockSpec((rows, tile), lambda j, place: (0, j)),
            ]
            + [pl.BlockSpec((rows, group), lambda j, place: (0, 0))] * pieces
            + [pl.BlockSpec((weights[0].shape[0], tile), lambda j, place: (0, j))] * parts,
            out_specs=[whole, whole]
            + [pl.BlockSpec((rows, group), lambda j, place: (0, 0))] * pieces,
            scratch_shapes=[pltpu.VMEM((pieces, rows, group), BF16)],
        ),
        out_shape=[
            jax.ShapeDtypeStruct((rows, width), F32),
            jax.ShapeDtypeStruct((rows, width), BF16),
        ]
        + [jax.ShapeDtypeStruct((rows, group), BF16)] * pieces,
        compiler_params=pltpu.CompilerParams(vmem_limit_bytes=VMEM_LIMIT),
        name="merge_heads",
    )(places, gain, tokens, *mixed, *weights)


def feed_kernel(parts, places_ref, *refs):
    normed_refs, grad_ref = refs[:parts], refs[parts]
    gate_refs, wide_refs = refs[parts + 1 : 2 * parts + 1], refs[2 * parts + 1 : 3 * parts + 1]
    outs, hidden_ref = refs[3 * parts + 1 : 4 * parts + 1], refs[4 * parts + 1]
    normed_all, grad_all = refs[4 * parts + 2 :]
    step_id = pl.program_id(0)
    rows, depth = normed_refs[0].shape[0], gate_refs[0].shape[0]

    @pl.when(step_id == 0)
    def _():
        for at in range(parts):
            where = slice(at * rows, (at + 1) * rows)
            for step in range(parts):
                first = pl.multiple_of(jnp.bitwise_xor(places_ref[1], step) * depth, 128)
                normed_all[step, where] = normed_refs[at][:, pl.ds(first, depth)]
        grad_all[...] = jnp.zeros_like(grad_all)

    gate, wide = None, None
    for step in range(parts):
        left = normed_all[step]
        one = jnp.dot(left, gate_refs[step][...], preferred_element_type=F32)
        two = jnp.dot(left, wide_refs[step][...], preferred_element_type=F32)
        gate, wide = (one, two) if gate is None else (gate + one, wide + two)
    hidden_grad = grad_ref[...]
    slope = jax.nn.sigmoid(gate)
    hidden_ref[...] = (gate * slope * wide).astype(BF16)
    gate_grad = (hidden_grad * wide * (slope * (1.0 + gate * (1.0 - slope)))).astype(BF16)
    wide_grad = (hidden_grad * gate * slope).astype(BF16)
    for step in range(parts):
        grad_all[step] += mm(gate_grad, gate_refs[step][...], ROWS_ROWS) + mm(
            wide_grad, wide_refs[step][...], ROWS_ROWS
        )

    @pl.when(step_id == pl.num_programs(0) - 1)
    def _():
        for at in range(parts):
            where = slice(at * rows, (at + 1) * rows)
            for step in range(parts):
                outs[at][step ^ at] = grad_all[step, where]


def feed(places, normed, hidden_grad, weights):
    rows, width = normed[0].shape
    parts = len(weights)
    depth = weights[0].shape[0]
    shard_columns = hidden_grad.shape[1]
    tile = 256 if shard_columns % 256 == 0 else shard_columns
    if tile == 256:
        sources = [(part, part) for part in weights]
        columns = weights[0].shape[1] // 2
        gate_at = lambda j, place: (0, place[1] * (shard_columns // tile) + j)
        wide_at = lambda j, place: (
            0,
            columns // tile + place[1] * (shard_columns // tile) + j,
        )
    else:
        shard = lax.axis_index("shard")
        sources = [
            (
                part_of(part[:, : part.shape[1] // 2], shard, parts, 1),
                part_of(part[:, part.shape[1] // 2 :], shard, parts, 1),
            )
            for part in weights
        ]
        gate_at = wide_at = lambda j, place: (0, j)
    whole = pl.BlockSpec((rows, width), lambda j, place: (0, 0))
    narrow = pl.BlockSpec((parts * rows, tile), lambda j, place: (0, j))
    return pl.pallas_call(
        functools.partial(feed_kernel, parts),
        grid_spec=pltpu.PrefetchScalarGridSpec(
            num_scalar_prefetch=1,
            grid=(shard_columns // tile,),
            in_specs=[whole] * parts
            + [narrow]
            + [pl.BlockSpec((depth, tile), gate_at)] * parts
            + [pl.BlockSpec((depth, tile), wide_at)] * parts,
            out_specs=[pl.BlockSpec((parts, rows, depth), lambda j, place: (0, 0, 0))] * parts
            + [narrow],
            scratch_shapes=[
                pltpu.VMEM((parts, parts * rows, depth), BF16),
                pltpu.VMEM((parts, parts * rows, depth), F32),
            ],
        ),
        out_shape=[jax.ShapeDtypeStruct((parts, rows, depth), F32)] * parts
        + [jax.ShapeDtypeStruct((parts * rows, shard_columns), BF16)],
        compiler_params=pltpu.CompilerParams(vmem_limit_bytes=VMEM_LIMIT),
        name="feed_forward",
    )(
        places,
        *normed,
        hidden_grad,
        *[source[0] for source in sources],
        *[source[1] for source in sources],
    )


def unmerge_kernel(parts, pieces, places_ref, gain_ref, middle_ref, up_ref, *refs):
    grad_refs, weight_refs = refs[:parts], refs[parts : 2 * parts]
    grad_out, sent_out, gain_out = refs[2 * parts : 2 * parts + 3]
    piece_outs = refs[2 * parts + 3 : 2 * parts + 3 + pieces]
    gathered = refs[-1]
    step_id = pl.program_id(0)
    depth = grad_refs[0].shape[2]

    @pl.when(step_id == 0)
    def _():
        for step in range(parts):
            first = pl.multiple_of(jnp.bitwise_xor(places_ref[1], step) * depth, 128)
            total = grad_refs[0][step]
            for ref in grad_refs[1:]:
                total = total + ref[step]
            grad_out[:, pl.ds(first, depth)] = total
        values, grad, gain = middle_ref[...], grad_out[...], gain_ref[...]
        scale = lax.rsqrt(jnp.mean(values * values, -1, keepdims=True) + EPS)
        unit_rows = values * scale
        weighted = grad * gain
        inner = jnp.mean(weighted * unit_rows, -1, keepdims=True)
        gain_out[...] = jnp.sum(grad * unit_rows, 0, keepdims=True)
        total = scale * (weighted - unit_rows * inner) + up_ref[...].astype(F32)
        grad_out[...] = total
        sent_out[...] = total.astype(BF16)

    count = pl.num_programs(0)
    group = gathered.shape[2]
    for step, ref in enumerate(weight_refs):
        width = ref.shape[0]
        first = jnp.bitwise_xor(places_ref[1], step) * (width * count) + step_id * width
        whose = jnp.bitwise_xor(first // group, places_ref[0])
        at = pl.multiple_of(first % group, 128) if width < group else 0
        gathered[whose, :, pl.ds(at, width)] = mm(sent_out[...], ref[...], ROWS_ROWS).astype(BF16)

    @pl.when(step_id == count - 1)
    def _():
        for at, ref in enumerate(piece_outs):
            ref[...] = gathered[at]


def unmerge(places, gain, middle, upstream, grads, weights, pieces):
    rows, width = middle.shape
    parts = len(weights)
    depth = grads[0].shape[2]
    group = VD // pieces
    tile = min(weights[0].shape[0], group)
    whole = pl.BlockSpec((rows, width), lambda j, place: (0, 0))
    one_row = pl.BlockSpec((1, width), lambda j, place: (0, 0))
    return pl.pallas_call(
        functools.partial(unmerge_kernel, parts, pieces),
        grid_spec=pltpu.PrefetchScalarGridSpec(
            num_scalar_prefetch=1,
            grid=(weights[0].shape[0] // tile,),
            in_specs=[one_row, whole, whole]
            + [pl.BlockSpec((parts, rows, depth), lambda j, place: (0, 0, 0))] * parts
            + [pl.BlockSpec((tile, width), lambda j, place: (j, 0))] * parts,
            out_specs=[whole, whole, one_row]
            + [pl.BlockSpec((rows, group), lambda j, place: (0, 0))] * pieces,
            scratch_shapes=[pltpu.VMEM((pieces, rows, group), BF16)],
        ),
        out_shape=[
            jax.ShapeDtypeStruct((rows, width), F32),
            jax.ShapeDtypeStruct((rows, width), BF16),
            jax.ShapeDtypeStruct((1, width), F32),
        ]
        + [jax.ShapeDtypeStruct((rows, group), BF16)] * pieces,
        compiler_params=pltpu.CompilerParams(vmem_limit_bytes=VMEM_LIMIT),
        name="split_heads",
    )(places, gain, middle, upstream, *grads, *weights)


def outer_kernel(parts, places_ref, *refs):
    left_refs, right_refs, out_refs = refs[:parts], refs[parts : 2 * parts], refs[2 * parts :]
    total = None
    for left, right in zip(left_refs, right_refs):
        term = mm(left[...], right[...], COLS_COLS)
        total = term if total is None else total + term
    (out_ref,) = out_refs
    chunks, several, height, _ = out_ref.shape
    for one in range(several):
        for at in range(chunks):
            first = (one * chunks + at) * height
            out_ref[at, one] = total[first : first + height].astype(out_ref.dtype)


def outer_products(places, lefts, own_right, rights, owners, chunks):
    rows, width = lefts[0].shape
    parts = len(lefts)
    columns = own_right.shape[1] // parts
    own = width // owners
    tile = max(own, 256)
    fixed = pl.BlockSpec((rows, columns), lambda j, place: (0, 0))
    return pl.pallas_call(
        functools.partial(outer_kernel, parts),
        grid_spec=pltpu.PrefetchScalarGridSpec(
            num_scalar_prefetch=1,
            grid=(width // tile,),
            in_specs=[pl.BlockSpec((rows, tile), lambda j, place: (0, j))] * parts
            + [pl.BlockSpec((rows, columns), lambda j, place: (0, place[1]))]
            + [fixed] * (parts - 1),
            out_specs=pl.BlockSpec(
                (chunks, tile // own, own // chunks, columns), lambda j, place: (0, j, 0, 0)
            ),
        ),
        out_shape=jax.ShapeDtypeStruct((chunks, owners, own // chunks, columns), BF16),
        compiler_params=pltpu.CompilerParams(vmem_limit_bytes=VMEM_LIMIT),
        name="outer_products",
    )(places, *lefts, own_right, *rights)


def rows_kernel(pieces, places_ref, *refs):
    left_refs, right_refs, out_ref, left, right = (
        refs[:pieces], refs[pieces : 2 * pieces], refs[2 * pieces], refs[-2], refs[-1],
    )
    rows = left_refs[0].shape[0]

    @pl.when(pl.program_id(0) == 0)
    def _():
        for at, ref in enumerate(left_refs):
            left[at * rows : (at + 1) * rows] = ref[...]

    for at, ref in enumerate(right_refs):
        right[at * rows : (at + 1) * rows] = ref[...]
    parts, height, _ = out_ref.shape
    for step in range(parts):
        first = pl.multiple_of(jnp.bitwise_xor(places_ref[1], step) * height, 128)
        out_ref[step] = mm(left[:, pl.ds(first, height)], right[...], COLS_COLS).astype(
            out_ref.dtype
        )


def own_rows(places, lefts, rights, parts):
    pieces = len(lefts)
    rows, columns = lefts[0].shape
    height = columns // parts
    width = rights[0].shape[1]
    tile = 512
    return pl.pallas_call(
        functools.partial(rows_kernel, pieces),
        grid_spec=pltpu.PrefetchScalarGridSpec(
            num_scalar_prefetch=1,
            grid=(width // tile,),
            in_specs=[pl.BlockSpec((rows, columns), lambda j, place: (0, 0))] * pieces
            + [pl.BlockSpec((rows, tile), lambda j, place: (0, j))] * pieces,
            out_specs=pl.BlockSpec((parts, height, tile), lambda j, place: (0, 0, j)),
            scratch_shapes=[
                pltpu.VMEM((pieces * rows, columns), BF16),
                pltpu.VMEM((pieces * rows, tile), BF16),
            ],
        ),
        out_shape=jax.ShapeDtypeStruct((parts, height, width), BF16),
        compiler_params=pltpu.CompilerParams(vmem_limit_bytes=VMEM_LIMIT),
        name="own_rows",
    )(places, *lefts, *rights)


def again_kernel(parts, places_ref, normed_ref, up_ref, *refs):
    gate_refs, wide_refs, down_ref = refs[:parts], refs[parts : 2 * parts], refs[2 * parts]
    hidden_ref, gate_out, wide_out = refs[-3:]
    depth = gate_refs[0].shape[0]
    gate, wide = None, None
    for step in range(parts):
        first = pl.multiple_of(jnp.bitwise_xor(places_ref[1], step) * depth, 128)
        left = normed_ref[:, pl.ds(first, depth)]
        one, two = mm(left, gate_refs[step][...]), mm(left, wide_refs[step][...])
        gate, wide = (one, two) if gate is None else (gate + one, wide + two)
    hidden_grad = mm(up_ref[...], down_ref[...], ROWS_ROWS)
    slope = jax.nn.sigmoid(gate)
    hidden_ref[...] = (gate * slope * wide).astype(BF16)
    gate_out[...] = (hidden_grad * wide * (slope * (1.0 + gate * (1.0 - slope)))).astype(BF16)
    wide_out[...] = (hidden_grad * gate * slope).astype(BF16)


def feed_again(places, normed, upstream, gates, wides, down, step, before=()):
    count, width = normed.shape
    parts = len(gates)
    depth, columns = gates[0].shape
    tile = 256
    tiles = count // tile
    there = lambda j, place: (jnp.bitwise_xor(place[1], step) * tiles + j, 0)
    here = lambda j, place: (j, 0)
    fixed = pl.BlockSpec((depth, columns), lambda j, place: (0, 0))
    carried = 1 + 2 + 2 * parts + 1
    return pl.pallas_call(
        functools.partial(again_kernel, parts),
        grid_spec=pltpu.PrefetchScalarGridSpec(
            num_scalar_prefetch=1,
            grid=(tiles,),
            in_specs=[pl.BlockSpec((tile, width), here), pl.BlockSpec((tile, width), there)]
            + [fixed] * (2 * parts)
            + [pl.BlockSpec((columns, width), lambda j, place: (0, 0))]
            + [pl.BlockSpec(memory_space=pl.ANY)] * len(before),
            out_specs=[pl.BlockSpec((tile, columns), there)]
            + [pl.BlockSpec((tile, columns), here)] * 2,
        ),
        out_shape=[
            jax.ShapeDtypeStruct((upstream.shape[0], columns), BF16),
            jax.ShapeDtypeStruct((count, columns), BF16),
            jax.ShapeDtypeStruct((count, columns), BF16),
        ],
        input_output_aliases={carried + at: at for at in range(len(before))},
        compiler_params=pltpu.CompilerParams(vmem_limit_bytes=VMEM_LIMIT),
        name="feed_again",
    )(places, normed, upstream, *gates, *wides, down, *before)


def place_in_kernel(columns_of, head_of, in_ref, out_ref, held, sems):
    step_id = pl.program_id(0)
    slot = lax.rem(step_id, 2)

    def copies(which, where):
        found = []
        for number, (low, width, first) in enumerate(columns_of):
            at = pl.multiple_of(first + head_of(which) * width, 128)
            found.append(
                pltpu.make_async_copy(
                    held.at[where, :, pl.ds(low, width)],
                    out_ref.at[:, pl.ds(at, width)],
                    sems.at[where, number],
                )
            )
        return found

    @pl.when(step_id >= 2)
    def _():
        for copy in copies(step_id - 2, slot):
            copy.wait()

    held[slot] = in_ref[:, 0].astype(F32).reshape(held.shape[1:])
    for copy in copies(step_id, slot):
        copy.start()

    @pl.when(step_id == pl.num_programs(0) - 1)
    def _():
        for copy in copies(step_id - 1, 1 - slot) + copies(step_id, slot):
            copy.wait()


def place_in(value, seqs):
    blocks, sources, rows, columns = value.shape
    heads = HEADS // seqs
    per_source = columns // HEAD_WIDTH
    columns_of = [(0, DK, 0), (DK, DK, KD), (2 * DK, DV, 2 * KD), (2 * DK + DV, DV, CONVW)]

    def head_of(step):
        source = step // per_source
        return source % seqs * heads + source // seqs * per_source + step % per_source

    return pl.pallas_call(
        functools.partial(place_in_kernel, columns_of, head_of),
        grid=(sources * per_source,),
        in_specs=[
            pl.BlockSpec(
                (blocks, 1, rows, HEAD_WIDTH), lambda h: (0, h // per_source, 0, h % per_source)
            )
        ],
        out_specs=pl.BlockSpec(memory_space=pl.ANY),
        out_shape=jax.ShapeDtypeStruct((blocks * rows, PROJW), F32),
        scratch_shapes=[
            pltpu.VMEM((2, blocks * rows, HEAD_WIDTH), F32),
            pltpu.SemaphoreType.DMA((2, len(columns_of))),
        ],
        compiler_params=pltpu.CompilerParams(vmem_limit_bytes=VMEM_LIMIT),
        name="place_w_in",
    )(value)


def place_gu_kernel(half, gate_ref, wide_ref, out_ref):
    def put(ref):
        width = ref.shape[2]
        for at in range(ref.shape[0]):
            out_ref[:, at * width : (at + 1) * width] = ref[at].astype(F32)

    @pl.when(pl.program_id(0) < half)
    def _():
        put(gate_ref)

    @pl.when(pl.program_id(0) >= half)
    def _():
        put(wide_ref)


def place_gu(gate, wide):
    sources, rows, width = gate.shape
    together = 1
    while together * width % 128:
        together *= 2
    half = sources // together
    return pl.pallas_call(
        functools.partial(place_gu_kernel, half),
        grid=(2 * half,),
        in_specs=[
            pl.BlockSpec((together, rows, width), lambda j: (jnp.minimum(j, half - 1), 0, 0)),
            pl.BlockSpec((together, rows, width), lambda j: (jnp.maximum(j - half, 0), 0, 0)),
        ],
        out_specs=pl.BlockSpec((rows, together * width), lambda j: (0, j)),
        out_shape=jax.ShapeDtypeStruct((rows, 2 * sources * width), F32),
        compiler_params=pltpu.CompilerParams(vmem_limit_bytes=VMEM_LIMIT),
        name="place_w_gu",
    )(gate, wide)


def line_first(value):
    return lax.ppermute(value, "replica", [(0, 1), (3, 2)])


def line_second(value):
    return lax.ppermute(value, "replica", [(1, 2), (2, 1)])


def line_third(value):
    return lax.ppermute(value, "replica", [(1, 0), (2, 3)])


def added(left, right):
    return (left.astype(F32) + right.astype(F32)).astype(BF16)


def pinned(*values):
    return lax.optimization_barrier(values)


def line_sum(value):
    value = added(value, line_first(value))
    value = added(value, line_second(value))
    return settled_pair((value, line_third(value)))


def settled_pair(pair):
    place = lax.axis_index("replica")
    return jnp.where((place == 1) | (place == 2), pair[0], pair[1]).astype(F32)


def swapped(value, axis, step):
    count = lax.axis_size(axis)
    return lax.ppermute(value, axis, [(source, source ^ step) for source in range(count)])


def around(value, axis):
    return [value] + [swapped(value, axis, step) for step in range(1, lax.axis_size(axis))]


def settled(parts, index):
    stacked = jnp.stack(parts)
    return [
        lax.dynamic_index_in_dim(stacked, jnp.bitwise_xor(index, at), 0, keepdims=False)
        for at in range(len(parts))
    ]


def part_of(value, index, count, axis):
    width = value.shape[axis] // count
    return lax.dynamic_slice_in_dim(value, index * width, width, axis)


def dot(left, right):
    return jnp.dot(left, right, preferred_element_type=F32)


def dot_rows(left, right):
    return lax.dot_general(left, right, (((1,), (1,)), ((), ())), preferred_element_type=F32)


def dot_cols(left, right):
    return lax.dot_general(left, right, (((0,), (0,)), ((), ())), preferred_element_type=F32)


def rms_parts(values):
    return lax.rsqrt(jnp.mean(values * values, -1, keepdims=True) + EPS)


def rms_back(values, scale, gain, grad):
    weighted = grad * gain
    unit_rows = values * scale
    inner = jnp.mean(weighted * unit_rows, -1, keepdims=True)
    return scale * (weighted - unit_rows * inner), jnp.sum(grad * unit_rows, 0)


def body(
    tokens,
    cotangent,
    lengths,
    norm_gains,
    w_in,
    w_ab,
    conv_weight,
    gate_params,
    onorm_gain,
    w_o,
    w_gu,
    w_down,
):
    shards, seqs, replicas = (lax.axis_size(name) for name in EVERY)
    shard, seq = lax.axis_index("shard"), lax.axis_index("seq")
    owners = shards * seqs
    owner = shard * seqs + seq
    micro, row = tokens.shape[0], tokens.shape[1]
    flat = micro * row
    length = row * seqs
    heads = HEADS // seqs
    depth = D // shards
    seq_place = jnp.reshape(seq, (1,)).astype(jnp.int32)
    shard_place = jnp.reshape(shard, (1,)).astype(jnp.int32)
    places = jnp.stack([seq, shard]).astype(jnp.int32)

    def blocks(value, count, axis=1):
        return [part_of(value, jnp.bitwise_xor(shard, step), count, axis) for step in range(count)]

    flat_tokens = tokens.reshape(flat, D)
    in_own = pick_heads(seq_place, w_in, heads)
    sent_tokens, in_own = pinned(flat_tokens, in_own)
    pieces = around(sent_tokens, "seq")
    gain_parts = around(norm_gains, "shard")
    in_parts = around(in_own, "shard")
    taps_parts = around(conv_weight, "shard")
    ab_parts = around(w_ab, "shard")
    gains = jnp.concatenate(settled(gain_parts, shard), 1).astype(F32)
    gain_first, gain_second = gains[:1], gains[1:]
    taps = jnp.concatenate(settled(taps_parts, shard), 1)
    upstream = cotangent.reshape(flat, D)
    up_parts = around(upstream, "shard")
    hidden_grad = dot_rows(jnp.concatenate(up_parts, 0), w_down)
    own_out, own_gu, late_up, hidden_grad, *arrived = pinned(
        w_o, w_gu, upstream, hidden_grad, *pieces, *in_parts
    )
    pieces, in_parts = arrived[:seqs], arrived[seqs:]
    all_up = lax.all_gather(late_up, EVERY, axis=0, tiled=True)
    out_parts = around(own_out, "shard")
    gu_parts = around(own_gu, "shard")

    normed, projected = project(shard_place, gain_first, pieces, in_parts)
    rate_in = sum(dot(left, right) for left, right in zip(blocks(normed, shards), ab_parts))
    rate_in = part_of(rate_in.reshape(seqs, micro, row, 2, HEADS), seq, seqs, 4)
    rate_in = jnp.stack(settled(list(rate_in), seq))
    rate_in = jnp.transpose(rate_in, (3, 1, 4, 0, 2)).reshape(2, micro, heads, length)
    position = jnp.arange(length, dtype=jnp.int32)
    valid = (position[None, :] < lengths[:, None]).astype(F32)[:, None, :]
    own_params = part_of(gate_params, seq, seqs, 1)[:, None, :, None]
    rate_shifted = rate_in[0] + own_params[1]
    decays = -jnp.exp(own_params[0]) * jax.nn.softplus(rate_shifted) * valid
    written = jax.nn.sigmoid(rate_in[1])
    rates = jnp.stack([jnp.maximum(decays, LOWEST_DECAY), written * valid], 2)
    rates = jnp.pad(rates, ((0, 0), (0, 0), (0, SMALL_ROWS - 2), (0, 0)))
    gain_row = onorm_gain.reshape(1, DV)
    projected = projected.reshape(seqs, micro, row, -1)
    *gated, inverse, update = mixer_forward(seq_place, projected, taps, rates, gain_row, 2)
    gated = [item.reshape(flat, heads * DV) for item in gated]

    mixed_parts = [gated[0]] + [swapped(gated[step], "seq", step) for step in range(1, seqs)]
    arrived = pinned(*mixed_parts, *gu_parts)
    mixed_parts, gu_parts = list(arrived[:seqs]), list(arrived[seqs:])

    middle, renormed, *mixed_left = merge(
        places, gain_second, flat_tokens, mixed_parts, out_parts
    )
    line_renormed = lax.all_gather(renormed, "replica", axis=0, tiled=True)

    mixed_left = [
        swapped(item, "seq", step) if step else item for step, item in enumerate(mixed_left)
    ]
    fed = feed(places, around(renormed, "shard"), hidden_grad, gu_parts)
    fed = pinned(*fed, *mixed_left)
    fed, mixed_left = fed[: shards + 1], fed[shards + 1 :]
    grads_back = [fed[0]] + [swapped(fed[step], "shard", step) for step in range(1, shards)]
    middle_grad, mixed_grad, gain2_grad, *gated_grad = unmerge(
        places, gain_second, middle, upstream, grads_back, out_parts, seqs
    )
    hidden = fed[shards]

    ff_own = FF // owners
    own_down = part_of(w_down, seq, seqs, 0)
    own_gate = [part_of(part, owner, 2 * owners, 1) for part in gu_parts]
    own_wide = [part_of(part, owners + owner, 2 * owners, 1) for part in gu_parts]

    gated_grad = [
        swapped(item, "seq", step) if step else item for step, item in enumerate(gated_grad)
    ]
    all_up, mixed_grad, own_down, *others = pinned(
        all_up, mixed_grad, own_down, *own_gate, *own_wide, *gated_grad
    )
    own_gate, own_wide = others[:shards], others[shards : 2 * shards]
    gated_grad = others[2 * shards :]
    gated_grad = [item.reshape(micro, row, heads * DV) for item in gated_grad]
    mid_pieces = around(mixed_grad, "seq")
    proj_grad, small_grad = mixer_backward(
        seq_place, projected, taps, rates, gain_row, inverse, update, gated_grad, 1
    )
    proj_grad, *mid_pieces = pinned(proj_grad, *mid_pieces)
    rows_all = seqs * flat
    proj_grad = proj_grad.reshape(rows_all, -1)
    pair_proj = [
        swapped(part_of(proj_grad, jnp.bitwise_xor(shard, step), shards, 1), "shard", step)
        for step in range(1, shards)
    ]

    pair_normed = around(normed, "shard")
    spread = jnp.broadcast_to(line_renormed[None], (seqs,) + line_renormed.shape)
    spread, *pair_proj = pinned(spread, *pair_proj)
    grad_in = outer_products(places, pair_normed, proj_grad, pair_proj, owners, replicas)
    width = grad_in.shape[3]
    proj_grad, small_grad, grad_in, spread, *mid_pieces = pinned(
        proj_grad, small_grad, grad_in, spread, *mid_pieces
    )
    grad_in = lax.psum_scatter(grad_in, "replica", scatter_dimension=0, tiled=False)
    own_renormed = lax.all_to_all(spread, "seq", split_axis=0, concat_axis=0).reshape(-1, D)

    grad_out = own_rows(places, mixed_left, mid_pieces, shards)
    grad_out = functools.reduce(
        added, [grad_out[0]] + [swapped(grad_out[step], "shard", step) for step in range(1, shards)]
    )

    def input_gradient_parts(proj_grad, small_grad):
        decay_grad = small_grad[:, :, 5, :length]
        write_grad = small_grad[:, :, 6, :length]
        shifted_grad = decay_grad * -jnp.exp(own_params[0]) * jax.nn.sigmoid(rate_shifted) * valid
        params_grad = jnp.stack(
            [jnp.sum(decay_grad * decays, (0, 2)), jnp.sum(shifted_grad, (0, 2))]
        )
        rate_grad = jnp.stack([shifted_grad, write_grad * written * (1.0 - written) * valid])
        rate_grad = jnp.transpose(rate_grad.reshape(2, micro, heads, seqs, row), (3, 1, 4, 0, 2))
        rate_grad = jnp.stack(settled(list(rate_grad), seq))
        rate_grad = rate_grad.reshape(rows_all, 2 * heads)
        grad_ab = lax.dot_general(
            rate_grad, normed.astype(F32), (((0,), (0,)), ((), ())), precision=HIGHEST
        )
        own_ab = [
            part_of(part.reshape(depth, 2, HEADS), seq, seqs, 2).reshape(depth, 2 * heads)
            for part in ab_parts
        ]
        normed_grad = [
            dot_rows(proj_grad, part)
            + lax.dot_general(
                rate_grad, ab.astype(F32), (((1,), (1,)), ((), ())), precision=HIGHEST
            )
            for part, ab in zip(in_parts, own_ab)
        ]
        return (*normed_grad, grad_ab, params_grad)

    def input_gradient(*normed_grad):
        *normed_grad, grad_ab, params_grad = normed_grad
        normed_grad = jnp.concatenate(settled(normed_grad, shard), 1).reshape(seqs, flat, D)
        normed_grad = normed_grad[0] + sum(
            swapped(normed_grad[step].astype(BF16), "seq", step).astype(F32)
            for step in range(1, seqs)
        )
        flat_in = flat_tokens.astype(F32)
        inputs_grad, gain1_grad = rms_back(flat_in, rms_parts(flat_in), gains[0], normed_grad)
        input_grads = (inputs_grad + middle_grad).astype(BF16).reshape(micro, row, D)
        return input_grads, gain1_grad, grad_ab, params_grad

    def to_group(value):
        return lax.all_to_all(value, GROUP, split_axis=0, concat_axis=0, tiled=False)

    def to_owners(value):
        return to_group(value.astype(BF16).reshape(owners, D // owners, ff_own))

    normed_parts = input_gradient_parts(proj_grad, small_grad)
    own_renormed, grad_out, *normed_parts = pinned(own_renormed, grad_out, *normed_parts)
    replica = lax.axis_index("replica")
    grad_out = [
        swapped(part_of(grad_out, jnp.bitwise_xor(replica, step), replicas, 0), "replica", step)
        if step
        else part_of(grad_out, replica, replicas, 0)
        for step in range(replicas)
    ]
    input_grads, gain1_grad, grad_ab, params_grad = input_gradient(*normed_parts)
    gain2_grad = gain2_grad[0]
    all_renormed = around(own_renormed, "shard")

    def again(at, before=()):
        return feed_again(
            places, all_renormed[at], all_up, own_gate, own_wide, own_down, at, before
        )

    def over_tokens(lefts, rights):
        return sum(dot_cols(left, right) for left, right in zip(lefts, rights))

    parts = [again(0)]
    input_grads, gain1_grad, grad_ab, params_grad, *others = pinned(
        input_grads, gain1_grad, grad_ab, params_grad, *grad_out, *parts[0]
    )
    grad_out, parts[0] = others[:replicas], others[replicas:]
    grad_out = sum(item.astype(F32) for item in grad_out).astype(BF16)
    taps_grad = jnp.sum(small_grad[:, :, :KERNEL], 0)
    conv_grad = jnp.concatenate(
        [
            jnp.swapaxes(taps_grad[..., low:high], 0, 1).reshape(KERNEL, -1)
            for low, high in ((0, DK), (DK, 2 * DK), (2 * DK, 2 * DK + DV))
        ],
        1,
    )
    onorm_grad = jnp.sum(small_grad[:, :, 4, :DV], (0, 1))
    loose = jnp.concatenate([onorm_grad, params_grad.reshape(-1)])
    loose = jnp.pad(loose, (0, D - loose.size))
    rows_ab = 2 * heads
    smalls = jnp.concatenate(
        [grad_ab, conv_grad, loose[None], gain1_grad[None], gain2_grad[None]], 0
    )
    step = 1
    while step < shards:
        smalls = smalls + swapped(smalls, "shard", step)
        step *= 2
    rows_small = smalls.shape[0]
    high = lax.optimization_barrier(smalls.astype(BF16))
    low = (smalls - high.astype(F32)).astype(BF16)
    fill = jnp.zeros((-(2 * rows_small) % 16, D), BF16)
    rows_own = grad_out.shape[0]
    grad_out = jnp.concatenate([grad_out, high, low, fill], 0)
    grad_out, *all_renormed = pinned(grad_out, *all_renormed)
    grad_out = lax.all_gather(grad_out, "replica", axis=0)
    for at in range(1, shards):
        parts.append(again(at, parts[-1][:1]))
    grad_in, hidden, own_hidden = pinned(grad_in, hidden, parts[-1][0])
    grad_in = to_group(grad_in)
    gate_grad, wide_grad = ([part[which] for part in parts] for which in (1, 2))
    grad_gate = over_tokens(all_renormed, gate_grad).astype(BF16)
    grad_in, grad_gate, own_hidden, *wide_grad = pinned(
        grad_in, grad_gate, own_hidden, *wide_grad
    )
    grad_in = lax.all_gather(grad_in, "replica", axis=0)
    grad_gate = to_owners(grad_gate)
    grad_wide = over_tokens(all_renormed, wide_grad).astype(BF16)
    grad_down = dot_cols(own_hidden, all_up)
    grad_wide, grad_gate, grad_out = pinned(grad_wide, grad_gate, grad_out)
    grad_wide = to_owners(grad_wide)
    rows_down = dot(hidden, w_down).reshape(shards, flat, D)
    result = (
        middle
        + rows_down[0]
        + sum(swapped(rows_down[step], "shard", step) for step in range(1, shards))
    )
    results = result.astype(BF16).reshape(micro, row, D)
    smalls = grad_out[:, rows_own : rows_own + 2 * rows_small].astype(F32)
    smalls = jnp.sum(smalls[:, :rows_small] + smalls[:, rows_small:], 0)
    grad_out = grad_out[:, :rows_own].reshape(replicas * rows_own, D).astype(F32)
    every = jnp.stack(settled(around(smalls, "seq"), seq))
    grad_gu = place_gu(grad_gate, grad_wide)
    if width % HEAD_WIDTH == 0:
        grad_in = place_in(grad_in, seqs)
    else:
        grad_in = grad_in.reshape(replicas, shards, seqs, -1, width)
        grad_in = jnp.transpose(grad_in, (0, 3, 2, 1, 4)).reshape(D // owners, HEADS, HEAD_WIDTH)
        cuts = (0, DK, 2 * DK, 2 * DK + DV, HEAD_WIDTH)
        grad_in = jnp.concatenate(
            [
                grad_in[..., low:high].reshape(D // owners, -1)
                for low, high in zip(cuts[:-1], cuts[1:])
            ],
            1,
        ).astype(F32)

    ab_total = jnp.transpose(every[:, :rows_ab].reshape(seqs, 2, heads, D), (3, 1, 0, 2))
    ab_total = ab_total.reshape(D, 2 * HEADS)
    conv_all = every[:, rows_ab : rows_ab + KERNEL]
    conv_total = jnp.concatenate(
        [
            jnp.swapaxes(conv_all[..., low:high], 0, 1).reshape(KERNEL, -1)
            for low, high in (
                (0, heads * DK),
                (heads * DK, 2 * heads * DK),
                (2 * heads * DK, heads * (2 * DK + DV)),
            )
        ],
        1,
    )
    loose_all = every[:, rows_ab + KERNEL]
    onorm_total = jnp.sum(loose_all[:, :DV], 0)
    params_total = loose_all[:, DV : DV + 2 * heads].reshape(seqs, 2, heads)
    params_total = jnp.swapaxes(params_total, 0, 1).reshape(2, HEADS)
    gains_total = jnp.sum(every[:, rows_ab + KERNEL + 1 : rows_ab + KERNEL + 3], 0)
    gains_own = part_of(gains_total, owner, owners, 1)
    ab_own = part_of(ab_total, owner, owners, 0)
    conv_own = part_of(conv_total, owner, owners, 1)
    return (
        results,
        input_grads,
        gains_own,
        grad_in,
        ab_own,
        conv_own,
        params_total,
        onorm_total,
        grad_out,
        grad_gu,
        grad_down,
    )


def solution(mesh):
    in_specs = (
        P(("shard", "replica"), "seq", None),
        P(("shard", "replica"), "seq", None),
        P(("shard", "replica")),
        P(None, "shard"),
        P("shard", None),
        P("shard", None),
        P(None, "shard"),
        P(),
        P(),
        P("shard", None),
        P("shard", None),
        P("shard", None),
    )
    out_specs = (
        P(("shard", "replica"), "seq", None),
        P(("shard", "replica"), "seq", None),
        P(None, ("shard", "seq")),
        P(("shard", "seq"), None),
        P(("shard", "seq"), None),
        P(None, ("shard", "seq")),
        P(),
        P(),
        P(("shard", "seq"), None),
        P(("shard", "seq"), None),
        P(("shard", "seq"), None),
    )
    return jax.shard_map(body, mesh=mesh, in_specs=in_specs, out_specs=out_specs, check_vma=False)
```
